128 devices in a mesh: shard: 4 (over x), context: 8 (over z, y_lo), tensor: 4 (over y_hi, core).
Axes of the slice: x: 4, y: 4 (y_hi: 2, y_lo: 2; y = y_hi * 2 + y_lo), z: 4, core: 2. Of those that a mesh axis runs over, the one named last changes fastest.
Arguments:
- tokens: bfloat16 [8, 1024, 2048], P('shard', 'context'), may hold values from -6 to 6
- lengths: int32 [8], P('shard'), may hold values from 256 to 1024, as said below
- routes: int32 [8, 1024, 8], P('shard', 'context'), may hold values from 0 to 9, all different within a row
- attn_gain: bfloat16 [2048], P(('shard', 'context')), may hold values from 0.099609375 to 1.8984375
- q_gain: bfloat16 [16, 128], P('tensor', ('shard', 'context')), may hold values from 0.099609375 to 1.8984375
- k_gain: bfloat16 [16, 128], P('tensor', ('shard', 'context')), may hold values from 0.099609375 to 1.8984375
- w_query: bfloat16 [2048, 2048], P(('shard', 'context'), 'tensor'), may hold values from -0.125 to 0.125
- w_key: bfloat16 [2048, 2048], P(('shard', 'context'), 'tensor'), may hold values from -0.125 to 0.125
- w_value: bfloat16 [2048, 2048], P(('shard', 'context'), 'tensor'), may hold values from -0.125 to 0.125
- w_out: bfloat16 [2048, 2048], P('tensor', ('shard', 'context')), may hold values from -1 to 1
- mlp_gain: bfloat16 [2048], P(('shard', 'context')), may hold values from 0.099609375 to 1.8984375
- router: bfloat16 [2048, 10], P(('shard', 'context')), may hold values from -0.0625 to 0.0625
- w_gate: bfloat16 [10, 2048, 1024], P(None, ('shard', 'context'), 'tensor'), may hold values from -0.125 to 0.125
- w_up: bfloat16 [10, 2048, 1024], P(None, ('shard', 'context'), 'tensor'), may hold values from -0.125 to 0.125
- w_down: bfloat16 [10, 1024, 2048], P(None, 'tensor', ('shard', 'context')), may hold values from -0.75 to 0.75
- cotangent: bfloat16 [8, 1024, 2048], P('shard', 'context'), may hold values from -6 to 6
Outputs:
- output: bfloat16 [8, 1024, 2048], P('shard', 'context')
- grad_input: float32 [8, 1024, 2048], P('shard', 'context')
- attn_gain_grad: float32 [2048], P(('shard', 'context'))
- q_gain_grad: float32 [16, 128], P('tensor', ('shard', 'context'))
- k_gain_grad: float32 [16, 128], P('tensor', ('shard', 'context'))
- w_query_grad: float32 [2048, 2048], P(('shard', 'context'), 'tensor')
- w_key_grad: float32 [2048, 2048], P(('shard', 'context'), 'tensor')
- w_value_grad: float32 [2048, 2048], P(('shard', 'context'), 'tensor')
- w_out_grad: float32 [2048, 2048], P('tensor', ('shard', 'context'))
- mlp_gain_grad: float32 [2048], P(('shard', 'context'))
- router_grad: float32 [2048, 10], P(('shard', 'context'))
- w_gate_grad: float32 [10, 2048, 1024], P(None, ('shard', 'context'), 'tensor')
- w_up_grad: float32 [10, 2048, 1024], P(None, ('shard', 'context'), 'tensor')
- w_down_grad: float32 [10, 1024, 2048], P(None, 'tensor', ('shard', 'context'))
The draws below stay inside these ranges and needn't reach their ends.
Inputs may be any that keep to these rules, and one draw needn't show every extreme that they name: `lengths`: among the slots held by each index of shard, one, drawn from the seed, has length 1024. `routes`: each token names 8 different experts.
All inputs are finite; a program needn't handle non-finite values.
Results may differ from the reference program's by a relative error of at most 0.035.
Values may be sent and summed in bfloat16 or wider, within the bound.
No kernel may reach another device: no remote copies, remote signals or barrier semaphores. Data moves between devices by JAX's collectives and lax.ppermute only.
A program may use at most 256 MiB of HBM per device.

```python
import math
import jax
import jax.numpy as jnp
from jax import lax

D = 2048
HEADS = 16
HD = 128
FF = 1024
TOP = 8
EXPERTS = 10
SEQ = 1024
MB = 2
SLOT_MB = 1
SLOTS = 8


def draw_lengths(key, part):
    key = jax.random.fold_in(key, 17)
    first_key, second_key = jax.random.split(key)
    group_size = MB * SLOT_MB
    base_lengths = jax.random.randint(first_key, (SLOTS,), SEQ // 4, SEQ + 1)
    pick_slot = jax.random.randint(second_key, (SLOTS // group_size,), 0, group_size)
    slot_index = jnp.arange(SLOTS) % group_size
    whole_slot = slot_index == jnp.repeat(pick_slot, group_size, total_repeat_length=SLOTS)
    return jnp.where(whole_slot, SEQ, base_lengths).astype(jnp.int32)


def level_of(rng, shape, cuts, smallest, high):
    loudness, own = 1.0, jax.random.fold_in(rng, 6)
    for axis_at, shards_of in cuts:
        heights = jnp.exp(jax.random.uniform(jax.random.fold_in(own, axis_at), (shards_of,), jnp.float32, smallest / len(cuts), high / len(cuts)))
        loudness = loudness * jnp.repeat(heights, shape[axis_at] // shards_of).reshape([-1 if axis == axis_at else 1 for axis in range(len(shape))])
    return loudness


def choose_distinct(own_key, rows, count, top, lift):
    order = jax.random.permutation(jax.random.fold_in(own_key, 1), count)
    favour = order
    for power in range(3):
        favour = favour * favour // count
    favour = favour * lift // count
    chance = jax.random.randint(jax.random.fold_in(own_key, 2), (rows, count), 0, 4096) + favour
    sure = jax.random.permutation(jax.random.fold_in(own_key, 3), rows)[jnp.arange(count) % rows]
    chance = jnp.where(jnp.arange(rows)[:, None] == sure[None, :], 1 << 14, chance)
    score = chance * count + jnp.arange(count)
    return lax.top_k(score.astype(jnp.int32), top)[1].astype(jnp.int32)


def noise(rng, dims, width, reach, shards=(), kind=jnp.bfloat16):
    drawn = jax.random.normal(rng, dims, jnp.float32) * width
    if len(shards) > 0:
        drawn = level_of(rng, dims, shards, -0.22, 0.18) * drawn
    return jnp.clip(drawn, min=-reach, max=reach).astype(kind)


def setup_inputs(seed: int = 0) -> dict:
    streams_of = jax.random.split(jax.random.key(seed), 17)
    return {
        "tokens": noise(streams_of[0], (SLOTS, SEQ, D), 1.0, 6.0, ((0, 4), (1, 8))),
        "lengths": draw_lengths(jax.random.fold_in(streams_of[16], 71), 0),
        "routes": choose_distinct(streams_of[2], SLOTS * SEQ, EXPERTS, TOP, 6553).reshape((SLOTS, SEQ, TOP)),
        "attn_gain": jnp.clip(1.0 + 0.18 * jax.random.normal(streams_of[3], (D,), jnp.float32), 0.099609375, 1.8984375).astype(jnp.bfloat16),
        "q_gain": jnp.clip(1.0 + 0.18 * jax.random.normal(streams_of[4], (HEADS, HD), jnp.float32), 0.099609375, 1.8984375).astype(jnp.bfloat16),
        "k_gain": jnp.clip(1.0 + 0.18 * jax.random.normal(streams_of[5], (HEADS, HD), jnp.float32), 0.099609375, 1.8984375).astype(jnp.bfloat16),
        "w_query": noise(streams_of[6], (D, D), D ** -0.5, 0.125, ((0, 32), (1, 4))),
        "w_key": noise(streams_of[7], (D, D), D ** -0.5, 0.125, ((0, 32), (1, 4))),
        "w_value": noise(streams_of[8], (D, D), D ** -0.5, 0.125, ((0, 32), (1, 4))),
        "w_out": noise(streams_of[9], (D, D), (D // 64) ** -0.5, 1.0, ((0, 4), (1, 32))),
        "mlp_gain": jnp.clip(1.0 + 0.18 * jax.random.normal(streams_of[10], (D,), jnp.float32), 0.099609375, 1.8984375).astype(jnp.bfloat16),
        "router": noise(streams_of[11], (D, EXPERTS), (4 * D) ** -0.5, 0.0625, ((0, 32),)),
        "w_gate": noise(streams_of[12], (EXPERTS, D, FF), D ** -0.5, 0.125, ((1, 32), (2, 4))),
        "w_up": noise(streams_of[13], (EXPERTS, D, FF), D ** -0.5, 0.125, ((1, 32), (2, 4))),
        "w_down": noise(streams_of[14], (EXPERTS, FF, D), (FF // 16) ** -0.5, 0.75, ((1, 4), (2, 32))),
        "cotangent": noise(streams_of[15], (SLOTS, SEQ, D), 1.0, 6.0, ((0, 4), (1, 8))),
    }


EPSILON = 1e-05
ROPE_BASE = 10000.0
HIGHEST_PRECISION = lax.Precision.HIGHEST

@jax.custom_vjp
def low(v):
    return lax.optimization_barrier(v.astype(jnp.bfloat16)).astype(jnp.float32)

@jax.custom_vjp
def low_back(v):
    return v

def low_keep(v):
    return (low(v), None)

def low_pass(kept, grad):
    return (grad,)

def back_keep(v):
    return (v, None)

def back_low(kept, grad):
    return (low(grad),)
low.defvjp(low_keep, low_pass)
low_back.defvjp(back_keep, back_low)

def angles(positions, head_size):
    steps_half = jnp.arange(head_size // 2).astype(jnp.float32)
    frequency = jnp.exp(steps_half * (-2.0 * math.log(ROPE_BASE) / head_size))
    turned = positions.astype(jnp.float32)[:, None] * frequency[None, :]
    return (jnp.cos(turned), jnp.sin(turned))

def rotate(values, cosine, sine_table):
    half_width = values.shape[-1] // 2
    first_half = values[..., :half_width]
    second_half = values[..., half_width:]
    return jnp.concatenate([first_half * cosine - second_half * sine_table, second_half * cosine + first_half * sine_table], axis=-1)

def scaled_norm(values, gain_row):
    rate = lax.rsqrt(lax.optimization_barrier(jnp.mean(values * values, axis=-1, keepdims=True)) + EPSILON)
    return values * rate * gain_row

def layer_forward(tokens, attn_gain, q_gain, k_gain, w_query, w_key, w_value, w_out, mlp_gain, router, w_gate, w_up, w_down, lengths, routes):
    slot_count, seq_len, model_width = tokens.shape
    head_count, head_size = q_gain.shape
    expert_count = router.shape[1]
    flat_rows = tokens.reshape(slot_count * seq_len, model_width)
    normed = low(scaled_norm(flat_rows, attn_gain))
    q_proj = low_back(jnp.dot(normed, w_query, precision=HIGHEST_PRECISION))
    k_proj = low_back(jnp.dot(normed, w_key, precision=HIGHEST_PRECISION))
    value_rows = low(low_back(jnp.dot(normed, w_value, precision=HIGHEST_PRECISION)))
    q_norm = scaled_norm(q_proj, q_gain.reshape(model_width))
    k_norm = scaled_norm(k_proj, k_gain.reshape(model_width))
    positions = jnp.arange(seq_len).astype(jnp.int32)
    cosine, sine_table = angles(positions, head_size)
    cosine = cosine[:, None, :]
    sine_table = sine_table[:, None, :]
    queries = low(rotate(q_norm.reshape(slot_count, seq_len, head_count, head_size), cosine, sine_table))
    key_rows = low(rotate(k_norm.reshape(slot_count, seq_len, head_count, head_size), cosine, sine_table))
    value_heads = value_rows.reshape(slot_count, seq_len, head_count, head_size)
    scale_factor = head_size ** (-0.5)

    def attend(block_in):
        query_set, key_set, value_set, slot_length = block_in
        scores = low_back(jnp.einsum('qhd,khd->hqk', query_set, key_set, precision=HIGHEST_PRECISION) * scale_factor)
        allowed = (positions[None, :] <= positions[:, None]) & (positions[None, :] < slot_length)
        attn_probs = jax.nn.softmax(jnp.where(allowed[None], scores, -1e+30), axis=-1)
        mixed = jnp.einsum('hqk,khd->qhd', low(attn_probs), value_set, precision=HIGHEST_PRECISION)
        return low_back(mixed)
    attended = lax.map(jax.checkpoint(attend), (queries, key_rows, value_heads, lengths))
    attended = low(attended.reshape(slot_count * seq_len, model_width))
    middle = flat_rows + low_back(jnp.dot(attended, w_out, precision=HIGHEST_PRECISION))
    mixed_in = low(scaled_norm(middle, mlp_gain))
    logits = low_back(jnp.dot(mixed_in, router, precision=HIGHEST_PRECISION))
    route_probs = jax.nn.softmax(logits, axis=-1)
    expert_ids = jnp.arange(expert_count).astype(jnp.int32)
    flat_routes = routes.reshape(slot_count * seq_len, routes.shape[-1])
    chosen = lax.optimization_barrier(jnp.sum((flat_routes[:, :, None] == expert_ids[None, None, :]).astype(jnp.float32), axis=1))
    gate_values = route_probs * chosen

    def expert(carried, block_in):
        gate_w, up_w, down_w, gate_share = block_in
        gate_h = low_back(jnp.dot(mixed_in, gate_w, precision=HIGHEST_PRECISION))
        up_h = low_back(jnp.dot(mixed_in, up_w, precision=HIGHEST_PRECISION))
        activated = low(jax.nn.silu(gate_h) * up_h)
        expert_out = low_back(jnp.dot(activated, down_w, precision=HIGHEST_PRECISION))
        return (carried + gate_share[:, None] * expert_out, None)
    mixture, unused_out = lax.scan(jax.checkpoint(expert), jnp.zeros_like(middle), (w_gate, w_up, w_down, gate_values.T))
    return (middle + mixture).reshape(slot_count, seq_len, model_width)

def reference(tokens, lengths, routes, attn_gain, q_gain, k_gain, w_query, w_key, w_value, w_out, mlp_gain, router, w_gate, w_up, w_down, cotangent):
    float_args = tuple((item.astype(jnp.float32) for item in (tokens, attn_gain, q_gain, k_gain, w_query, w_key, w_value, w_out, mlp_gain, router, w_gate, w_up, w_down)))

    def apply_layer(*values):
        return layer_forward(*values, lengths, routes)
    result, pullback = jax.vjp(apply_layer, *float_args)
    positions = jnp.arange(tokens.shape[1]).astype(jnp.int32)
    valid_mask = (positions[None, :] < lengths[:, None]).astype(jnp.float32)
    all_grads = pullback(cotangent.astype(jnp.float32) * valid_mask[:, :, None])
    return (result.astype(jnp.bfloat16), all_grads[0], all_grads[1], all_grads[2], all_grads[3], all_grads[4], all_grads[5], all_grads[6], all_grads[7], all_grads[8], all_grads[9], all_grads[10], all_grads[11], all_grads[12])
```

```python
import math

import jax
import jax.numpy as jnp
from jax import lax
from jax.sharding import Mesh
from jax.sharding import PartitionSpec as P

EPSILON = 1e-05
ROPE_BASE = 10000.0
BF = jnp.bfloat16
F32 = jnp.float32

AXES = ("x", "z", "yl", "yh", "c")
SIZES = (4, 4, 2, 2, 2)
CONTEXT = ("z", "yl")
TENSOR = ("yh", "c")
WEIGHT = ("x", "z", "yl")
Y = ("yl", "yh")
SWAP = ("yl", "c")


def exchange(axes, size, mask):
    pairs = [(at, at ^ mask) for at in range(size)]
    return lambda v: lax.ppermute(v, axes, pairs)


CUBE = (exchange("z", 4, 1), exchange(Y, 4, 2), exchange("z", 4, 3), exchange(Y, 4, 3))
swap_cores = lambda v: lax.ppermute(v, SWAP, [(0, 0), (1, 2), (2, 1), (3, 3)])


def dot(a, b, left=1, right=0):
    return lax.dot_general(a, b, (((left,), (right,)), ((), ())), preferred_element_type=F32)


def cube_gather(own):
    rows = own.shape[0] // 4
    parts = [own[i * rows : (i + 1) * rows] for i in range(4)]
    for step in range(4):
        arrived = lax.optimization_barrier(
            tuple(CUBE[(i + step) % 4](parts[i]) for i in range(4))
        )
        parts = [jnp.concatenate([a, b], axis=0) for a, b in zip(parts, arrived)]
    return jnp.concatenate(parts, axis=0)


def cube_scatter(total):
    rows = total.shape[0] // 4
    parts = [total[i * rows : (i + 1) * rows] for i in range(4)]
    for step in (3, 2, 1, 0):
        half = parts[0].shape[0] // 2
        arrived = lax.optimization_barrier(
            tuple(CUBE[(i + step) % 4](parts[i][half:].astype(BF)) for i in range(4))
        )
        parts = [a[:half].astype(F32) + b.astype(F32) for a, b in zip(parts, arrived)]
    return jnp.concatenate(parts, axis=0)


def cube_sum(rows_of):
    count = rows_of.shape[1]
    held = rows_of.reshape(4, 2, 2, 2, 2, 16, count)
    for dim in range(4):
        arrived = CUBE[dim](held)
        turned = jnp.stack(
            [jnp.flip(arrived[i], axis=3 - (dim - i) % 4) for i in range(4)], axis=0
        )
        held = held + turned
    return held.reshape(rows_of.shape)


def row_positions():
    at = jnp.arange(1024, dtype=jnp.int32)
    part, block, row = at >> 8, (at >> 4) & 15, at & 15
    turned = [(block >> ((dim - part) & 3)) & 1 for dim in range(4)]
    z = lax.axis_index("z") ^ (turned[0] ^ (3 * turned[2]))
    y = (2 * lax.axis_index("yh") + lax.axis_index("yl")) ^ (turned[1] ^ (3 * turned[3]))
    return (2 * z + (y & 1)) * 128 + (y >> 1) * 64 + 16 * part + row


def angles(positions, head_size):
    steps_half = jnp.arange(head_size // 2).astype(F32)
    frequency = jnp.exp(steps_half * (-2.0 * math.log(ROPE_BASE) / head_size))
    turned = positions.astype(F32)[:, None] * frequency[None, :]
    return (jnp.cos(turned), jnp.sin(turned))


def rotate(values, cosine, sine_table):
    half_width = values.shape[-1] // 2
    first_half = values[..., :half_width]
    second_half = values[..., half_width:]
    return jnp.concatenate(
        [
            first_half * cosine - second_half * sine_table,
            second_half * cosine + first_half * sine_table,
        ],
        axis=-1,
    )


def spread(packed):
    held = lax.all_to_all(packed, "z", split_axis=0, concat_axis=0, tiled=True)
    held = swap_cores(held)
    held = lax.all_gather(held, "x", axis=0, tiled=False)
    held = lax.all_gather(held, "c", axis=2, tiled=False)
    return held.reshape(2048, packed.shape[-1])


def collect(grads):
    width = grads.shape[-1]
    held = grads.astype(BF).reshape(4, 4, 2, 64, width)
    held = lax.psum_scatter(held, "c", scatter_dimension=2, tiled=False)
    held = lax.psum_scatter(held, "x", scatter_dimension=0, tiled=False)
    held = swap_cores(held)
    return lax.all_to_all(held, "z", split_axis=0, concat_axis=0, tiled=True)


def per_device(
    tokens,
    lengths,
    routes,
    attn_gain,
    q_gain,
    k_gain,
    w_query,
    w_key,
    w_value,
    w_out,
    mlp_gain,
    router,
    w_gate,
    w_up,
    w_down,
    cotangent,
):
    z = lax.axis_index("z")
    yh = lax.axis_index("yh")
    core = lax.axis_index("c")

    def four(w):
        return w.reshape(64, 4, -1).transpose(1, 0, 2)

    def pack_experts(w):
        return four(w.transpose(1, 0, 2).reshape(64, 2560))

    def per_row(v):
        return jnp.broadcast_to(v[None], (4,) + v.shape)

    gains = jnp.stack([q_gain, k_gain], axis=-1)
    extra = jnp.concatenate(
        [
            per_row(attn_gain[:, None]),
            per_row(mlp_gain[:, None]),
            per_row(router),
            jnp.pad(gains, ((0, 0), (0, 60), (0, 0))),
            jnp.zeros((4, 64, 114), BF),
        ],
        axis=-1,
    )
    first_pack = jnp.concatenate(
        [four(w_query), four(w_key), four(w_value), extra, four(w_out.T)], axis=-1
    )
    second_pack = jnp.concatenate(
        [pack_experts(w_gate), pack_experts(w_up), four(w_down.reshape(2560, 64).T)], axis=-1
    )
    first_all = spread(first_pack)
    second_all = spread(second_pack)
    w_qkv = first_all[:, :384]
    extra_all = first_all[:, 384:512]
    out_t = first_all[:, 512:]
    w_in = second_all[:, :1280]
    down_t = second_all[:, 1280:]
    attn_row = extra_all[:, 0].astype(F32)[None]
    mlp_row = extra_all[:, 1].astype(F32)[None]
    router_all = jnp.pad(extra_all[:, 2:12], ((0, 0), (0, 118)))
    gain_rows = extra_all[:, 12:14].reshape(32, 64, 2)[:, :4].reshape(128, 2).T.astype(F32)
    q_row, k_row = gain_rows[:1], gain_rows[1:]

    own_start = (core, yh * 64, 0)
    own_tokens = lax.dynamic_slice(tokens, own_start, (1, 64, 2048))[0]
    own_cot = lax.dynamic_slice(cotangent, own_start, (1, 64, 2048))[0]
    own_routes = lax.dynamic_slice(routes, own_start, (1, 64, 8))[0]
    slot_length = lax.dynamic_index_in_dim(lengths, core, keepdims=False)
    expert_ids = jnp.arange(10, dtype=jnp.int32)
    own_chosen = jnp.sum((own_routes[:, :, None] == expert_ids).astype(BF), axis=1)
    all_tokens = cube_gather(own_tokens)
    with_routes = cube_gather(
        jnp.concatenate([own_cot, jnp.pad(own_chosen, ((0, 0), (0, 118)))], axis=1)
    )
    positions = row_positions()
    valid = positions < slot_length
    grad_out = jnp.where(valid[:, None], with_routes[:, :2048], jnp.zeros((), BF))
    chosen = with_routes[:, 2048:2058].astype(F32)
    own_valid = (
        (2 * z + lax.axis_index("yl")) * 128 + yh * 64 + jnp.arange(64, dtype=jnp.int32)
    ) < slot_length
    own_grad_out = jnp.where(own_valid[:, None], own_cot.astype(F32), 0.0)

    all_rows = all_tokens.astype(F32)
    all_rate = lax.rsqrt(jnp.mean(all_rows * all_rows, axis=-1, keepdims=True) + EPSILON)
    normed = (all_rows * all_rate * attn_row).astype(BF)
    qkv = dot(normed, w_qkv)
    q_proj, k_proj = qkv[:, :128], qkv[:, 128:256]
    values = qkv[:, 256:].astype(BF)
    squares = cube_sum(
        jnp.stack([jnp.sum(q_proj * q_proj, axis=1), jnp.sum(k_proj * k_proj, axis=1)], axis=1)
    )
    rates = lax.rsqrt(squares / 2048 + EPSILON)
    q_rate, k_rate = rates[:, :1], rates[:, 1:]
    cosine, sine_table = angles(positions, 128)
    queries = rotate(q_proj * q_rate * q_row, cosine, sine_table).astype(BF)
    keys = rotate(k_proj * k_rate * k_row, cosine, sine_table).astype(BF)
    allowed = (positions[None, :] <= positions[:, None]) & valid[None, :]
    scale = 128 ** (-0.5)
    scores = jnp.where(allowed, dot(queries, keys, 1, 1) * scale, -1e30)
    peak = jnp.max(scores, axis=-1, keepdims=True)
    raised = jnp.where(allowed, jnp.exp(scores - peak), 0.0)
    row_total = jnp.sum(raised, axis=-1, keepdims=True)
    probs = raised / row_total
    low_probs = probs.astype(BF)
    attended = dot(low_probs, values).astype(BF)
    own_rows = own_tokens.astype(F32)
    middle = own_rows + cube_scatter(dot(attended, out_t, 1, 1))

    second_rate = lax.rsqrt(jnp.mean(middle * middle, axis=-1, keepdims=True) + EPSILON)
    mixed_in = cube_gather((middle * second_rate * mlp_row).astype(BF))
    logits = dot(mixed_in, router_all)[:, :10]
    route_probs = jax.nn.softmax(logits, axis=-1)
    gate_values = route_probs * chosen
    tile_expert = (5 * z + jnp.arange(5, dtype=jnp.int32)) // 2
    tile_of = (tile_expert[None, :] == expert_ids[:, None]).astype(F32)
    tile_gates = jnp.sum(gate_values[:, :, None] * tile_of[None], axis=1)
    wide_gates = jnp.repeat(tile_gates, 128, axis=1)
    hidden = dot(mixed_in, w_in)
    gate_h, up_h = hidden[:, :640], hidden[:, 640:]
    sig = jax.nn.sigmoid(gate_h)
    silu = gate_h * sig
    activated = (silu * up_h).astype(BF).astype(F32)
    gated = (activated * wide_gates).astype(BF)
    mixture = cube_scatter(dot(gated, down_t, 1, 1))
    own_output = (middle + mixture).astype(BF)
    out_grad = dot(grad_out, down_t)
    tile_parts = jnp.sum((activated * out_grad).reshape(1024, 5, 128), axis=-1)
    gate_part = jnp.sum(tile_parts[:, None, :] * tile_of[None], axis=-1)
    act_grad = out_grad * wide_gates
    gate_h_grad = (act_grad * up_h * sig * (1.0 + gate_h * (1.0 - sig))).astype(BF)
    up_h_grad = (act_grad * silu).astype(BF)
    chosen_grad = gate_part * chosen
    logit_grad = (
        route_probs * (chosen_grad - jnp.sum(chosen_grad * route_probs, axis=-1, keepdims=True))
    ).astype(BF)
    hidden_grad = jnp.concatenate(
        [gate_h_grad, up_h_grad, jnp.pad(logit_grad, ((0, 0), (0, 118)))], axis=1
    )
    in_grads = dot(mixed_in, hidden_grad, 0, 0)
    down_grads = dot(grad_out, gated, 0, 0)
    mixed_grad = cube_scatter(
        dot(hidden_grad, jnp.concatenate([w_in, router_all], axis=1), 1, 1)
    )
    expert_grads = collect(jnp.concatenate([in_grads, down_grads], axis=1))
    scaled = mixed_grad * mlp_row
    middle_grad = (
        own_grad_out
        + second_rate * scaled
        - middle * second_rate**3 * jnp.mean(scaled * middle, axis=-1, keepdims=True)
    )

    branch_grad = cube_gather(middle_grad.astype(BF))
    out_grads = dot(branch_grad, attended, 0, 0)
    attended_grad = dot(branch_grad, out_t).astype(BF)
    prob_grad = dot(attended_grad, values, 1, 1)
    delta = jnp.sum(probs * prob_grad, axis=-1, keepdims=True)
    score_grad = (probs * (prob_grad - delta)).astype(BF)
    query_grad = dot(score_grad, keys) * scale
    key_grad = dot(score_grad, queries, 0, 0) * scale
    v_proj_grad = dot(low_probs, attended_grad, 0, 0).astype(BF)
    q_norm_grad = rotate(query_grad, cosine, -sine_table)
    k_norm_grad = rotate(key_grad, cosine, -sine_table)
    q_scaled = q_norm_grad * q_row
    k_scaled = k_norm_grad * k_row
    inner = cube_sum(
        jnp.stack([jnp.sum(q_scaled * q_proj, axis=1), jnp.sum(k_scaled * k_proj, axis=1)], axis=1)
    )
    q_proj_grad = (q_rate * q_scaled - q_proj * q_rate**3 * inner[:, :1] / 2048).astype(BF)
    k_proj_grad = (k_rate * k_scaled - k_proj * k_rate**3 * inner[:, 1:] / 2048).astype(BF)
    qkv_grad = jnp.concatenate([q_proj_grad, k_proj_grad, v_proj_grad], axis=1)
    qkv_grads = dot(normed, qkv_grad, 0, 0)
    normed_grad = cube_scatter(dot(qkv_grad, w_qkv, 1, 1))
    gain_grads = jnp.stack(
        [
            jnp.sum(q_norm_grad * q_proj * q_rate, axis=0),
            jnp.sum(k_norm_grad * k_proj * k_rate, axis=0),
        ],
        axis=1,
    )
    gain_block = jnp.pad(gain_grads.reshape(32, 4, 2), ((0, 0), (0, 60), (0, 126)))
    attn_grads = collect(
        jnp.concatenate([qkv_grads, out_grads, gain_block.reshape(2048, 128)], axis=1)
    )
    scaled = normed_grad * attn_row
    own_rate = lax.rsqrt(jnp.mean(own_rows * own_rows, axis=-1, keepdims=True) + EPSILON)
    own_input_grad = (
        middle_grad
        + own_rate * scaled
        - own_rows * own_rate**3 * jnp.mean(scaled * own_rows, axis=-1, keepdims=True)
    )

    def whole(own):
        held = lax.all_gather(own, "yh", axis=0, tiled=True)
        return lax.all_gather(held, "c", axis=0, tiled=False)

    def wide(grads):
        return grads.transpose(1, 0, 2).reshape(64, -1).astype(F32)

    def experts(grads):
        return wide(grads).reshape(64, 10, 256).transpose(1, 0, 2)

    q_grads = wide(attn_grads[:, :, :128])
    k_grads = wide(attn_grads[:, :, 128:256])
    v_grads = wide(attn_grads[:, :, 256:384])
    o_grads = wide(attn_grads[:, :, 384:512]).T
    q_gain_grad = attn_grads[:, :4, 512].astype(F32)
    k_gain_grad = attn_grads[:, :4, 513].astype(F32)
    gate_grads = experts(expert_grads[:, :, :640])
    up_grads = experts(expert_grads[:, :, 640:1280])
    router_part = jnp.sum(expert_grads[:, :, 1280:1290].astype(F32), axis=0)
    down_out = wide(expert_grads[:, :, 1408:]).T.reshape(10, 256, 64)

    def row_sums(*pairs):
        return sum(jnp.sum(w.astype(F32) * g, axis=tuple(range(2, w.ndim)) or None) for w, g in pairs)

    attn_part = sum(
        jnp.sum(w.astype(F32) * g, axis=1)
        for w, g in ((w_query, q_grads), (w_key, k_grads), (w_value, v_grads))
    )
    mlp_part = sum(
        jnp.sum(w.astype(F32) * g, axis=(0, 2)) for w, g in ((w_gate, gate_grads), (w_up, up_grads))
    ) + jnp.sum(router.astype(F32) * router_part, axis=1)
    summed = lax.psum(
        jnp.concatenate([router_part, attn_part[:, None], mlp_part[:, None]], axis=1), TENSOR
    )
    return (
        whole(own_output),
        whole(own_input_grad.astype(BF)).astype(F32),
        summed[:, 10] / attn_gain.astype(F32),
        q_gain_grad,
        k_gain_grad,
        q_grads,
        k_grads,
        v_grads,
        o_grads,
        summed[:, 11] / mlp_gain.astype(F32),
        summed[:, :10],
        gate_grads,
        up_grads,
        down_out,
    )


def solution(mesh):
    fine = Mesh(mesh.devices.reshape(SIZES), AXES)
    rows = P("x", CONTEXT, None)
    vector = P(WEIGHT)
    gains = P(TENSOR, WEIGHT)
    tall = P(WEIGHT, TENSOR)
    routed = P(WEIGHT, None)
    hidden = P(None, WEIGHT, TENSOR)
    back = P(None, TENSOR, WEIGHT)
    weights = (vector, gains, gains, tall, tall, tall, gains, vector, routed, hidden, hidden, back)
    return jax.shard_map(
        per_device,
        mesh=fine,
        in_specs=(rows, P("x"), rows) + weights + (rows,),
        out_specs=(rows, rows) + weights,
        check_vma=False,
    )
```

```python
import math

import jax
import jax.numpy as jnp
from jax import lax
from jax.sharding import Mesh
from jax.sharding import PartitionSpec as P
from jax.experimental import pallas as pl
from jax.experimental.pallas import tpu as pltpu

EPSILON = 1e-05
ROPE_BASE = 10000.0
BF = jnp.bfloat16
F32 = jnp.float32

AXES = ("x", "z", "yl", "yh", "c")
SIZES = (4, 4, 2, 2, 2)
CONTEXT = ("z", "yl")
TENSOR = ("yh", "c")
WEIGHT = ("x", "z", "yl")
Y = ("yl", "yh")
SWAP = ("yl", "c")


def exchange(axes, size, mask):
    pairs = [(at, at ^ mask) for at in range(size)]
    return lambda v: lax.ppermute(v, axes, pairs)


CUBE = (exchange("z", 4, 1), exchange(Y, 4, 2), exchange("z", 4, 3), exchange(Y, 4, 3))
swap_cores = lambda v: lax.ppermute(v, SWAP, [(0, 0), (1, 2), (2, 1), (3, 3)])
other_core = exchange("c", 2, 1)
other_half = exchange("yh", 2, 1)
GROUP = ("z", "yl", "yh")
VMEM = pl.BlockSpec(memory_space=pltpu.VMEM)
SMEM = pl.BlockSpec(memory_space=pltpu.SMEM)
LIMIT = 56 * 1024 * 1024


def dot(a, b, left=1, right=0):
    return lax.dot_general(a, b, (((left,), (right,)), ((), ())), preferred_element_type=F32)


def kernel_call(body, outs, in_specs, cost=None):
    return pl.pallas_call(
        body,
        out_shape=[jax.ShapeDtypeStruct(shape, kind) for shape, kind in outs],
        in_specs=in_specs,
        out_specs=[VMEM] * len(outs),
        compiler_params=pltpu.CompilerParams(vmem_limit_bytes=LIMIT),
        cost_estimate=cost,
    )


def cube_gather(own):
    rows = own.shape[0] // 4
    parts = [own[i * rows : (i + 1) * rows] for i in range(4)]
    for step in range(4):
        arrived = [CUBE[(i + step) % 4](parts[i]) for i in range(4)]
        if step < 3:
            parts = [jnp.concatenate([a, b], axis=0) for a, b in zip(parts, arrived)]
    return jnp.concatenate(parts + arrived, axis=0)


def project_kernel(rows_ref, weight_ref, *outs):
    for at, out in enumerate(outs):
        out[...] = dot(rows_ref[at * 128 : (at + 1) * 128, :], weight_ref[...], 1, 1).astype(BF)


def project(rows, weight):
    depth = rows.shape[1]
    return pl.pallas_call(
        project_kernel,
        grid=(4,),
        out_shape=[jax.ShapeDtypeStruct((128, 2048), BF)] * 8,
        in_specs=[
            pl.BlockSpec((1024, depth), lambda n: (0, 0)),
            pl.BlockSpec((512, depth), lambda n: (n, 0)),
        ],
        out_specs=[pl.BlockSpec((128, 512), lambda n: (0, n))] * 8,
        compiler_params=pltpu.CompilerParams(vmem_limit_bytes=LIMIT),
        cost_estimate=pl.CostEstimate(
            flops=2 * 1024 * 2048 * depth,
            bytes_accessed=2 * (3072 * depth + 1024 * 2048),
            transcendentals=0,
        ),
    )(rows, weight)


def fold_kernel(*refs):
    half = refs[0].shape[0] // 2
    for i in range(4):
        kept, arrived, keep, send = refs[i], refs[4 + i], refs[8 + i], refs[12 + i]
        keep[...] = (kept[:half].astype(F32) + arrived[:half].astype(F32)).astype(BF)
        send[...] = (kept[half:].astype(F32) + arrived[half:].astype(F32)).astype(BF)


def cube_scatter(pieces):
    kept, sent = pieces[:4], pieces[4:]
    for step in (3, 2, 1, 0):
        arrived = [CUBE[(i + step) % 4](sent[i]) for i in range(4)]
        if step:
            half = ((kept[0].shape[0] // 2, 2048), BF)
            folded = kernel_call(fold_kernel, [half] * 8, [VMEM] * 8)(*kept, *arrived)
            kept, sent = folded[:4], folded[4:]
    return jnp.concatenate([a.astype(F32) + b.astype(F32) for a, b in zip(kept, arrived)], axis=0)


def block_places():
    at = jnp.arange(64, dtype=jnp.int32)
    part, block = (at >> 3) & 3, (at & 7) | ((at >> 5) << 3)
    turned = [(block >> ((dim - part) & 3)) & 1 for dim in range(4)]
    z = lax.axis_index("z") ^ (turned[0] ^ (3 * turned[2]))
    y = (2 * lax.axis_index("yh") + lax.axis_index("yl")) ^ (turned[1] ^ (3 * turned[3]))
    return ((2 * z + (y & 1)) * 2 + (y >> 1)) * 4 + part


def cotangent_kernel(places, length, source, grad, chosen):
    row = lax.broadcasted_iota(jnp.int32, (16, 2048), 0)
    for at in range(64):
        start = pl.multiple_of(places[at] * 16, 16)
        held = source[pl.ds(start, 16), :]
        inside = row < length[0] - start
        grad[at * 16 : (at + 1) * 16, :] = jnp.where(inside, held[:, :2048], jnp.zeros((), BF))
        chosen[at * 16 : (at + 1) * 16, :] = held[:, 2048:]


def place_kernel(places, source, out):
    for at in range(64):
        out[pl.ds(pl.multiple_of(places[at] * 16, 16), 16), :] = source[at * 16 : (at + 1) * 16, :]


def token_sums(columns, place_of):
    count = len(columns)
    held = jnp.stack([v.reshape(64, 16) for v in columns], axis=1).reshape(64, 16 * count)
    placed = lax.dot_general(
        place_of, held, (((0,), (0,)), ((), ())), precision=lax.Precision.HIGHEST
    )
    sent = jnp.broadcast_to(placed[None], (16,) + placed.shape)
    total = jnp.sum(lax.all_to_all(sent, GROUP, split_axis=0, concat_axis=0, tiled=True), axis=0)
    back = lax.dot_general(
        place_of, total, (((1,), (0,)), ((), ())), precision=lax.Precision.HIGHEST
    )
    return back.reshape(64, count, 16).transpose(0, 2, 1).reshape(1024, count)


def angles(positions, head_size):
    steps_half = jnp.arange(head_size // 2).astype(F32)
    frequency = jnp.exp(steps_half * (-2.0 * math.log(ROPE_BASE) / head_size))
    turned = positions.astype(F32)[:, None] * frequency[None, :]
    cosine, sine = jnp.cos(turned), jnp.sin(turned)
    return (
        jnp.concatenate([cosine, cosine], axis=-1),
        jnp.concatenate([-sine, sine], axis=-1),
    )


SCALE = 128 ** (-0.5)


def forward_kernel(
    qkv, rates, gains, cosine, sine, q_pos, k_pos, queries, keys, values, attended, log_total
):
    def turn(held):
        return held * cosine[...] + pltpu.roll(held, 64, 1) * sine[...]

    queries[...] = turn(qkv[:, :128] * rates[:, 0:1] * gains[0:1, :]).astype(BF)
    keys[...] = turn(qkv[:, 128:256] * rates[:, 1:2] * gains[1:2, :]).astype(BF)
    values[...] = qkv[:, 256:].astype(BF)
    for at in range(4):
        rows = slice(at * 256, (at + 1) * 256)
        scores = dot(queries[rows, :], keys[...], 1, 1) * SCALE
        scores = jnp.where(k_pos[...] <= q_pos[rows, :], scores, -1e30)
        peak = jnp.max(scores, axis=1, keepdims=True)
        raised = jnp.exp(scores - peak)
        total = jnp.sum(raised, axis=1, keepdims=True)
        probs = (raised * (1.0 / total)).astype(BF)
        attended[rows, :] = dot(probs, values[...]).astype(BF)
        log_total[rows, :] = peak + jnp.log(total)


def backward_kernel(
    qkv, rates, gains, cosine, sine, q_pos, k_pos, queries, keys, values, log_total, grad,
    q_scaled, k_scaled, v_grad, inner, gain_grads, key_grad, value_grad,
):
    def turn_back(held):
        return held * cosine[...] - pltpu.roll(held, 64, 1) * sine[...]

    for at in range(4):
        rows = slice(at * 256, (at + 1) * 256)
        scores = dot(queries[rows, :], keys[...], 1, 1) * SCALE
        allowed = k_pos[...] <= q_pos[rows, :]
        probs = jnp.where(allowed, jnp.exp(scores - log_total[rows, :]), 0.0)
        prob_grad = dot(grad[rows, :], values[...], 1, 1)
        delta = jnp.sum(probs * prob_grad, axis=1, keepdims=True)
        score_grad = (probs * (prob_grad - delta)).astype(BF)
        q_scaled[rows, :] = dot(score_grad, keys[...]) * SCALE
        key_part = dot(score_grad, queries[rows, :], 0, 0) * SCALE
        value_part = dot(probs.astype(BF), grad[rows, :], 0, 0)
        if at == 0:
            key_grad[...] = key_part
            value_grad[...] = value_part
        else:
            key_grad[...] += key_part
            value_grad[...] += value_part
    v_grad[...] = value_grad[...].astype(BF)
    q_norm_grad = turn_back(q_scaled[...])
    k_norm_grad = turn_back(key_grad[...])
    q_turned = q_norm_grad * qkv[:, :128]
    k_turned = k_norm_grad * qkv[:, 128:256]
    gain_grads[0:1, :] = jnp.sum(q_turned * rates[:, 0:1], axis=0, keepdims=True)
    gain_grads[1:2, :] = jnp.sum(k_turned * rates[:, 1:2], axis=0, keepdims=True)
    inner[:, 0:1] = jnp.sum(q_turned * gains[0:1, :], axis=1, keepdims=True)
    inner[:, 1:2] = jnp.sum(k_turned * gains[1:2, :], axis=1, keepdims=True)
    q_scaled[...] = q_norm_grad * gains[0:1, :]
    k_scaled[...] = k_norm_grad * gains[1:2, :]


def attention_cost(products):
    return pl.CostEstimate(
        flops=products * 2 * 1024 * 1024 * 128, bytes_accessed=6 << 20, transcendentals=1 << 20
    )


def core_fold(grads):
    held = grads.astype(BF)
    return (held[:1024].astype(F32) + other_core(held[1024:]).astype(F32)).astype(BF)


def per_device(
    tokens,
    lengths,
    routes,
    attn_gain,
    q_gain,
    k_gain,
    w_query,
    w_key,
    w_value,
    w_out,
    mlp_gain,
    router,
    w_gate,
    w_up,
    w_down,
    cotangent,
):
    z = lax.axis_index("z")
    yh = lax.axis_index("yh")
    core = lax.axis_index("c")

    def four(w):
        return w.reshape(64, 4, -1).transpose(1, 0, 2)

    def pack_experts(w):
        return four(w.transpose(1, 0, 2).reshape(64, 2560))

    def per_row(v):
        return jnp.broadcast_to(v[None], (4,) + v.shape)

    gains = jnp.stack([q_gain, k_gain], axis=-1)
    extra = jnp.concatenate(
        [
            per_row(attn_gain[:, None]),
            per_row(mlp_gain[:, None]),
            per_row(router),
            jnp.pad(gains, ((0, 0), (0, 60), (0, 0))),
            jnp.zeros((4, 64, 114), BF),
        ],
        axis=-1,
    )
    first_pack = jnp.concatenate(
        [four(w_query), four(w_key), four(w_value), extra, four(w_out.T)], axis=-1
    )
    second_pack = jnp.concatenate(
        [pack_experts(w_gate), pack_experts(w_up), four(w_down.reshape(2560, 64).T)], axis=-1
    )
    first_held = swap_cores(first_pack)
    first_held = lax.all_to_all(
        jnp.broadcast_to(first_held[None], (4, 4, 64, 640)).reshape(16, 64, 640),
        ("x", "z"),
        split_axis=0,
        concat_axis=0,
        tiled=True,
    ).reshape(1024, 640)
    first_all = jnp.concatenate([first_held, other_core(first_held)], axis=0)
    second_held = lax.all_to_all(
        swap_cores(second_pack), "z", split_axis=0, concat_axis=0, tiled=True
    )
    second_held = lax.all_gather(second_held, "x", axis=0, tiled=False).reshape(1024, 1920)
    second_all = jnp.concatenate([second_held, other_core(second_held)], axis=0)
    w_qkv = first_all[:, :384]
    extra_all = first_all[:, 384:512]
    out_t = first_all[:, 512:]
    w_in = second_all[:, :1280]
    down_t = second_all[:, 1280:]
    attn_row = extra_all[:, 0].astype(F32)[None]
    mlp_row = extra_all[:, 1].astype(F32)[None]
    router_all = jnp.pad(extra_all[:, 2:12], ((0, 0), (0, 118)))
    gain_blocks = extra_all[:, 12:14].reshape(2, 16, 64, 2)[:, :, :4]
    gain_blocks = jnp.where(core == 0, gain_blocks, gain_blocks[::-1])
    gain_rows = gain_blocks.transpose(3, 1, 0, 2).reshape(2, 128).astype(F32)

    own_start = (core, yh * 64, 0)
    own_tokens = lax.dynamic_slice(tokens, own_start, (1, 64, 2048))[0]
    own_cot = lax.dynamic_slice(cotangent, own_start, (1, 64, 2048))[0]
    own_routes = lax.dynamic_slice(routes, own_start, (1, 64, 8))[0]
    slot_length = lax.dynamic_index_in_dim(lengths, core, keepdims=False)
    expert_ids = jnp.arange(10, dtype=jnp.int32)
    own_chosen = jnp.sum((own_routes[:, :, None] == expert_ids).astype(BF), axis=1)

    def own_first(v):
        halves = v.reshape(64, 16, 2, 64)
        halves = jnp.where(core == 0, halves, halves[:, :, ::-1])
        return halves.transpose(0, 2, 1, 3).reshape(64, 2048)

    def natural(v):
        halves = v.reshape(64, 2, 16, 64).transpose(0, 2, 1, 3)
        return jnp.where(core == 0, halves, halves[:, :, ::-1]).reshape(64, 2048)

    own_tokens = own_first(own_tokens)
    own_cot = own_first(own_cot)
    all_tokens = cube_gather(own_tokens)
    with_routes = lax.all_gather(
        jnp.concatenate([own_cot, jnp.pad(own_chosen, ((0, 0), (0, 118)))], axis=1),
        GROUP,
        axis=0,
        tiled=True,
    )
    places = block_places()
    place_of = (places[:, None] == jnp.arange(64, dtype=jnp.int32)[None]).astype(F32)
    positions = (places[:, None] * 16 + jnp.arange(16, dtype=jnp.int32)[None]).reshape(1024)
    grad_out, chosen = kernel_call(
        cotangent_kernel, [((1024, 2048), BF), ((1024, 128), BF)], [SMEM, SMEM, VMEM]
    )(places, slot_length[None], with_routes)
    chosen = chosen[:, :10].astype(F32)
    own_positions = (
        (2 * z + lax.axis_index("yl")) * 128 + yh * 64 + jnp.arange(64, dtype=jnp.int32)
    )
    own_grad_out = jnp.where((own_positions < slot_length)[:, None], own_cot.astype(F32), 0.0)

    all_rows = all_tokens.astype(F32)
    all_rate = lax.rsqrt(jnp.mean(all_rows * all_rows, axis=-1, keepdims=True) + EPSILON)
    normed = (all_rows * all_rate * attn_row).astype(BF)
    qkv = dot(normed, w_qkv)
    squares = token_sums(
        [
            jnp.sum(qkv[:, :128] * qkv[:, :128], axis=1),
            jnp.sum(qkv[:, 128:256] * qkv[:, 128:256], axis=1),
        ],
        place_of,
    )
    rates = lax.rsqrt(squares / 2048 + EPSILON)
    cosine, sine = angles(positions, 128)
    q_pos = positions[:, None]
    k_pos = jnp.where(positions < slot_length, positions, 1 << 20)[None]
    head = ((1024, 128), BF)
    queries, keys, values, attended, log_total = kernel_call(
        forward_kernel, [head, head, head, head, ((1024, 1), F32)], [VMEM] * 7, attention_cost(2)
    )(qkv, rates, gain_rows, cosine, sine, q_pos, k_pos)
    own_rows = own_tokens.astype(F32)
    middle = own_rows + cube_scatter(project(attended, out_t))

    second_rate = lax.rsqrt(jnp.mean(middle * middle, axis=-1, keepdims=True) + EPSILON)
    mixed_in = cube_gather((middle * second_rate * mlp_row).astype(BF))
    logits = dot(mixed_in, router_all)[:, :10]
    route_probs = jax.nn.softmax(logits, axis=-1)
    gate_values = route_probs * chosen
    tile_expert = (5 * z + jnp.arange(5, dtype=jnp.int32)) // 2
    tile_of = (tile_expert[None, :] == expert_ids[:, None]).astype(F32)
    tile_gates = jnp.sum(gate_values[:, :, None] * tile_of[None], axis=1)
    wide_gates = jnp.repeat(tile_gates, 128, axis=1)
    hidden = dot(mixed_in, w_in)
    gate_h, up_h = hidden[:, :640], hidden[:, 640:]
    sig = jax.nn.sigmoid(gate_h)
    silu = gate_h * sig
    activated = (silu * up_h).astype(BF).astype(F32)
    gated = (activated * wide_gates).astype(BF)
    (placed,) = kernel_call(place_kernel, [((1024, 640), BF)], [SMEM, VMEM])(places, gated)
    mixture = lax.all_to_all(
        dot(placed, down_t, 1, 1).astype(BF).reshape(16, 64, 2048),
        GROUP,
        split_axis=0,
        concat_axis=0,
        tiled=True,
    )
    own_output = (middle + jnp.sum(mixture.astype(F32), axis=0)).astype(BF)
    out_grad = dot(grad_out, down_t)
    tile_parts = jnp.sum((activated * out_grad).reshape(1024, 5, 128), axis=-1)
    gate_part = jnp.sum(tile_parts[:, None, :] * tile_of[None], axis=-1)
    act_grad = out_grad * wide_gates
    gate_h_grad = (act_grad * up_h * sig * (1.0 + gate_h * (1.0 - sig))).astype(BF)
    up_h_grad = (act_grad * silu).astype(BF)
    chosen_grad = gate_part * chosen
    logit_grad = (
        route_probs * (chosen_grad - jnp.sum(chosen_grad * route_probs, axis=-1, keepdims=True))
    ).astype(BF)
    hidden_grad = jnp.concatenate(
        [gate_h_grad, up_h_grad, jnp.pad(logit_grad, ((0, 0), (0, 118)))], axis=1
    )
    in_grads = dot(mixed_in, hidden_grad, 0, 0)
    down_grads = dot(grad_out, gated, 0, 0)
    mixed_grad = cube_scatter(
        project(hidden_grad, jnp.concatenate([w_in, router_all], axis=1))
    )
    expert_grads = core_fold(jnp.concatenate([in_grads, down_grads], axis=1))
    expert_grads = lax.psum_scatter(
        expert_grads.reshape(4, 256, 2048), "x", scatter_dimension=0, tiled=False
    ).reshape(4, 64, 2048)
    expert_grads = lax.all_to_all(
        swap_cores(expert_grads), "z", split_axis=0, concat_axis=0, tiled=True
    )
    scaled = mixed_grad * mlp_row
    middle_grad = (
        own_grad_out
        + second_rate * scaled
        - middle * second_rate**3 * jnp.mean(scaled * middle, axis=-1, keepdims=True)
    )

    branch_grad = cube_gather(middle_grad.astype(BF))
    out_grads = dot(branch_grad, attended, 0, 0)
    attended_grad = dot(branch_grad, out_t).astype(BF)
    wide_head = ((1024, 128), F32)
    q_scaled, k_scaled, v_proj_grad, inner, gain_grads, _, _ = kernel_call(
        backward_kernel,
        [wide_head, wide_head, head, ((1024, 2), F32), ((2, 128), F32), wide_head, wide_head],
        [VMEM] * 12,
        attention_cost(5),
    )(
        qkv, rates, gain_rows, cosine, sine, q_pos, k_pos,
        queries, keys, values, log_total, attended_grad,
    )
    inner = token_sums([inner[:, 0], inner[:, 1]], place_of) * rates**3 / 2048
    q_proj_grad = (rates[:, :1] * q_scaled - qkv[:, :128] * inner[:, :1]).astype(BF)
    k_proj_grad = (rates[:, 1:] * k_scaled - qkv[:, 128:256] * inner[:, 1:]).astype(BF)
    qkv_grad = jnp.concatenate([q_proj_grad, k_proj_grad, v_proj_grad], axis=1)
    qkv_grads = dot(normed, qkv_grad, 0, 0)
    normed_grad = cube_scatter(project(qkv_grad, w_qkv))
    gain_block = gain_grads.reshape(2, 16, 2, 4)
    gain_block = jnp.where(core == 0, gain_block, gain_block[:, :, ::-1])
    gain_block = gain_block.transpose(2, 1, 3, 0)
    gain_block = jnp.pad(gain_block, ((0, 0), (0, 0), (0, 60), (0, 126))).reshape(2048, 128)
    attn_grads = core_fold(jnp.concatenate([qkv_grads, out_grads, gain_block], axis=1))
    attn_grads = lax.all_to_all(
        attn_grads.reshape(16, 64, 640), ("x", "z"), split_axis=0, concat_axis=0, tiled=True
    )
    attn_grads = jnp.sum(attn_grads.reshape(4, 4, 64, 640).astype(F32), axis=0).astype(BF)
    attn_grads = swap_cores(attn_grads)
    scaled = normed_grad * attn_row
    own_rate = lax.rsqrt(jnp.mean(own_rows * own_rows, axis=-1, keepdims=True) + EPSILON)
    own_input_grad = (
        middle_grad
        + own_rate * scaled
        - own_rows * own_rate**3 * jnp.mean(scaled * own_rows, axis=-1, keepdims=True)
    )

    def whole(own):
        far = other_half(own)
        both = jnp.where(yh == 0, jnp.concatenate([own, far]), jnp.concatenate([far, own]))
        there = other_core(both)
        return jnp.where(core == 0, jnp.stack([both, there]), jnp.stack([there, both]))

    def wide(grads):
        return grads.transpose(1, 0, 2).reshape(64, -1).astype(F32)

    def experts(grads):
        return wide(grads).reshape(64, 10, 256).transpose(1, 0, 2)

    q_grads = wide(attn_grads[:, :, :128])
    k_grads = wide(attn_grads[:, :, 128:256])
    v_grads = wide(attn_grads[:, :, 256:384])
    o_grads = wide(attn_grads[:, :, 384:512]).T
    q_gain_grad = attn_grads[:, :4, 512].astype(F32)
    k_gain_grad = attn_grads[:, :4, 513].astype(F32)
    gate_grads = experts(expert_grads[:, :, :640])
    up_grads = experts(expert_grads[:, :, 640:1280])
    router_part = jnp.sum(expert_grads[:, :, 1280:1290].astype(F32), axis=0)
    down_out = wide(expert_grads[:, :, 1408:]).T.reshape(10, 256, 64)

    attn_part = sum(
        jnp.sum(w.astype(F32) * g, axis=1)
        for w, g in ((w_query, q_grads), (w_key, k_grads), (w_value, v_grads))
    )
    mlp_part = sum(
        jnp.sum(w.astype(F32) * g, axis=(0, 2)) for w, g in ((w_gate, gate_grads), (w_up, up_grads))
    ) + jnp.sum(router.astype(F32) * router_part, axis=1)
    summed = jnp.concatenate([router_part, attn_part[:, None], mlp_part[:, None]], axis=1)
    summed = summed + other_core(summed)
    summed = summed + other_half(summed)
    return (
        whole(natural(own_output)),
        whole(natural(own_input_grad.astype(BF))).astype(F32),
        summed[:, 10] / attn_gain.astype(F32),
        q_gain_grad,
        k_gain_grad,
        q_grads,
        k_grads,
        v_grads,
        o_grads,
        summed[:, 11] / mlp_gain.astype(F32),
        summed[:, :10],
        gate_grads,
        up_grads,
        down_out,
    )


def solution(mesh):
    fine = Mesh(mesh.devices.reshape(SIZES), AXES)
    rows = P("x", CONTEXT, None)
    vector = P(WEIGHT)
    gains = P(TENSOR, WEIGHT)
    tall = P(WEIGHT, TENSOR)
    routed = P(WEIGHT, None)
    hidden = P(None, WEIGHT, TENSOR)
    back = P(None, TENSOR, WEIGHT)
    weights = (vector, gains, gains, tall, tall, tall, gains, vector, routed, hidden, hidden, back)
    return jax.shard_map(
        per_device,
        mesh=fine,
        in_specs=(rows, P("x"), rows) + weights + (rows,),
        out_specs=(rows, rows) + weights,
        check_vma=False,
    )
```

```python
import math

import jax
import jax.numpy as jnp
from jax import lax
from jax.experimental import pallas as pl
from jax.experimental.pallas import tpu as pltpu
from jax.sharding import Mesh
from jax.sharding import PartitionSpec as P

EPSILON = 1e-05
ROPE_BASE = 10000.0
SCALE = 128 ** (-0.5)
BF = jnp.bfloat16
F32 = jnp.float32
HIGHEST = lax.Precision.HIGHEST

AXES = ("x", "z", "yl", "yh", "c")
SIZES = (4, 4, 2, 2, 2)
CONTEXT = ("z", "yl")
TENSOR = ("yh", "c")
WEIGHT = ("x", "z", "yl")
GROUP = ("z", "yl", "yh")
Y = ("yl", "yh")
SWAP = ("yl", "c")
VMEM = pl.BlockSpec(memory_space=pltpu.VMEM)
SMEM = pl.BlockSpec(memory_space=pltpu.SMEM)
MIB = 1024 * 1024


def exchange(axes, size, mask):
    pairs = [(at, at ^ mask) for at in range(size)]
    return lambda v: lax.ppermute(v, axes, pairs)


CUBE = (exchange("z", 4, 1), exchange(Y, 4, 2), exchange("z", 4, 3), exchange(Y, 4, 3))
swap_cores = lambda v: lax.ppermute(v, SWAP, [(0, 0), (1, 2), (2, 1), (3, 3)])
other_core = exchange("c", 2, 1)
other_half = exchange("yh", 2, 1)


def dot(a, b, left=1, right=0, precision=None):
    return lax.dot_general(
        a, b, (((left,), (right,)), ((), ())), preferred_element_type=F32, precision=precision
    )


def all_to_all(v, axes):
    return lax.all_to_all(v, axes, split_axis=0, concat_axis=0, tiled=True)


def kernel_call(body, outs, in_specs, limit, flops=0, scratch=()):
    return pl.pallas_call(
        body,
        out_shape=[jax.ShapeDtypeStruct(shape, kind) for shape, kind in outs],
        in_specs=in_specs,
        out_specs=[VMEM] * len(outs),
        scratch_shapes=list(scratch),
        compiler_params=pltpu.CompilerParams(vmem_limit_bytes=limit * MIB),
        cost_estimate=pl.CostEstimate(flops=flops, bytes_accessed=4 * MIB, transcendentals=0),
    )


PIECE = ((128, 2048), BF)
HEAD = ((1024, 128), BF)
WIDE_HEAD = ((1024, 128), F32)


def rows_at(places, at):
    return pl.ds(pl.multiple_of(places[at] * 16, 16), 16)


def join_kernel(*refs):
    half = refs[0].shape[0]
    for i in range(4):
        refs[8 + i][:half, :] = refs[i][...]
        refs[8 + i][half:, :] = refs[4 + i][...]


def cube_gather(parts):
    parts = list(parts)
    for step in range(4):
        arrived = [CUBE[(i + step) % 4](parts[i]) for i in range(4)]
        if step < 3:
            rows = 2 * parts[0].shape[0]
            parts = kernel_call(join_kernel, [((rows, 2048), BF)] * 4, [VMEM] * 8, 8)(
                *parts, *arrived
            )
    return list(parts) + arrived


def fold_kernel(*refs):
    half = refs[0].shape[0] // 2
    for i in range(4):
        kept, arrived, keep, send = refs[i], refs[4 + i], refs[8 + i], refs[12 + i]
        keep[...] = (kept[:half, :].astype(F32) + arrived[:half, :].astype(F32)).astype(BF)
        send[...] = (kept[half:, :].astype(F32) + arrived[half:, :].astype(F32)).astype(BF)


def cube_scatter(pieces):
    kept, sent = pieces[:4], pieces[4:]
    for step in (3, 2, 1, 0):
        arrived = [CUBE[(i + step) % 4](sent[i]) for i in range(4)]
        if step:
            half = ((kept[0].shape[0] // 2, 2048), BF)
            folded = kernel_call(fold_kernel, [half] * 8, [VMEM] * 8, 10)(*kept, *arrived)
            kept, sent = folded[:4], folded[4:]
    return list(kept) + arrived


def block_places():
    at = jnp.arange(64, dtype=jnp.int32)
    part, block = (at >> 3) & 3, (at & 7) | ((at >> 5) << 3)
    turned = [(block >> ((dim - part) & 3)) & 1 for dim in range(4)]
    z = lax.axis_index("z") ^ (turned[0] ^ (3 * turned[2]))
    y = (2 * lax.axis_index("yh") + lax.axis_index("yl")) ^ (turned[1] ^ (3 * turned[3]))
    return ((2 * z + (y & 1)) * 2 + (y >> 1)) * 4 + part


def put_pieces(places, pieces, out):
    for k, piece in enumerate(pieces):
        for j in range(8):
            out[rows_at(places, 8 * k + j), :] = piece[16 * j : 16 * j + 16, :]


def take_rows(places, source, out):
    for n in range(64):
        out[16 * n : 16 * n + 16, :] = source[rows_at(places, n), :]


def project(rows, near, far, columns, pieces):
    for b in range(4):
        held = rows[256 * b : 256 * b + 256, :]
        for at, weight in enumerate((near, far)):
            wide = dot(held, weight[:, columns], 1, 1).astype(BF)
            for k in range(2):
                pieces[2 * b + k][:, 1024 * at : 1024 * at + 1024] = wide[128 * k : 128 * k + 128]


def row_sums(v):
    return dot(jnp.ones((8, 128), F32), v, 1, 1, HIGHEST)[0:1]


def enter_kernel(places, *refs):
    pieces, (gain, near, far, normed, qkv, stats) = refs[:8], refs[8:]
    for k in range(8):

        def norm_rows(j, _):
            held = pieces[k][pl.ds(pl.multiple_of(j * 16, 16), 16), :].astype(F32)
            rate = lax.rsqrt(jnp.mean(held * held, axis=1, keepdims=True) + EPSILON)
            normed[rows_at(places, 8 * k + j), :] = (held * rate * gain[...]).astype(BF)
            return 0

        lax.fori_loop(0, 8, norm_rows, 0)
    for b in range(4):
        rows = slice(256 * b, 256 * b + 256)
        held = dot(normed[rows, :1024], near[:, :384]) + dot(normed[rows, 1024:], far[:, :384])
        qkv[rows, :] = held
        stats[0:1, rows] = row_sums(held[:, :128] * held[:, :128])
        stats[1:2, rows] = row_sums(held[:, 128:256] * held[:, 128:256])


def allowed_block(length, at):
    q_pos = 256 * at + lax.broadcasted_iota(jnp.int32, (256, 256 * at + 256), 0)
    k_pos = lax.broadcasted_iota(jnp.int32, (256, 256 * at + 256), 1)
    return jnp.logical_and(k_pos <= q_pos, k_pos < length[0])


def forward_kernel(
    places, length, qkv, rates, gains, cosine, sine, near, far,
    queries, keys, values, attended, log_total, *rest,
):
    pieces, ordered = rest[:8], rest[8]

    def turn(held):
        return held * cosine[...] + pltpu.roll(held, 64, 1) * sine[...]

    queries[...] = turn(qkv[:, :128] * rates[:, 0:1] * gains[0:1, :]).astype(BF)
    keys[...] = turn(qkv[:, 128:256] * rates[:, 1:2] * gains[1:2, :]).astype(BF)
    values[...] = qkv[:, 256:].astype(BF)
    for at in range(4):
        rows, upto = slice(256 * at, 256 * at + 256), slice(0, 256 * at + 256)
        scores = dot(queries[rows, :], keys[upto, :], 1, 1) * SCALE
        scores = jnp.where(allowed_block(length, at), scores, -1e30)
        peak = jnp.max(scores, axis=1, keepdims=True)
        raised = jnp.exp(scores - peak)
        total = jnp.sum(raised, axis=1, keepdims=True)
        probs = (raised * (1.0 / total)).astype(BF)
        attended[rows, :] = dot(probs, values[upto, :]).astype(BF)
        log_total[rows, :] = peak + jnp.log(total)
    take_rows(places, attended, ordered)
    project(ordered, near, far, slice(512, 640), pieces)


def middle_kernel(*refs):
    terms, (own, gain, middle), outs = refs[:8], refs[8:11], refs[11:]
    for i in range(4):
        rows = slice(16 * i, 16 * i + 16)
        held = own[rows, :].astype(F32) + (terms[i][...].astype(F32) + terms[4 + i][...].astype(F32))
        middle[rows, :] = held
        rate = lax.rsqrt(jnp.mean(held * held, axis=1, keepdims=True) + EPSILON)
        outs[i][...] = (held * rate * gain[...]).astype(BF)


def mixture_kernel(places, length, *refs):
    pieces, (routed, near, far, spread), refs = refs[:8], refs[8:12], refs[12:]
    (mixed, grad_out, gated, hidden_grad), outs, ordered = refs[:4], refs[4:12], refs[12]
    put_pieces(places, pieces, mixed)
    lane = lax.broadcasted_iota(jnp.int32, (256, 128), 1)

    def block(b, _):
        rows = pl.ds(pl.multiple_of(b * 256, 256), 256)
        inside = b * 256 + lax.broadcasted_iota(jnp.int32, (256, 1), 0) < length[0]
        grad_out[rows, :] = jnp.where(inside, routed[rows, :2048], jnp.zeros((), BF))
        chosen = routed[rows, 2048:].astype(F32)
        hidden = dot(mixed[rows, :1024], near[:, :1408]) + dot(mixed[rows, 1024:], far[:, :1408])
        out_grad = dot(grad_out[rows, :1024], near[:, 1408:]) + dot(
            grad_out[rows, 1024:], far[:, 1408:]
        )
        gate_h, up_h = hidden[:, :640], hidden[:, 640:1280]
        logits = jnp.where(lane < 10, hidden[:, 1280:], -1e30)
        raised = jnp.exp(logits - jnp.max(logits, axis=1, keepdims=True))
        route_probs = raised / jnp.sum(raised, axis=1, keepdims=True)
        gates = dot(route_probs * chosen, spread[...], 1, 0, HIGHEST)
        sig = 1.0 / (1.0 + jnp.exp(-gate_h))
        silu = gate_h * sig
        activated = (silu * up_h).astype(BF).astype(F32)
        gated[rows, :] = (activated * gates).astype(BF)
        act_grad = out_grad * gates
        hidden_grad[rows, :640] = (act_grad * up_h * sig * (1.0 + gate_h * (1.0 - sig))).astype(BF)
        hidden_grad[rows, 640:1280] = (act_grad * silu).astype(BF)
        chosen_grad = dot(activated * out_grad, spread[...], 1, 1, HIGHEST) * chosen
        inner = jnp.sum(chosen_grad * route_probs, axis=1, keepdims=True)
        hidden_grad[rows, 1280:] = (route_probs * (chosen_grad - inner)).astype(BF)
        return 0

    lax.fori_loop(0, 4, block, 0)
    take_rows(places, hidden_grad, ordered)
    project(ordered, near, far, slice(0, 1408), outs)


def output_kernel(gated, near, far, out):
    for b in range(4):
        rows = slice(256 * b, 256 * b + 256)
        out[rows, :1024] = dot(gated[rows, :], near[:, 1408:], 1, 1).astype(BF)
        out[rows, 1024:] = dot(gated[rows, :], far[:, 1408:], 1, 1).astype(BF)


def middle_grad_kernel(start, length, *refs):
    terms, (middle, cot, gain, middle_grad), outs = refs[:8], refs[8:12], refs[12:]
    for i in range(4):
        rows = slice(16 * i, 16 * i + 16)
        inside = (
            start[0] + 16 * i + lax.broadcasted_iota(jnp.int32, (16, 1), 0) < length[0]
        )
        grad = jnp.where(inside, cot[rows, :].astype(F32), 0.0)
        scaled = (terms[i][...].astype(F32) + terms[4 + i][...].astype(F32)) * gain[...]
        held = middle[rows, :]
        rate = lax.rsqrt(jnp.mean(held * held, axis=1, keepdims=True) + EPSILON)
        inner = jnp.mean(scaled * held, axis=1, keepdims=True)
        total = grad + rate * scaled - held * (rate * rate * rate * inner)
        middle_grad[rows, :] = total
        outs[i][...] = total.astype(BF)


def backward_kernel(places, length, *refs):
    pieces, refs = refs[:8], refs[8:]
    (near, far, qkv, rates, gains, cosine, sine, queries, keys, values, log_total) = refs[:11]
    (branch, q_scaled, k_scaled, v_grad, inner, gain_grads) = refs[11:17]
    grad, key_grad, value_grad = refs[17:]

    def turn_back(held):
        return held * cosine[...] - pltpu.roll(held, 64, 1) * sine[...]

    put_pieces(places, pieces, branch)
    key_grad[...] = jnp.zeros_like(key_grad)
    value_grad[...] = jnp.zeros_like(value_grad)
    for at in range(4):
        rows, upto = slice(256 * at, 256 * at + 256), slice(0, 256 * at + 256)
        held = dot(branch[rows, :1024], near[:, 512:]) + dot(branch[rows, 1024:], far[:, 512:])
        grad[rows, :] = held.astype(BF)
        scores = dot(queries[rows, :], keys[upto, :], 1, 1) * SCALE
        probs = jnp.where(allowed_block(length, at), jnp.exp(scores - log_total[rows, :]), 0.0)
        prob_grad = dot(grad[rows, :], values[upto, :], 1, 1)
        delta = jnp.sum(probs * prob_grad, axis=1, keepdims=True)
        score_grad = (probs * (prob_grad - delta)).astype(BF)
        q_scaled[rows, :] = dot(score_grad, keys[upto, :]) * SCALE
        key_grad[upto, :] += dot(score_grad, queries[rows, :], 0, 0) * SCALE
        value_grad[upto, :] += dot(probs.astype(BF), grad[rows, :], 0, 0)
    v_grad[...] = value_grad[...].astype(BF)
    q_norm_grad = turn_back(q_scaled[...])
    k_norm_grad = turn_back(key_grad[...])
    q_turned = q_norm_grad * qkv[:, :128]
    k_turned = k_norm_grad * qkv[:, 128:256]
    gain_grads[0:1, :] = jnp.sum(q_turned * rates[:, 0:1], axis=0, keepdims=True)
    gain_grads[1:2, :] = jnp.sum(k_turned * rates[:, 1:2], axis=0, keepdims=True)
    inner[0:1, :] = row_sums(q_turned * gains[0:1, :])
    inner[1:2, :] = row_sums(k_turned * gains[1:2, :])
    q_scaled[...] = q_norm_grad * gains[0:1, :]
    k_scaled[...] = k_norm_grad * gains[1:2, :]


def exit_kernel(places, q_scaled, k_scaled, v_grad, qkv, rates, inner, near, far, grad, *rest):
    pieces, ordered = rest[:8], rest[8]
    for at, scaled in enumerate((q_scaled, k_scaled)):
        columns = slice(128 * at, 128 * at + 128)
        rate = rates[:, at : at + 1]
        factor = rate * rate * rate * inner[:, at : at + 1] * (1.0 / 2048)
        grad[:, columns] = (rate * scaled[...] - qkv[:, columns] * factor).astype(BF)
    grad[:, 256:] = v_grad[...]
    take_rows(places, grad, ordered)
    project(ordered, near, far, slice(0, 384), pieces)


def input_grad_kernel(*refs):
    terms, (middle_grad, own, gain, out) = refs[:8], refs[8:]
    for i in range(4):
        rows = slice(16 * i, 16 * i + 16)
        scaled = (terms[i][...].astype(F32) + terms[4 + i][...].astype(F32)) * gain[...]
        held = own[rows, :].astype(F32)
        rate = lax.rsqrt(jnp.mean(held * held, axis=1, keepdims=True) + EPSILON)
        inner = jnp.mean(scaled * held, axis=1, keepdims=True)
        total = middle_grad[rows, :] + rate * scaled - held * (rate * rate * rate * inner)
        out[rows, :] = total.astype(BF)


def token_sums(stats):
    held = stats.reshape(1, 16, 128)
    arrived = all_to_all(jnp.broadcast_to(held, (16, 16, 128)), GROUP)
    return jnp.sum(arrived, axis=0).reshape(2, 1024).T


def angles(head_size):
    steps_half = jnp.arange(head_size // 2).astype(F32)
    frequency = jnp.exp(steps_half * (-2.0 * math.log(ROPE_BASE) / head_size))
    turned = jnp.arange(1024, dtype=jnp.int32).astype(F32)[:, None] * frequency[None, :]
    cosine, sine = jnp.cos(turned), jnp.sin(turned)
    return (
        jnp.concatenate([cosine, cosine], axis=-1),
        jnp.concatenate([-sine, sine], axis=-1),
    )


def after(value, earlier):
    return lax.optimization_barrier((value, earlier))[0]


def per_device(
    tokens,
    lengths,
    routes,
    attn_gain,
    q_gain,
    k_gain,
    w_query,
    w_key,
    w_value,
    w_out,
    mlp_gain,
    router,
    w_gate,
    w_up,
    w_down,
    cotangent,
):
    z = lax.axis_index("z")
    yh = lax.axis_index("yh")
    core = lax.axis_index("c")

    def own_first(v):
        halves = v.reshape(64, 16, 2, 64)
        halves = jnp.where(core == 0, halves, halves[:, :, ::-1])
        return halves.transpose(0, 2, 1, 3).reshape(64, 2048)

    def natural(v):
        halves = v.reshape(64, 2, 16, 64).transpose(0, 2, 1, 3)
        return jnp.where(core == 0, halves, halves[:, :, ::-1]).reshape(64, 2048)

    own_start = (core, yh * 64, 0)
    own_tokens = own_first(lax.dynamic_slice(tokens, own_start, (1, 64, 2048))[0])
    token_pieces = cube_gather([own_tokens[16 * i : 16 * i + 16] for i in range(4)])
    places = block_places()
    slot_length = lax.dynamic_slice(lengths, (core,), (1,))

    def four(w):
        return w.reshape(64, 4, -1).transpose(1, 0, 2)

    def pack_experts(w):
        return four(w.transpose(1, 0, 2).reshape(64, 2560))

    def per_row(v):
        return jnp.broadcast_to(v[None], (4,) + v.shape)

    gains = jnp.stack([q_gain, k_gain], axis=-1)
    extra = jnp.concatenate(
        [
            per_row(jnp.stack([attn_gain, mlp_gain], axis=1)),
            jnp.pad(gains, ((0, 0), (0, 60), (0, 0))),
            jnp.zeros((4, 64, 124), BF),
        ],
        axis=-1,
    )
    first_pack = jnp.concatenate(
        [four(w_query), four(w_key), four(w_value), extra, four(w_out.T)], axis=-1
    )
    first = all_to_all(
        jnp.broadcast_to(swap_cores(first_pack)[None], (4, 4, 64, 640)).reshape(16, 64, 640),
        ("x", "z"),
    ).reshape(1024, 640)
    first_far = other_core(first)
    second_pack = jnp.concatenate(
        [
            pack_experts(w_gate),
            pack_experts(w_up),
            per_row(jnp.pad(router, ((0, 0), (0, 118)))),
            four(w_down.reshape(2560, 64).T),
        ],
        axis=-1,
    )
    second = all_to_all(swap_cores(after(second_pack, first)), "z")
    second = lax.all_gather(second, "x", axis=0, tiled=False).reshape(1024, 2048)
    second_far = other_core(second)
    extra_all = jnp.concatenate([first[:, 384:388], first_far[:, 384:388]], axis=0)
    gain_lines = extra_all[:, :2].astype(F32).T
    attn_row, mlp_row = gain_lines[0:1], gain_lines[1:2]
    gain_blocks = extra_all[:, 2:4].reshape(2, 16, 64, 2)[:, :, :4]
    gain_blocks = jnp.where(core == 0, gain_blocks, gain_blocks[::-1])
    gain_rows = gain_blocks.transpose(3, 1, 0, 2).reshape(2, 128).astype(F32)

    own_cot = own_first(lax.dynamic_slice(cotangent, own_start, (1, 64, 2048))[0])
    own_routes = lax.dynamic_slice(routes, own_start, (1, 64, 8))[0]
    expert_ids = jnp.arange(128, dtype=jnp.int32)
    own_chosen = jnp.sum((own_routes[:, :, None] == expert_ids).astype(BF), axis=1)
    routed = after(jnp.concatenate([own_cot, own_chosen], axis=1), first)
    routed = all_to_all(jnp.broadcast_to(routed[None], (16, 64, 2176)), GROUP).reshape(1024, 2176)

    normed, qkv, stats = kernel_call(
        enter_kernel,
        [((1024, 2048), BF), ((1024, 384), F32), ((2, 1024), F32)],
        [SMEM] + [VMEM] * 11,
        24,
        2 * 1024 * 2048 * 384,
    )(places, *token_pieces, attn_row, first, first_far)
    rates = lax.rsqrt(token_sums(stats) / 2048 + EPSILON)
    cosine, sine = angles(128)
    queries, keys, values, attended, log_total, *pieces = kernel_call(
        forward_kernel,
        [HEAD, HEAD, HEAD, HEAD, ((1024, 1), F32)] + [PIECE] * 8,
        [SMEM, SMEM] + [VMEM] * 7,
        28,
        4 * 1024 * 1024 * 128,
        [pltpu.VMEM((1024, 128), BF)],
    )(places, slot_length, qkv, rates, gain_rows, cosine, sine, first, first_far)
    own_row = ((64, 2048), F32)
    own_part = ((16, 2048), BF)
    middle, *parts = kernel_call(middle_kernel, [own_row] + [own_part] * 4, [VMEM] * 10, 8)(
        *cube_scatter(pieces), own_tokens, mlp_row
    )

    tile_expert = (5 * z + jnp.arange(640, dtype=jnp.int32) // 128) // 2
    tile_of = (tile_expert[None, :] == expert_ids[:, None]).astype(F32)
    mixed, grad_out, gated, hidden_grad, *pieces = kernel_call(
        mixture_kernel,
        [((1024, 2048), BF), ((1024, 2048), BF), ((1024, 640), BF), ((1024, 1408), BF)]
        + [PIECE] * 8,
        [SMEM, SMEM] + [VMEM] * 12,
        56,
        2 * 1024 * 2048 * 3456,
        [pltpu.VMEM((1024, 1408), BF)],
    )(places, slot_length, *cube_gather(parts), routed, second, second_far, tile_of)
    own_place = ((2 * z + lax.axis_index("yl")) * 128 + yh * 64)[None]
    middle_grad, *parts = kernel_call(
        middle_grad_kernel, [own_row] + [own_part] * 4, [SMEM, SMEM] + [VMEM] * 11, 8
    )(own_place, slot_length, *cube_scatter(pieces), middle, own_cot, mlp_row)

    def fold_cores(left, right):
        near = dot(left[:, :1024], right, 0, 0)
        far = other_core(dot(left[:, 1024:], right, 0, 0).astype(BF))
        return (near + far.astype(F32)).astype(BF)

    def fold_shards(grads):
        return lax.psum_scatter(
            grads.reshape(4, 256, -1), "x", scatter_dimension=0, tiled=False
        ).reshape(4, 64, -1)

    expert_grads = jnp.concatenate(
        [fold_shards(fold_cores(mixed, hidden_grad)), fold_shards(fold_cores(grad_out, gated))],
        axis=-1,
    )
    expert_grads = all_to_all(swap_cores(expert_grads), "z")

    branch, q_scaled, k_scaled, v_grad, inner, gain_grads = kernel_call(
        backward_kernel,
        [((1024, 2048), BF), WIDE_HEAD, WIDE_HEAD, HEAD, ((2, 1024), F32), ((2, 128), F32)],
        [SMEM, SMEM] + [VMEM] * 19,
        40,
        10 * 1024 * 1024 * 128,
        [pltpu.VMEM((1024, 128), BF), pltpu.VMEM((1024, 128), F32), pltpu.VMEM((1024, 128), F32)],
    )(
        places, slot_length, *cube_gather(parts), first, first_far,
        qkv, rates, gain_rows, cosine, sine, queries, keys, values, log_total,
    )
    (products,) = kernel_call(
        output_kernel, [((1024, 2048), BF)], [VMEM] * 3, 20, 2 * 1024 * 2048 * 640
    )(gated, second, second_far)
    products = after(products, inner)
    mixture = all_to_all(products.reshape(16, 64, 2048), GROUP)
    own_output = (middle + jnp.sum(mixture.astype(F32), axis=0)).astype(BF)
    qkv_grad, *pieces = kernel_call(
        exit_kernel,
        [((1024, 384), BF)] + [PIECE] * 8,
        [SMEM] + [VMEM] * 8,
        20,
        2 * 1024 * 2048 * 384,
        [pltpu.VMEM((1024, 384), BF)],
    )(places, q_scaled, k_scaled, v_grad, qkv, rates, token_sums(inner), first, first_far)
    (own_input_grad,) = kernel_call(input_grad_kernel, [((64, 2048), BF)], [VMEM] * 11, 8)(
        *cube_scatter(pieces), middle_grad, own_tokens, attn_row
    )
    gain_block = gain_grads.reshape(2, 16, 2, 4)
    gain_block = jnp.where(core == 0, gain_block, gain_block[:, :, ::-1])
    gain_block = gain_block.transpose(2, 1, 3, 0)
    gain_block = jnp.pad(gain_block, ((0, 0), (0, 0), (0, 60), (0, 126))).reshape(2048, 128)
    gain_block = gain_block[:1024] + other_core(gain_block[1024:])
    attn_grads = jnp.concatenate(
        [fold_cores(normed, qkv_grad), fold_cores(branch, attended), gain_block.astype(BF)], axis=1
    )
    attn_grads = all_to_all(attn_grads.reshape(16, 64, 640), ("x", "z"))
    attn_grads = jnp.sum(attn_grads.reshape(4, 4, 64, 640).astype(F32), axis=0).astype(BF)
    attn_grads = swap_cores(attn_grads)

    def whole(own):
        far = other_half(own)
        both = jnp.where(yh == 0, jnp.concatenate([own, far]), jnp.concatenate([far, own]))
        there = other_core(both)
        return jnp.where(core == 0, jnp.stack([both, there]), jnp.stack([there, both]))

    def wide(grads):
        return grads.transpose(1, 0, 2).reshape(64, -1).astype(F32)

    def experts(grads):
        return wide(grads).reshape(64, 10, 256).transpose(1, 0, 2)

    q_grads = wide(attn_grads[:, :, :128])
    k_grads = wide(attn_grads[:, :, 128:256])
    v_grads = wide(attn_grads[:, :, 256:384])
    o_grads = wide(attn_grads[:, :, 384:512]).T
    q_gain_grad = attn_grads[:, :4, 512].astype(F32)
    k_gain_grad = attn_grads[:, :4, 513].astype(F32)
    gate_grads = experts(expert_grads[:, :, :640])
    up_grads = experts(expert_grads[:, :, 640:1280])
    router_part = jnp.sum(expert_grads[:, :, 1280:1290].astype(F32), axis=0)
    down_out = wide(expert_grads[:, :, 1408:]).T.reshape(10, 256, 64)

    attn_part = sum(
        jnp.sum(w.astype(F32) * g, axis=1)
        for w, g in ((w_query, q_grads), (w_key, k_grads), (w_value, v_grads))
    )
    mlp_part = sum(
        jnp.sum(w.astype(F32) * g, axis=(0, 2)) for w, g in ((w_gate, gate_grads), (w_up, up_grads))
    ) + jnp.sum(router.astype(F32) * router_part, axis=1)
    summed = jnp.concatenate([router_part, attn_part[:, None], mlp_part[:, None]], axis=1)
    summed = summed + other_core(summed)
    summed = summed + other_half(summed)
    return (
        whole(natural(own_output)),
        whole(natural(own_input_grad)).astype(F32),
        summed[:, 10] / attn_gain.astype(F32),
        q_gain_grad,
        k_gain_grad,
        q_grads,
        k_grads,
        v_grads,
        o_grads,
        summed[:, 11] / mlp_gain.astype(F32),
        summed[:, :10],
        gate_grads,
        up_grads,
        down_out,
    )


def solution(mesh):
    fine = Mesh(mesh.devices.reshape(SIZES), AXES)
    rows = P("x", CONTEXT, None)
    vector = P(WEIGHT)
    gains = P(TENSOR, WEIGHT)
    tall = P(WEIGHT, TENSOR)
    routed = P(WEIGHT, None)
    hidden = P(None, WEIGHT, TENSOR)
    back = P(None, TENSOR, WEIGHT)
    weights = (vector, gains, gains, tall, tall, tall, gains, vector, routed, hidden, hidden, back)
    return jax.shard_map(
        per_device,
        mesh=fine,
        in_specs=(rows, P("x"), rows) + weights + (rows,),
        out_specs=(rows, rows) + weights,
        check_vma=False,
    )
```

```python
import math

import jax
import jax.numpy as jnp
import numpy as np
from jax import lax
from jax.experimental import pallas as pl
from jax.experimental.pallas import tpu as pltpu
from jax.sharding import Mesh
from jax.sharding import PartitionSpec as P

EPSILON = 1e-05
ROPE_BASE = 10000.0
SCALE = 128 ** (-0.5)
BF = jnp.bfloat16
F32 = jnp.float32
HIGHEST = lax.Precision.HIGHEST

AXES = ("x", "z", "yl", "yh", "c")
SIZES = (4, 4, 2, 2, 2)
CONTEXT = ("z", "yl")
TENSOR = ("yh", "c")
WEIGHT = ("x", "z", "yl")
GROUP = ("z", "yl", "yh")
Y = ("yl", "yh")
SWAP = ("yl", "c")
VMEM = pl.BlockSpec(memory_space=pltpu.VMEM)
SMEM = pl.BlockSpec(memory_space=pltpu.SMEM)
ANY = pl.BlockSpec(memory_space=pl.ANY)
MIB = 1024 * 1024


def exchange(axes, size, mask):
    pairs = [(at, at ^ mask) for at in range(size)]
    return lambda v: lax.ppermute(v, axes, pairs)


CUBE = (exchange("z", 4, 1), exchange(Y, 4, 2), exchange("z", 4, 3), exchange(Y, 4, 3))
ALONG_Z = (exchange("z", 4, 1), exchange("z", 4, 3), exchange("z", 4, 2))
ALONG_Y = (exchange(Y, 4, 2), exchange(Y, 4, 3), exchange(Y, 4, 1))
X_PAIR, X_ACROSS = exchange("x", 4, 1), exchange("x", 4, 3)
swap_cores = lambda v: lax.ppermute(v, SWAP, [(0, 0), (1, 2), (2, 1), (3, 3)])
other_core = exchange("c", 2, 1)
other_half = exchange("yh", 2, 1)


def dot(a, b, left=1, right=0, precision=None):
    return lax.dot_general(
        a, b, (((left,), (right,)), ((), ())), preferred_element_type=F32, precision=precision
    )


def all_to_all(v, axes):
    return lax.all_to_all(v, axes, split_axis=0, concat_axis=0, tiled=True)


def kernel_call(body, outs, in_specs, limit, flops=0, scratch=(), earlier=()):
    def whole_body(*refs):
        body(*refs[len(earlier) :])

    call = pl.pallas_call(
        whole_body,
        out_shape=[jax.ShapeDtypeStruct(shape, kind) for shape, kind in outs],
        in_specs=[ANY] * len(earlier) + in_specs,
        out_specs=[VMEM] * len(outs),
        scratch_shapes=list(scratch),
        compiler_params=pltpu.CompilerParams(vmem_limit_bytes=limit * MIB),
        cost_estimate=pl.CostEstimate(flops=flops, bytes_accessed=4 * MIB, transcendentals=0),
    )
    return lambda *args: call(*earlier, *args)


PIECE = ((128, 2048), BF)
HEAD = ((1024, 128), BF)
WIDE_HEAD = ((1024, 128), F32)


def rows_at(places, at):
    return pl.ds(pl.multiple_of(places[at] * 16, 16), 16)


def join_kernel(*refs):
    half, cuts = refs[0].shape[0], len(refs[8:]) // 4
    for i in range(4):
        at = 0
        for out in refs[8 + cuts * i : 8 + cuts * i + cuts]:
            columns = slice(at, at + out.shape[1])
            out[:half, :] = refs[i][:, columns]
            out[half:, :] = refs[4 + i][:, columns]
            at += out.shape[1]


def join(parts, arrived, widths, earlier=()):
    rows = 2 * parts[0].shape[0]
    outs = [((rows, width), BF) for width in widths] * 4
    return kernel_call(join_kernel, outs, [VMEM] * 8, 16, earlier=earlier)(*parts, *arrived)


def cube_step(parts, step):
    return [CUBE[(i + step) % 4](parts[i]) for i in range(4)]


def cube_gather(parts, seen=None):
    parts = list(parts)
    for step in range(3):
        arrived = cube_step(parts, step)
        parts = join(parts, arrived, [parts[0].shape[1]])
        if seen is not None:
            seen.append(arrived)
    return list(parts) + cube_step(parts, 3)


def pick_kernel(ids, blocks, *outs):
    for mask, out in zip((0, 1, 3, 2), outs):
        out[...] = blocks[pl.ds(ids[3] ^ mask, 1)]


def place_kernel(ids, own, a, b, c, out):
    for mask, held in zip((0, 1, 3, 2), (own, a, b, c)):
        out[pl.ds(ids[3] ^ mask, 1)] = held[...]


def pair_kernel(bit, ids, own, far, out):
    rows = own.shape[0]
    here = pl.multiple_of(ids[bit] * rows, rows)
    out[pl.ds(here, rows), :] = own[...]
    out[pl.ds(rows - here, rows), :] = far[...]


def pair(bit, ids, own, far):
    rows, width = own.shape
    return kernel_call(
        lambda *refs: pair_kernel(bit, *refs),
        [((2 * rows, width), BF)],
        [SMEM] + [VMEM] * 2,
        max(4, rows * width * 8 // MIB + 2),
    )(ids, own, far)[0]


def split_kernel(bit, ids, a, b, keep, send):
    rows = keep.shape[0]
    here = pl.multiple_of(ids[bit] * rows, rows)
    for out, at in ((keep, here), (send, rows - here)):
        for n in range(0, rows, 64):
            held = pl.ds(pl.multiple_of(at + n, 64), 64)
            out[n : n + 64, :] = (a[held, :].astype(F32) + b[held, :].astype(F32)).astype(BF)


def split(bit, ids, a, b):
    rows, width = a.shape
    return kernel_call(
        lambda *refs: split_kernel(bit, *refs),
        [((rows // 2, width), BF)] * 2,
        [SMEM] + [VMEM] * 2,
        max(4, rows * width * 8 // MIB + 2),
    )(ids, a, b)


def line_exchange(blocks, ids):
    sent = kernel_call(pick_kernel, [((1,) + blocks.shape[1:], BF)] * 4, [SMEM, VMEM], 8)(
        ids, blocks
    )
    arrived = [move(held) for move, held in zip(ALONG_Z, sent[1:])]
    return kernel_call(
        place_kernel, [(blocks.shape, BF)], [SMEM] + [VMEM] * 4, 8
    )(ids, sent[0], *arrived)[0]


def token_terms(stats):
    held = stats + ALONG_Z[0](stats) + ALONG_Z[1](stats) + ALONG_Z[2](stats)
    return [held] + [move(held) for move in ALONG_Y]


def fold_kernel(*refs):
    half = refs[0].shape[0] // 2
    for i in range(4):
        kept, arrived, keep, send = refs[i], refs[4 + i], refs[8 + i], refs[12 + i]
        keep[...] = (kept[:half, :].astype(F32) + arrived[:half, :].astype(F32)).astype(BF)
        send[...] = (kept[half:, :].astype(F32) + arrived[half:, :].astype(F32)).astype(BF)


def cube_scatter(pieces, seen=None):
    kept, sent = pieces[:4], pieces[4:]
    for step in (3, 2, 1, 0):
        arrived = cube_step(sent, step)
        if seen is not None:
            seen.append(arrived)
        if step:
            half = ((kept[0].shape[0] // 2, kept[0].shape[1]), BF)
            folded = kernel_call(fold_kernel, [half] * 8, [VMEM] * 8, 16)(*kept, *arrived)
            kept, sent = folded[:4], folded[4:]
    return list(kept) + arrived


def block_places():
    at = jnp.arange(64, dtype=jnp.int32)
    part, block = (at >> 3) & 3, (at & 7) | ((at >> 5) << 3)
    turned = [(block >> ((dim - part) & 3)) & 1 for dim in range(4)]
    z = lax.axis_index("z") ^ (turned[0] ^ (3 * turned[2]))
    y = (2 * lax.axis_index("yh") + lax.axis_index("yl")) ^ (turned[1] ^ (3 * turned[3]))
    return ((2 * z + (y & 1)) * 2 + (y >> 1)) * 4 + part


def put_pieces(places, pieces, out):
    for k, piece in enumerate(pieces):
        for j in range(8):
            out[rows_at(places, 8 * k + j), :] = piece[16 * j : 16 * j + 16, :]


def take_rows(places, source, out, start=0):
    for n in range(out.shape[0] // 16):
        out[16 * n : 16 * n + 16, :] = source[rows_at(places, start + n), :]


def project(rows, near, far, columns, pieces, start=0):
    for b in range(len(pieces) // 2):
        held = rows[256 * b : 256 * b + 256, :]
        for at, weight in enumerate((near, far)):
            wide = dot(held, weight[:, columns], 1, 1).astype(BF)
            place = slice(start + 1024 * at, start + 1024 * at + 1024)
            for k in range(2):
                pieces[2 * b + k][:, place] = wide[128 * k : 128 * k + 128]


def natural_order(near, core, out):
    first = lax.broadcasted_iota(jnp.int32, (near.shape[0], 128), 1) < 64
    for j in range(8):
        mine = near[:, 128 * j : 128 * j + 128]
        other = near[:, 1024 + 128 * j : 1024 + 128 * j + 128]
        low = jnp.where(core == 0, mine, other)
        high = jnp.where(core == 0, other, mine)
        out[:, 256 * j : 256 * j + 128] = jnp.where(first, low, pltpu.roll(high, 64, 1)).astype(BF)
        out[:, 256 * j + 128 : 256 * j + 256] = jnp.where(
            first, pltpu.roll(low, 64, 1), high
        ).astype(BF)


def prepare_kernel(ids, places, length, tokens, cot, routes, own_tokens, own_cot, p0, p1, p2, p3, wide):
    core, parts = ids[0], (p0, p1, p2, p3)
    first = lax.broadcasted_iota(jnp.int32, (64, 128), 1) < 64
    for source, out, at in ((tokens, own_tokens, 0), (cot, own_cot, 2048)):
        for j in range(8):
            a = source[0, :, 256 * j : 256 * j + 128].astype(F32)
            b = source[0, :, 256 * j + 128 : 256 * j + 256].astype(F32)
            low = jnp.where(first, a, pltpu.roll(b, 64, 1))
            high = jnp.where(first, pltpu.roll(a, 64, 1), b)
            out[:, 128 * j : 128 * j + 128] = jnp.where(core == 0, low, high).astype(BF)
            out[:, 1024 + 128 * j : 1152 + 128 * j] = jnp.where(core == 0, high, low).astype(BF)
        for i in range(4):
            parts[i][:, at : at + 2048] = out[16 * i : 16 * i + 16, :]
    expert = lax.broadcasted_iota(jnp.int32, (128, 128), 0)
    chosen = jnp.zeros((128, 128), F32)
    for k in range(8):
        chosen += (expert == routes[0, k : k + 1, :]).astype(F32)
    wide[...] = dot(chosen.astype(BF), identity(128, BF), 0, 0)
    for i in range(4):
        rows = pl.ds(pl.multiple_of(ids[1] * 64 + 16 * i, 16), 16)
        parts[i][:, 4096:] = wide[rows, :].astype(BF)


def prepare(ids, places, length, tokens, cot, routes):
    own = lambda n, ids: (ids[0], ids[1], 0)
    whole = lambda n, ids: (0, 0)
    return pl.pallas_call(
        prepare_kernel,
        grid_spec=pltpu.PrefetchScalarGridSpec(
            num_scalar_prefetch=1,
            grid=(1,),
            in_specs=[
                SMEM,
                SMEM,
                pl.BlockSpec((1, 64, 2048), own),
                pl.BlockSpec((1, 64, 2048), own),
                pl.BlockSpec((1, 8, 128), lambda n, ids: (ids[0], 0, 0)),
            ],
            out_specs=[pl.BlockSpec((64, 2048), whole)] * 2 + [pl.BlockSpec((16, 4224), whole)] * 4,
            scratch_shapes=[pltpu.VMEM((128, 128), F32)],
        ),
        out_shape=[jax.ShapeDtypeStruct((64, 2048), BF)] * 2
        + [jax.ShapeDtypeStruct((16, 4224), BF)] * 4,
        compiler_params=pltpu.CompilerParams(vmem_limit_bytes=8 * MIB),
    )(ids, places, length, tokens, cot, routes)


def identity(size, kind):
    row = lax.broadcasted_iota(jnp.int32, (size, size), 0)
    return (row == lax.broadcasted_iota(jnp.int32, (size, size), 1)).astype(kind)


def first_pack_kernel(query, key, value, w_out, attn_gain, mlp_gain, q_gain, k_gain, out):
    row = lax.broadcasted_iota(jnp.int32, (64, 128), 0)
    lane = lax.broadcasted_iota(jnp.int32, (64, 128), 1)
    extra = jnp.zeros((64, 128), F32)
    for at, gain in enumerate((attn_gain, mlp_gain)):
        column = jnp.sum(gain[...].astype(F32) * identity(64, F32), axis=1, keepdims=True)
        extra = jnp.where(lane == at, column, extra)
    for k in range(4):
        columns = slice(128 * k, 128 * k + 128)
        for at, w in ((0, query), (128, key), (256, value), (512, w_out)):
            out[k, :, at : at + 128] = w[:, columns]
        held = extra
        for at, gain in enumerate((q_gain, k_gain)):
            for j in range(4):
                here = jnp.logical_and(row == j, lane == 2 + at)
                held = jnp.where(here, gain[k : k + 1, j : j + 1].astype(F32), held)
        out[k, :, 384:512] = held.astype(BF)


def second_pack_kernel(gate, up, down, router, out):
    lane = lax.broadcasted_iota(jnp.int32, (64, 128), 1)
    routed = jnp.zeros((64, 128), F32)
    for e in range(10):
        column = jnp.sum(
            router[e : e + 1, :].astype(F32) * identity(64, F32), axis=1, keepdims=True
        )
        routed = jnp.where(lane == e, column, routed)
    for k in range(4):
        for m in range(5):
            tile = 5 * k + m
            columns = slice(128 * (tile % 2), 128 * (tile % 2) + 128)
            for w, at in ((gate, 0), (up, 640), (down, 1408)):
                out[k, :, at + 128 * m : at + 128 * m + 128] = w[tile // 2, :, columns]
        out[k, :, 1280:1408] = routed.astype(BF)


def second_unpack_kernel(grads, gate, up, router, gate_out, up_out, down_out, small):
    part = jnp.zeros((64, 1), F32)
    routed = jnp.zeros((64, 128), F32)
    for k in range(4):
        for m in range(5):
            tile = 5 * k + m
            expert, columns = tile // 2, slice(128 * (tile % 2), 128 * (tile % 2) + 128)
            for w, out, at in ((gate, gate_out, 0), (up, up_out, 640), (None, down_out, 1408)):
                held = grads[k, :, at + 128 * m : at + 128 * m + 128].astype(F32)
                out[expert, :, columns] = held
                if w is not None:
                    held = held * w[expert, :, columns].astype(F32)
                    part += jnp.sum(held, axis=1, keepdims=True)
        routed += grads[k, :, 1280:1408].astype(F32)
    weights = dot(identity(64, BF), router[...], 1, 1)
    part += jnp.sum(routed[:, :10] * weights, axis=1, keepdims=True)
    lane = lax.broadcasted_iota(jnp.int32, (64, 128), 1)
    small[...] = jnp.where(lane < 10, routed, 0.0) + jnp.where(lane == 10, part, 0.0)


def first_unpack_kernel(grads, query, key, value, query_out, key_out, value_out, out_out, small):
    part = jnp.zeros((64, 1), F32)
    for k in range(4):
        columns = slice(128 * k, 128 * k + 128)
        for at, (w, out) in enumerate(((query, query_out), (key, key_out), (value, value_out))):
            held = grads[k, :, 128 * at : 128 * at + 128].astype(F32)
            out[:, columns] = held
            part += jnp.sum(held * w[:, columns].astype(F32), axis=1, keepdims=True)
        out_out[:, columns] = grads[k, :, 384:512].astype(F32)
    small[...] = jnp.broadcast_to(part, (64, 128))


def as_column(rows):
    eye = identity(128, F32)
    return [
        jnp.sum(rows[n : n + 1, :] * eye, axis=1, keepdims=True) for n in range(rows.shape[0])
    ]


def row_sums(v):
    return dot(jnp.ones((8, 128), F32), v, 1, 1, HIGHEST)[0:1]


def put_sums(stats, at, b, row):
    for half in range(2):
        place = 8 * at + 2 * b + half
        stats[place : place + 1, :] = row[:, 128 * half : 128 * half + 128]


def gain_places(core, at):
    row = lax.broadcasted_iota(jnp.int32, (1024, 128), 0)
    element = lax.broadcasted_iota(jnp.int32, (1024, 128), 1)
    yl = core if at == 0 else 1 - core
    here = ((row >> 6) * 2 + yl) * 4 + (row & 63) == element
    return jnp.where(jnp.logical_and(here, (row & 63) < 4), 1.0, 0.0).astype(BF)


def enter_kernel(places, *refs):
    pieces, (ids, near, far, normed, qkv, stats, lines, gains) = refs[:8], refs[8:]
    eye = identity(128, F32)
    for at, weight in enumerate((near, far)):
        for b in range(8):
            held = weight[128 * b : 128 * b + 128, 384:512].astype(F32)
            for n in range(2):
                line = jnp.sum(held[:, n : n + 1] * eye, axis=0, keepdims=True)
                lines[n : n + 1, 1024 * at + 128 * b : 1024 * at + 128 * b + 128] = line
    total = jnp.zeros((128, 128), F32)
    for at, weight in enumerate((near, far)):
        total += dot(weight[:, 384:512], gain_places(ids[0], at), 0, 0)
    gains[...] = total[2:4, :]
    gain = lines.at[0:1, :]
    for k in range(8):

        def norm_rows(j, _):
            held = pieces[k][pl.ds(pl.multiple_of(j * 16, 16), 16), :].astype(F32)
            rate = lax.rsqrt(jnp.mean(held * held, axis=1, keepdims=True) + EPSILON)
            normed[rows_at(places, 8 * k + j), :] = (held * rate * gain[...]).astype(BF)
            return 0

        lax.fori_loop(0, 8, norm_rows, 0)
    for b in range(4):
        rows = slice(256 * b, 256 * b + 256)
        held = dot(normed[rows, :1024], near[:, :384]) + dot(normed[rows, 1024:], far[:, :384])
        qkv[rows, :] = held
        for at in range(2):
            columns = slice(128 * at, 128 * at + 128)
            put_sums(stats, at, b, row_sums(held[:, columns] * held[:, columns]))


def allowed_block(length, at):
    q_pos = 256 * at + lax.broadcasted_iota(jnp.int32, (256, 256 * at + 256), 0)
    k_pos = lax.broadcasted_iota(jnp.int32, (256, 256 * at + 256), 1)
    return jnp.logical_and(k_pos <= q_pos, k_pos < length[0])


def forward_kernel(
    places, length, qkv, s0, s1, s2, s3, gains, cosine, sine, near, far,
    rates, queries, keys, values, attended, log_total, *rest,
):
    pieces, ordered = rest[:8], rest[8]
    for n, column in enumerate(as_column((s0[...] + s1[...]) + (s2[...] + s3[...]))):
        rate = lax.rsqrt(column * (1.0 / 2048) + EPSILON)
        rates[128 * (n % 8) : 128 * (n % 8) + 128, n // 8 : n // 8 + 1] = rate

    def turn(held):
        return held * cosine[...] + pltpu.roll(held, 64, 1) * sine[...]

    queries[...] = turn(qkv[:, :128] * rates[:, 0:1] * gains[0:1, :]).astype(BF)
    keys[...] = turn(qkv[:, 128:256] * rates[:, 1:2] * gains[1:2, :]).astype(BF)
    values[...] = qkv[:, 256:].astype(BF)
    for at in range(4):
        rows, upto = slice(256 * at, 256 * at + 256), slice(0, 256 * at + 256)
        scores = dot(queries[rows, :], keys[upto, :], 1, 1) * SCALE
        scores = jnp.where(allowed_block(length, at), scores, -1e30)
        peak = jnp.max(scores, axis=1, keepdims=True)
        raised = jnp.exp(scores - peak)
        total = jnp.sum(raised, axis=1, keepdims=True)
        probs = (raised * (1.0 / total)).astype(BF)
        attended[rows, :] = dot(probs, values[upto, :]).astype(BF)
        log_total[rows, :] = peak + jnp.log(total)
    take_rows(places, attended, ordered)
    project(ordered, near, far, slice(512, 640), pieces)


def middle_kernel(*refs):
    terms, (own, gain, middle), outs = refs[:8], refs[8:11], refs[11:]
    for i in range(4):
        rows = slice(16 * i, 16 * i + 16)
        held = own[rows, :].astype(F32) + (terms[i][...].astype(F32) + terms[4 + i][...].astype(F32))
        middle[rows, :] = held
        rate = lax.rsqrt(jnp.mean(held * held, axis=1, keepdims=True) + EPSILON)
        outs[i][...] = (held * rate * gain[...]).astype(BF)


def mixture_kernel(places, length, ids, *refs):
    arrays, scratch = refs[:30], refs[30:]
    sources, outs = arrays[:18], arrays[18:]
    held, (mixed, grad_out, gated, hidden_grad), made = scratch[:18], scratch[18:22], scratch[22:30]
    chosen_rows, ordered, gated_ordered, spread, in_sems, out_sems = scratch[30:]
    loads = [
        pltpu.make_async_copy(source, target, in_sems.at[n])
        for n, (source, target) in enumerate(zip(sources, held))
    ]
    stores = [
        pltpu.make_async_copy(source, target, out_sems.at[n])
        for n, (source, target) in enumerate(
            zip((mixed, grad_out, gated, hidden_grad) + tuple(made), outs)
        )
    ]
    for load in loads:
        load.start()
    pieces, routed, (near, far) = held[:8], held[8:16], held[16:]
    expert = lax.broadcasted_iota(jnp.int32, (128, 640), 0)
    tile = 5 * ids[3] + (lax.broadcasted_iota(jnp.int32, (128, 640), 1) >> 7)
    spread[...] = ((tile >> 1) == expert).astype(F32)
    for load in loads[:8]:
        load.wait()
    put_pieces(places, pieces, mixed)
    stores[0].start()
    for load in loads[8:16]:
        load.wait()
    row = lax.broadcasted_iota(jnp.int32, (16, 1), 0)
    for k, piece in enumerate(routed):
        for j in range(8):
            rows = rows_at(places, 8 * k + j)
            inside = row < length[0] - places[8 * k + j] * 16
            kept = piece[16 * j : 16 * j + 16, :2048]
            grad_out[rows, :] = jnp.where(inside, kept, jnp.zeros((), BF))
            chosen_rows[rows, :] = piece[16 * j : 16 * j + 16, 2048:]
    stores[1].start()
    for load in loads[16:]:
        load.wait()
    lane = lax.broadcasted_iota(jnp.int32, (256, 128), 1)

    def block(b, _):
        rows = pl.ds(pl.multiple_of(b * 256, 256), 256)
        chosen = chosen_rows[rows, :].astype(F32)
        hidden = dot(mixed[rows, :1024], near[:, :1408]) + dot(mixed[rows, 1024:], far[:, :1408])
        out_grad = dot(grad_out[rows, :1024], near[:, 1408:]) + dot(
            grad_out[rows, 1024:], far[:, 1408:]
        )
        gate_h, up_h = hidden[:, :640], hidden[:, 640:1280]
        logits = jnp.where(lane < 10, hidden[:, 1280:], -1e30)
        raised = jnp.exp(logits - jnp.max(logits, axis=1, keepdims=True))
        route_probs = raised / jnp.sum(raised, axis=1, keepdims=True)
        gates = dot(route_probs * chosen, spread[...], 1, 0, HIGHEST)
        sig = 1.0 / (1.0 + jnp.exp(-gate_h))
        silu = gate_h * sig
        activated = (silu * up_h).astype(BF).astype(F32)
        gated[rows, :] = (activated * gates).astype(BF)
        act_grad = out_grad * gates
        hidden_grad[rows, :640] = (act_grad * up_h * sig * (1.0 + gate_h * (1.0 - sig))).astype(BF)
        hidden_grad[rows, 640:1280] = (act_grad * silu).astype(BF)
        chosen_grad = dot(activated * out_grad, spread[...], 1, 1, HIGHEST) * chosen
        inner = jnp.sum(chosen_grad * route_probs, axis=1, keepdims=True)
        hidden_grad[rows, 1280:] = (route_probs * (chosen_grad - inner)).astype(BF)
        return 0

    lax.fori_loop(0, 4, block, 0)
    stores[2].start()
    stores[3].start()
    for first in (4, 0):
        outs = made[first : first + 4]
        take_rows(places, hidden_grad, ordered, 8 * first)
        project(ordered, near, far, slice(0, 1408), outs)
        take_rows(places, gated, gated_ordered, 8 * first)
        project(gated_ordered, near, far, slice(1408, 2048), outs, 2048)
        for store in stores[4 + first : 8 + first]:
            store.start()
    for store in stores:
        store.wait()


def middle_grad_kernel(ids, length, *refs):
    terms, (middle, cot, gain, middle_grad, output), outs = refs[:8], refs[8:13], refs[13:]
    for i in range(4):
        rows = slice(16 * i, 16 * i + 16)
        inside = ids[2] + 16 * i + lax.broadcasted_iota(jnp.int32, (16, 1), 0) < length[0]
        grad = jnp.where(inside, cot[rows, :].astype(F32), 0.0)
        summed = terms[i][...].astype(F32) + terms[4 + i][...].astype(F32)
        scaled = summed[:, :2048] * gain[...]
        held = middle[rows, :]
        rate = lax.rsqrt(jnp.mean(held * held, axis=1, keepdims=True) + EPSILON)
        inner = jnp.mean(scaled * held, axis=1, keepdims=True)
        total = grad + rate * scaled - held * (rate * rate * rate * inner)
        middle_grad[rows, :] = total
        outs[i][...] = total.astype(BF)
        natural_order(held + summed[:, 2048:], ids[0], output.at[rows, :])


def backward_kernel(places, length, *refs):
    pieces, refs = refs[:8], refs[8:]
    (near, far, qkv, rates, gains, cosine, sine, queries, keys, values, log_total) = refs[:11]
    (branch, q_scaled, k_scaled, v_grad, inner, gain_grads) = refs[11:17]
    grad, key_grad, value_grad = refs[17:]

    def turn_back(held):
        return held * cosine[...] - pltpu.roll(held, 64, 1) * sine[...]

    put_pieces(places, pieces, branch)
    key_grad[...] = jnp.zeros_like(key_grad)
    value_grad[...] = jnp.zeros_like(value_grad)
    for at in range(4):
        rows, upto = slice(256 * at, 256 * at + 256), slice(0, 256 * at + 256)
        held = dot(branch[rows, :1024], near[:, 512:]) + dot(branch[rows, 1024:], far[:, 512:])
        grad[rows, :] = held.astype(BF)
        scores = dot(queries[rows, :], keys[upto, :], 1, 1) * SCALE
        probs = jnp.where(allowed_block(length, at), jnp.exp(scores - log_total[rows, :]), 0.0)
        prob_grad = dot(grad[rows, :], values[upto, :], 1, 1)
        delta = jnp.sum(probs * prob_grad, axis=1, keepdims=True)
        score_grad = (probs * (prob_grad - delta)).astype(BF)
        q_scaled[rows, :] = dot(score_grad, keys[upto, :]) * SCALE
        key_grad[upto, :] += dot(score_grad, queries[rows, :], 0, 0) * SCALE
        value_grad[upto, :] += dot(probs.astype(BF), grad[rows, :], 0, 0)
    v_grad[...] = value_grad[...].astype(BF)
    q_norm_grad = turn_back(q_scaled[...])
    k_norm_grad = turn_back(key_grad[...])
    q_turned = q_norm_grad * qkv[:, :128]
    k_turned = k_norm_grad * qkv[:, 128:256]
    gain_grads[0:1, :] = jnp.sum(q_turned * rates[:, 0:1], axis=0, keepdims=True)
    gain_grads[1:2, :] = jnp.sum(k_turned * rates[:, 1:2], axis=0, keepdims=True)
    for at, turned in enumerate((q_turned, k_turned)):
        products = turned * gains[at : at + 1, :]
        for b in range(4):
            put_sums(inner, at, b, row_sums(products[256 * b : 256 * b + 256]))
    q_scaled[...] = q_norm_grad * gains[0:1, :]
    k_scaled[...] = k_norm_grad * gains[1:2, :]


def exit_kernel(
    places, q_scaled, k_scaled, v_grad, qkv, rates, s0, s1, s2, s3, near, far, grad, *rest
):
    pieces, ordered = rest[:8], rest[8]
    for n, column in enumerate(as_column((s0[...] + s1[...]) + (s2[...] + s3[...]))):
        at, rows = n // 8, slice(128 * (n % 8), 128 * (n % 8) + 128)
        columns, scaled = slice(128 * at, 128 * at + 128), (q_scaled, k_scaled)[at]
        rate = rates[rows, at : at + 1]
        factor = rate * rate * rate * column * (1.0 / 2048)
        grad[rows, columns] = (rate * scaled[rows, :] - qkv[rows, columns] * factor).astype(BF)
    grad[:, 256:] = v_grad[...]
    take_rows(places, grad, ordered)
    project(ordered, near, far, slice(0, 384), pieces)


def exit_rest_kernel(places, grad, near, far, *refs):
    take_rows(places, grad, refs[4])
    project(refs[4], near, far, slice(0, 384), refs[:4])


def expert_weights_kernel(mixed, hidden_grad, grad_out, gated, near, far):
    for at, out in enumerate((near, far)):
        for n in range(1024 * at, 1024 * at + 1024, 512):
            rows, columns = slice(n - 1024 * at, n - 1024 * at + 512), slice(n, n + 512)
            out[rows, :1408] = dot(mixed[:, columns], hidden_grad[...], 0, 0).astype(BF)
            out[rows, 1408:] = dot(grad_out[:, columns], gated[...], 0, 0).astype(BF)


def attention_weights_kernel(ids, normed, qkv_grad, branch, attended, gain_grads, near, far):
    gains = jnp.concatenate([gain_grads[...], jnp.zeros((6, 128), F32)], axis=0).astype(BF)
    for at, out in enumerate((near, far)):
        columns = slice(1024 * at, 1024 * at + 1024)
        out[:, :384] = dot(normed[:, columns], qkv_grad[...], 0, 0).astype(BF)
        out[:, 384:512] = dot(branch[:, columns], attended[...], 0, 0).astype(BF)
        out[:, 512:] = jnp.zeros((1024, 128), BF)
        out[:, 512:520] = dot(gain_places(ids[0], at), gains, 1, 1).astype(BF)


def input_grad_kernel(ids, *refs):
    terms, (middle_grad, own, gain, out) = refs[:8], refs[8:]
    for i in range(4):
        rows = slice(16 * i, 16 * i + 16)
        scaled = (terms[i][...].astype(F32) + terms[4 + i][...].astype(F32)) * gain[...]
        held = own[rows, :].astype(F32)
        rate = lax.rsqrt(jnp.mean(held * held, axis=1, keepdims=True) + EPSILON)
        inner = jnp.mean(scaled * held, axis=1, keepdims=True)
        total = middle_grad[rows, :] + rate * scaled - held * (rate * rate * rate * inner)
        natural_order(total, ids[0], out.at[rows, :])


def both_kernel(ids, own, far, out):
    here = pl.multiple_of(ids[1] * 64, 64)
    out[pl.ds(here, 64), :] = own[...]
    out[pl.ds(64 - here, 64), :] = far[...]


def slots_kernel(ids, own, far, out):
    out[pl.ds(ids[0], 1), :, :] = own[...].astype(out.dtype)[None]
    out[pl.ds(1 - ids[0], 1), :, :] = far[...].astype(out.dtype)[None]


def angles(head_size):
    steps_half = np.arange(head_size // 2, dtype=np.float32)
    frequency = np.exp(steps_half * np.float32(-2.0 * math.log(ROPE_BASE) / head_size))
    turned = np.arange(1024, dtype=np.float32)[:, None] * frequency.astype(np.float32)[None, :]
    cosine, sine = np.cos(turned.astype(np.float64)), np.sin(turned.astype(np.float64))
    return (
        jnp.asarray(np.concatenate([cosine, cosine], axis=-1).astype(np.float32)),
        jnp.asarray(np.concatenate([-sine, sine], axis=-1).astype(np.float32)),
    )


def after(value, earlier):
    return lax.optimization_barrier((value, earlier))[0]


def per_device(
    tokens,
    lengths,
    routes,
    attn_gain,
    q_gain,
    k_gain,
    w_query,
    w_key,
    w_value,
    w_out,
    mlp_gain,
    router,
    w_gate,
    w_up,
    w_down,
    cotangent,
):
    z = lax.axis_index("z")
    yh = lax.axis_index("yh")
    core = lax.axis_index("c")

    own_place = (2 * z + lax.axis_index("yl")) * 128 + yh * 64
    x = lax.axis_index("x")
    ids = jnp.stack([core, yh, own_place, z, x & 1, x >> 1]).astype(jnp.int32)
    places = block_places()
    slot_length = lax.dynamic_slice(lengths, (core,), (1,))
    own_tokens, own_cot, *parts = prepare(
        ids, places, slot_length, tokens, cotangent, routes.swapaxes(1, 2)
    )
    (first_pack,) = kernel_call(first_pack_kernel, [((4, 64, 640), BF)], [VMEM] * 8, 8)(
        w_query, w_key, w_value, w_out.T, attn_gain[None], mlp_gain[None], q_gain, k_gain
    )

    swapped = swap_cores(after(first_pack, own_tokens))
    arrived = cube_step(parts, 0)
    parts = join(parts, arrived, [4224])
    held = all_to_all(after(swapped, arrived), "z").reshape(256, 640)
    arrived = cube_step(parts, 1)
    parts = join(parts, arrived, [4224])
    held = after(pair(4, ids, held, X_PAIR(held)), arrived)
    (second_pack,) = kernel_call(
        second_pack_kernel, [((4, 64, 2048), BF)], [VMEM] * 4, 12, earlier=arrived
    )(w_gate, w_up, w_down.swapaxes(1, 2), router.T)
    arrived = cube_step(parts, 2)
    joined = join(parts, arrived, [2048, 2176])
    first = after(pair(5, ids, held, X_ACROSS(held)), arrived)
    first_far = other_core(first)
    token_pieces, routed_pieces = list(joined[0::2]), list(joined[1::2])
    token_pieces += cube_step(token_pieces, 3)
    routed_pieces += cube_step(after(routed_pieces, token_pieces), 3)
    swapped = swap_cores(after(second_pack, token_pieces[4:]))

    normed, qkv, stats, lines, gain_rows = kernel_call(
        enter_kernel,
        [
            ((1024, 2048), BF),
            ((1024, 384), F32),
            ((16, 128), F32),
            ((2, 2048), F32),
            ((2, 128), F32),
        ],
        [SMEM] + [VMEM] * 8 + [SMEM] + [VMEM] * 2,
        24,
        2 * 1024 * 2048 * 384,
    )(places, *token_pieces, ids, first, first_far)
    attn_row, mlp_row = lines[0:1], lines[1:2]
    terms = token_terms(after(stats, routed_pieces[4:]))
    held = line_exchange(after(swapped, terms[0]), ids).reshape(256, 2048)
    cosine, sine = angles(128)
    rates, queries, keys, values, attended, log_total, *pieces = kernel_call(
        forward_kernel,
        [((1024, 2), F32), HEAD, HEAD, HEAD, HEAD, ((1024, 1), F32)] + [PIECE] * 8,
        [SMEM, SMEM] + [VMEM] * 10,
        28,
        4 * 1024 * 1024 * 128,
        [pltpu.VMEM((1024, 128), BF)],
    )(
        places, slot_length, qkv, *terms, gain_rows, cosine, sine, first, first_far
    )
    own_row = ((64, 2048), F32)
    own_part = ((16, 2048), BF)
    held = pair(4, ids, held, X_PAIR(after(held, pieces)))
    seen = []
    terms = cube_scatter(pieces, seen)
    second = pair(5, ids, held, X_ACROSS(after(held, seen[0])))
    middle, *parts = kernel_call(
        middle_kernel, [own_row] + [own_part] * 4, [VMEM] * 10, 8
    )(*terms, own_tokens, mlp_row)

    seen = []
    mixed_pieces = cube_gather(parts, seen)
    second_far = other_core(after(second, seen[1]))
    sums = [((1024, 2048), BF), ((1024, 2048), BF), ((1024, 640), BF), ((1024, 1408), BF)]
    sums += [((128, 4096), BF)] * 8
    taken = [*mixed_pieces, *routed_pieces, second, second_far]
    mixed, grad_out, gated, hidden_grad, *pieces = pl.pallas_call(
        mixture_kernel,
        out_shape=[jax.ShapeDtypeStruct(shape, kind) for shape, kind in sums],
        in_specs=[SMEM] * 3 + [ANY] * 18,
        out_specs=[ANY] * 12,
        scratch_shapes=[pltpu.VMEM(held.shape, BF) for held in taken]
        + [pltpu.VMEM(shape, BF) for shape, _ in sums]
        + [
            pltpu.VMEM((1024, 128), BF),
            pltpu.VMEM((512, 1408), BF),
            pltpu.VMEM((512, 640), BF),
            pltpu.VMEM((128, 640), F32),
            pltpu.SemaphoreType.DMA((18,)),
            pltpu.SemaphoreType.DMA((12,)),
        ],
        compiler_params=pltpu.CompilerParams(vmem_limit_bytes=58 * MIB),
        cost_estimate=pl.CostEstimate(
            flops=2 * 1024 * 2048 * 4096, bytes_accessed=36 * MIB, transcendentals=0
        ),
    )(places, slot_length, ids, *taken)
    seen = []
    terms = cube_scatter(pieces, seen)
    near, far = kernel_call(
        expert_weights_kernel,
        [((1024, 2048), BF)] * 2,
        [VMEM] * 4,
        40,
        2 * 1024 * 2048 * 2048,
    )(mixed, hidden_grad, grad_out, gated)
    keep, send = split(5, ids, near, other_core(after(far, seen[0])))
    far_seen = seen
    middle_grad, own_output, *parts = kernel_call(
        middle_grad_kernel,
        [own_row, ((64, 2048), BF)] + [own_part] * 4,
        [SMEM, SMEM] + [VMEM] * 11,
        8,
    )(ids, slot_length, *terms, middle, own_cot, mlp_row)
    seen = []
    branch_pieces = cube_gather(parts, seen)
    keep, send = split(4, ids, keep, X_ACROSS(after(send, far_seen[2])))
    send = after(send, seen[0])

    branch, q_scaled, k_scaled, v_grad, inner, gain_grads = kernel_call(
        backward_kernel,
        [((1024, 2048), BF), WIDE_HEAD, WIDE_HEAD, HEAD, ((16, 128), F32), ((2, 128), F32)],
        [SMEM, SMEM] + [VMEM] * 19,
        40,
        10 * 1024 * 1024 * 128,
        [pltpu.VMEM((1024, 128), BF), pltpu.VMEM((1024, 128), F32), pltpu.VMEM((1024, 128), F32)],
    )(
        places, slot_length, *branch_pieces, first, first_far,
        qkv, rates, gain_rows, cosine, sine, queries, keys, values, log_total,
    )
    def whole(own, kind, earlier=None):
        (both,) = kernel_call(both_kernel, [((128, 2048), BF)], [SMEM] + [VMEM] * 2, 4)(
            ids, own, other_half(own)
        )
        if earlier is not None:
            both = after(both, earlier)
        return kernel_call(slots_kernel, [((2, 128, 2048), kind)], [SMEM] + [VMEM] * 2, 8)(
            ids, both, other_core(both)
        )[0]

    expert_grads = (keep + X_PAIR(send)).reshape(4, 64, 2048)
    output = whole(after(own_output, seen[2]), BF, inner)
    qkv_grad, *pieces = kernel_call(
        exit_kernel,
        [((1024, 384), BF)] + [PIECE] * 8,
        [SMEM] + [VMEM] * 11,
        20,
        2 * 1024 * 2048 * 384,
        [pltpu.VMEM((1024, 384), BF)],
        [output, expert_grads],
    )(places, q_scaled, k_scaled, v_grad, qkv, rates, *token_terms(inner), first, first_far)
    seen = []
    terms = cube_scatter(pieces, seen)
    near, far = kernel_call(
        attention_weights_kernel,
        [((1024, 640), BF)] * 2,
        [SMEM] + [VMEM] * 5,
        24,
        2 * 1024 * 2048 * 512,
    )(ids, normed, qkv_grad, branch, attended, gain_grads)
    attn_grads = near + other_core(after(far, seen[0]))
    attn_grads = all_to_all(attn_grads.reshape(16, 64, 640), ("x", "z"))
    attn_grads = jnp.sum(attn_grads.reshape(4, 4, 64, 640).astype(F32), axis=0).astype(BF)
    attn_grads = swap_cores(attn_grads)
    (own_input_grad,) = kernel_call(
        input_grad_kernel, [((64, 2048), BF)], [SMEM] + [VMEM] * 11, 8, earlier=[attn_grads]
    )(ids, *terms, middle_grad, own_tokens, attn_row)
    expert_grads = swap_cores(after(expert_grads, seen[0]))
    expert_grads = line_exchange(after(expert_grads, own_input_grad), ids)

    q_grads, k_grads, v_grads, o_grads, attn_part = kernel_call(
        first_unpack_kernel,
        [((64, 512), F32)] * 4 + [((64, 128), F32)],
        [VMEM] * 4,
        8,
    )(attn_grads, w_query, w_key, w_value)
    o_grads = o_grads.T
    gate_grads, up_grads, down_grads, small = kernel_call(
        second_unpack_kernel,
        [((10, 64, 256), F32)] * 3 + [((64, 128), F32)],
        [VMEM] * 4,
        20,
    )(expert_grads, w_gate, w_up, router.T)
    summed = jnp.concatenate([small[:, :11], attn_part[:, :1]], axis=1)
    summed = summed + other_core(summed)
    summed = summed + other_half(summed)
    return (
        output,
        whole(own_input_grad, F32),
        summed[:, 11] / attn_gain.astype(F32),
        attn_grads[:, :4, 512].astype(F32),
        attn_grads[:, :4, 513].astype(F32),
        q_grads,
        k_grads,
        v_grads,
        o_grads,
        summed[:, 10] / mlp_gain.astype(F32),
        summed[:, :10],
        gate_grads,
        up_grads,
        down_grads.swapaxes(1, 2),
    )


def solution(mesh):
    fine = Mesh(mesh.devices.reshape(SIZES), AXES)
    rows = P("x", CONTEXT, None)
    vector = P(WEIGHT)
    gains = P(TENSOR, WEIGHT)
    tall = P(WEIGHT, TENSOR)
    routed = P(WEIGHT, None)
    hidden = P(None, WEIGHT, TENSOR)
    back = P(None, TENSOR, WEIGHT)
    weights = (vector, gains, gains, tall, tall, tall, gains, vector, routed, hidden, hidden, back)
    return jax.shard_map(
        per_device,
        mesh=fine,
        in_specs=(rows, P("x"), rows) + weights + (rows,),
        out_specs=(rows, rows) + weights,
        check_vma=False,
    )
```

```python
import math

import jax
import jax.numpy as jnp
import numpy as np
from jax import lax
from jax.experimental import pallas as pl
from jax.experimental.pallas import tpu as pltpu
from jax.sharding import Mesh
from jax.sharding import PartitionSpec as P

EPSILON = 1e-05
ROPE_BASE = 10000.0
SCALE = 128 ** (-0.5)
BF = jnp.bfloat16
F32 = jnp.float32
HIGHEST = lax.Precision.HIGHEST

AXES = ("x", "z", "yl", "yh", "c")
SIZES = (4, 4, 2, 2, 2)
CONTEXT = ("z", "yl")
TENSOR = ("yh", "c")
WEIGHT = ("x", "z", "yl")
GROUP = ("z", "yl", "yh")
Y = ("yl", "yh")
VMEM = pl.BlockSpec(memory_space=pltpu.VMEM)
SMEM = pl.BlockSpec(memory_space=pltpu.SMEM)
ANY = pl.BlockSpec(memory_space=pl.ANY)
MIB = 1024 * 1024


def exchange(axes, size, mask):
    pairs = [(at, at ^ mask) for at in range(size)]
    return lambda v: lax.ppermute(v, axes, pairs)


CUBE = (exchange("z", 4, 1), exchange(Y, 4, 2), exchange("z", 4, 3), exchange(Y, 4, 3))
ALONG_Z = (exchange("z", 4, 1), exchange("z", 4, 3), exchange("z", 4, 2))
ALONG_Y = (exchange(Y, 4, 2), exchange(Y, 4, 3), exchange(Y, 4, 1))
X_PAIR, X_ACROSS = exchange("x", 4, 1), exchange("x", 4, 3)
LINE = ("z", "yl", "c")


def swapped_along_z(mask):
    pairs = [
        (4 * z + 2 * yl + core, 4 * (z ^ mask) + 2 * core + yl)
        for z in range(4)
        for yl in range(2)
        for core in range(2)
    ]
    return lambda v: lax.ppermute(v, LINE, pairs)


SWAPPED = tuple(swapped_along_z(mask) for mask in (0, 1, 3, 2))
other_core = exchange("c", 2, 1)
other_half = exchange("yh", 2, 1)
other_both = exchange(TENSOR, 4, 3)


def dot(a, b, left=1, right=0, precision=None):
    return lax.dot_general(
        a, b, (((left,), (right,)), ((), ())), preferred_element_type=F32, precision=precision
    )


def dot_in_two(a, b, left, right):
    upper = a.astype(BF)
    return dot(upper, b, left, right) + dot((a - upper.astype(F32)).astype(BF), b, left, right)


def all_to_all(v, axes):
    return lax.all_to_all(v, axes, split_axis=0, concat_axis=0, tiled=True)


def kernel_call(body, outs, in_specs, limit, flops=0, scratch=(), earlier=()):
    def whole_body(*refs):
        body(*refs[len(earlier) :])

    call = pl.pallas_call(
        whole_body,
        out_shape=[jax.ShapeDtypeStruct(shape, kind) for shape, kind in outs],
        in_specs=[ANY] * len(earlier) + in_specs,
        out_specs=[VMEM] * len(outs),
        scratch_shapes=list(scratch),
        compiler_params=pltpu.CompilerParams(vmem_limit_bytes=limit * MIB),
        cost_estimate=pl.CostEstimate(flops=flops, bytes_accessed=4 * MIB, transcendentals=0),
    )
    return lambda *args: call(*earlier, *args)


PIECE = ((128, 2048), BF)
HEAD = ((1024, 128), BF)
WIDE_HEAD = ((1024, 128), F32)


def rows_at(places, at):
    return pl.ds(pl.multiple_of(places[at] * 16, 16), 16)


def join_kernel(*refs):
    half, cuts = refs[0].shape[0], len(refs[8:]) // 4
    for i in range(4):
        at = 0
        for out in refs[8 + cuts * i : 8 + cuts * i + cuts]:
            columns = slice(at, at + out.shape[1])
            out[:half, :] = refs[i][:, columns]
            out[half:, :] = refs[4 + i][:, columns]
            at += out.shape[1]


def join(parts, arrived, widths, earlier=()):
    rows = 2 * parts[0].shape[0]
    outs = [((rows, width), BF) for width in widths] * 4
    return kernel_call(join_kernel, outs, [VMEM] * 8, 16, earlier=earlier)(*parts, *arrived)


def cube_step(parts, step):
    return [CUBE[(i + step) % 4](parts[i]) for i in range(4)]


def cube_gather(parts, seen=None, earlier=None):
    parts = list(parts)
    for step in range(3):
        arrived = cube_step(parts, step)
        parts = join(parts, arrived, [parts[0].shape[1]], (earlier or {}).get(step, ()))
        if seen is not None:
            seen.append(arrived)
    return list(parts) + cube_step(parts, 3)


def pick_kernel(ids, blocks, *outs):
    for mask, out in zip((0, 1, 3, 2), outs):
        out[...] = blocks[pl.ds(ids[3] ^ mask, 1)]


def place_kernel(ids, own, a, b, c, out):
    for mask, held in zip((0, 1, 3, 2), (own, a, b, c)):
        out[pl.ds(ids[3] ^ mask, 1)] = held[...]


def pair_kernel(bit, ids, own, far, out):
    rows = own.shape[0]
    here = pl.multiple_of(ids[bit] * rows, rows)
    out[pl.ds(here, rows), :] = own[...]
    out[pl.ds(rows - here, rows), :] = far[...]


def pair(bit, ids, own, far):
    rows, width = own.shape
    return kernel_call(
        lambda *refs: pair_kernel(bit, *refs),
        [((2 * rows, width), BF)],
        [SMEM] + [VMEM] * 2,
        max(4, rows * width * 8 // MIB + 2),
    )(ids, own, far)[0]


def split_kernel(bit, ids, a, b, keep, send):
    rows = keep.shape[0]
    here = pl.multiple_of(ids[bit] * rows, rows)
    for out, at in ((keep, here), (send, rows - here)):
        for n in range(0, rows, 64):
            held = pl.ds(pl.multiple_of(at + n, 64), 64)
            out[n : n + 64, :] = (a[held, :].astype(F32) + b[held, :].astype(F32)).astype(BF)


def split(bit, ids, a, b):
    rows, width = a.shape
    return kernel_call(
        lambda *refs: split_kernel(bit, *refs),
        [((rows // 2, width), BF)] * 2,
        [SMEM] + [VMEM] * 2,
        max(4, rows * width * 8 // MIB + 2),
    )(ids, a, b)


def line_exchange(blocks, ids):
    sent = kernel_call(pick_kernel, [((1,) + blocks.shape[1:], BF)] * 4, [SMEM, VMEM], 8)(
        ids, blocks
    )
    arrived = [move(held) for move, held in zip(SWAPPED, sent)]
    return kernel_call(
        place_kernel, [(blocks.shape, BF)], [SMEM] + [VMEM] * 4, 8
    )(ids, *arrived)[0]


def token_terms(stats):
    held = stats + ALONG_Z[0](stats) + ALONG_Z[1](stats) + ALONG_Z[2](stats)
    return [held] + [move(held) for move in ALONG_Y]


def fold_kernel(*refs):
    half = refs[0].shape[0] // 2
    for i in range(4):
        kept, arrived, keep, send = refs[i], refs[4 + i], refs[8 + i], refs[12 + i]
        keep[...] = (kept[:half, :].astype(F32) + arrived[:half, :].astype(F32)).astype(BF)
        send[...] = (kept[half:, :].astype(F32) + arrived[half:, :].astype(F32)).astype(BF)


def cube_scatter(pieces, seen=None, earlier=None):
    kept, sent = pieces[:4], pieces[4:]
    for step in (3, 2, 1, 0):
        arrived = cube_step(sent, step)
        if seen is not None:
            seen.append(arrived)
        if step:
            half = ((kept[0].shape[0] // 2, kept[0].shape[1]), BF)
            folded = kernel_call(
                fold_kernel, [half] * 8, [VMEM] * 8, 16, earlier=(earlier or {}).get(step, ())
            )(*kept, *arrived)
            kept, sent = folded[:4], folded[4:]
    return list(kept) + arrived


def block_places():
    at = jnp.arange(64, dtype=jnp.int32)
    part, block = (at >> 3) & 3, (at & 7) | ((at >> 5) << 3)
    turned = [(block >> ((dim - part) & 3)) & 1 for dim in range(4)]
    z = lax.axis_index("z") ^ (turned[0] ^ (3 * turned[2]))
    y = (2 * lax.axis_index("yh") + lax.axis_index("yl")) ^ (turned[1] ^ (3 * turned[3]))
    return ((2 * z + (y & 1)) * 2 + (y >> 1)) * 4 + part


def put_pieces(places, pieces, out):
    for k, piece in enumerate(pieces):
        for j in range(8):
            out[rows_at(places, 8 * k + j), :] = piece[16 * j : 16 * j + 16, :]


def take_rows(places, source, out, start=0):
    for n in range(out.shape[0] // 16):
        out[16 * n : 16 * n + 16, :] = source[rows_at(places, start + n), :]


def project(rows, near, far, columns, pieces, start=0):
    for b in range(len(pieces) // 2):
        held = rows[256 * b : 256 * b + 256, :]
        for at, weight in enumerate((near, far)):
            wide = dot(held, weight[:, columns], 1, 1).astype(BF)
            place = slice(start + 1024 * at, start + 1024 * at + 1024)
            for k in range(2):
                pieces[2 * b + k][:, place] = wide[128 * k : 128 * k + 128]


def natural_order(near, core, out):
    first = lax.broadcasted_iota(jnp.int32, (near.shape[0], 128), 1) < 64
    for j in range(8):
        mine = near[:, 128 * j : 128 * j + 128]
        other = near[:, 1024 + 128 * j : 1024 + 128 * j + 128]
        low = jnp.where(core == 0, mine, other)
        high = jnp.where(core == 0, other, mine)
        out[:, 256 * j : 256 * j + 128] = jnp.where(first, low, pltpu.roll(high, 64, 1)).astype(BF)
        out[:, 256 * j + 128 : 256 * j + 256] = jnp.where(
            first, pltpu.roll(low, 64, 1), high
        ).astype(BF)


def prepare_kernel(ids, places, length, tokens, cot, routes, own_tokens, own_cot, p0, p1, p2, p3, wide):
    core, parts = ids[0], (p0, p1, p2, p3)
    first = lax.broadcasted_iota(jnp.int32, (64, 128), 1) < 64
    for source, out, at in ((tokens, own_tokens, 0), (cot, own_cot, 2048)):
        for j in range(8):
            a = source[0, :, 256 * j : 256 * j + 128].astype(F32)
            b = source[0, :, 256 * j + 128 : 256 * j + 256].astype(F32)
            low = jnp.where(first, a, pltpu.roll(b, 64, 1))
            high = jnp.where(first, pltpu.roll(a, 64, 1), b)
            out[:, 128 * j : 128 * j + 128] = jnp.where(core == 0, low, high).astype(BF)
            out[:, 1024 + 128 * j : 1152 + 128 * j] = jnp.where(core == 0, high, low).astype(BF)
        for i in range(4):
            parts[i][:, at : at + 2048] = out[16 * i : 16 * i + 16, :]
    expert = lax.broadcasted_iota(jnp.int32, (128, 128), 0)
    chosen = jnp.zeros((128, 128), F32)
    for k in range(8):
        chosen += (expert == routes[0, k : k + 1, :]).astype(F32)
    wide[...] = dot(chosen.astype(BF), identity(128, BF), 0, 0)
    for i in range(4):
        rows = pl.ds(pl.multiple_of(ids[1] * 64 + 16 * i, 16), 16)
        parts[i][:, 4096:] = wide[rows, :].astype(BF)


def prepare(ids, places, length, tokens, cot, routes):
    own = lambda n, ids: (ids[0], ids[1], 0)
    whole = lambda n, ids: (0, 0)
    return pl.pallas_call(
        prepare_kernel,
        grid_spec=pltpu.PrefetchScalarGridSpec(
            num_scalar_prefetch=1,
            grid=(1,),
            in_specs=[
                SMEM,
                SMEM,
                pl.BlockSpec((1, 64, 2048), own),
                pl.BlockSpec((1, 64, 2048), own),
                pl.BlockSpec((1, 8, 128), lambda n, ids: (ids[0], 0, 0)),
            ],
            out_specs=[pl.BlockSpec((64, 2048), whole)] * 2 + [pl.BlockSpec((16, 4224), whole)] * 4,
            scratch_shapes=[pltpu.VMEM((128, 128), F32)],
        ),
        out_shape=[jax.ShapeDtypeStruct((64, 2048), BF)] * 2
        + [jax.ShapeDtypeStruct((16, 4224), BF)] * 4,
        compiler_params=pltpu.CompilerParams(vmem_limit_bytes=8 * MIB),
    )(ids, places, length, tokens, cot, routes)


def identity(size, kind):
    row = lax.broadcasted_iota(jnp.int32, (size, size), 0)
    return (row == lax.broadcasted_iota(jnp.int32, (size, size), 1)).astype(kind)


def first_pack_kernel(query, key, value, w_out, attn_gain, mlp_gain, q_gain, k_gain, out):
    row = lax.broadcasted_iota(jnp.int32, (64, 128), 0)
    lane = lax.broadcasted_iota(jnp.int32, (64, 128), 1)
    extra = jnp.zeros((64, 128), F32)
    for at, gain in enumerate((attn_gain, mlp_gain)):
        column = jnp.sum(gain[...].astype(F32) * identity(64, F32), axis=1, keepdims=True)
        extra = jnp.where(lane == at, column, extra)
    for k in range(4):
        columns = slice(128 * k, 128 * k + 128)
        for at, w in ((0, query), (128, key), (256, value), (512, w_out)):
            out[k, :, at : at + 128] = w[:, columns]
        held = extra
        for at, gain in enumerate((q_gain, k_gain)):
            for j in range(4):
                here = jnp.logical_and(row == j, lane == 2 + at)
                held = jnp.where(here, gain[k : k + 1, j : j + 1].astype(F32), held)
        out[k, :, 384:512] = held.astype(BF)


def second_pack_kernel(gate, up, down, router, out):
    lane = lax.broadcasted_iota(jnp.int32, (64, 128), 1)
    routed = jnp.zeros((64, 128), F32)
    for e in range(10):
        column = jnp.sum(
            router[e : e + 1, :].astype(F32) * identity(64, F32), axis=1, keepdims=True
        )
        routed = jnp.where(lane == e, column, routed)
    for k in range(4):
        for m in range(5):
            tile = 5 * k + m
            columns = slice(128 * (tile % 2), 128 * (tile % 2) + 128)
            for w, at in ((gate, 0), (up, 640), (down, 1408)):
                out[k, :, at + 128 * m : at + 128 * m + 128] = w[tile // 2, :, columns]
        out[k, :, 1280:1408] = routed.astype(BF)


def second_unpack_kernel(grads, gate, up, router, gate_out, up_out, down_out, small):
    part = jnp.zeros((64, 1), F32)
    routed = jnp.zeros((64, 128), F32)
    for k in range(4):
        for m in range(5):
            tile = 5 * k + m
            expert, columns = tile // 2, slice(128 * (tile % 2), 128 * (tile % 2) + 128)
            for w, out, at in ((gate, gate_out, 0), (up, up_out, 640), (None, down_out, 1408)):
                held = grads[k, :, at + 128 * m : at + 128 * m + 128].astype(F32)
                out[expert, :, columns] = held
                if w is not None:
                    held = held * w[expert, :, columns].astype(F32)
                    part += jnp.sum(held, axis=1, keepdims=True)
        routed += grads[k, :, 1280:1408].astype(F32)
    weights = dot(identity(64, BF), router[...], 1, 1)
    part += jnp.sum(routed[:, :10] * weights, axis=1, keepdims=True)
    lane = lax.broadcasted_iota(jnp.int32, (64, 128), 1)
    small[...] = jnp.where(lane < 10, routed, 0.0) + jnp.where(lane == 10, part, 0.0)


def first_unpack_kernel(grads, query, key, value, query_out, key_out, value_out, out_out, small):
    part = jnp.zeros((64, 1), F32)
    for k in range(4):
        columns = slice(128 * k, 128 * k + 128)
        for at, (w, out) in enumerate(((query, query_out), (key, key_out), (value, value_out))):
            held = grads[k, :, 128 * at : 128 * at + 128].astype(F32)
            out[:, columns] = held
            part += jnp.sum(held * w[:, columns].astype(F32), axis=1, keepdims=True)
        out_out[:, columns] = grads[k, :, 384:512].astype(F32)
    small[...] = jnp.broadcast_to(part, (64, 128))


def as_column(rows):
    eye = identity(128, F32)
    return [
        jnp.sum(rows[n : n + 1, :] * eye, axis=1, keepdims=True) for n in range(rows.shape[0])
    ]


def row_sums(v):
    return dot(jnp.ones((8, 128), F32), v, 1, 1, HIGHEST)[0:1]


def put_sums(stats, at, b, row):
    for half in range(2):
        place = 8 * at + 2 * b + half
        stats[place : place + 1, :] = row[:, 128 * half : 128 * half + 128]


def gain_places(core, at):
    row = lax.broadcasted_iota(jnp.int32, (1024, 128), 0)
    element = lax.broadcasted_iota(jnp.int32, (1024, 128), 1)
    yl = core if at == 0 else 1 - core
    here = ((row >> 6) * 2 + yl) * 4 + (row & 63) == element
    return jnp.where(jnp.logical_and(here, (row & 63) < 4), 1.0, 0.0).astype(BF)


def gain_line(near, far, column, out):
    eye = identity(128, F32)
    for at, weight in enumerate((near, far)):
        for b in range(8):
            held = weight[128 * b : 128 * b + 128, 384:512].astype(F32)
            line = jnp.sum(held[:, column : column + 1] * eye, axis=0, keepdims=True)
            out[0:1, 1024 * at + 128 * b : 1024 * at + 128 * b + 128] = line


def gains_kernel(ids, near, far, line, gains):
    gain_line(near, far, 1, line)
    total = jnp.zeros((128, 128), F32)
    for at, weight in enumerate((near, far)):
        total += dot(weight[:, 384:512], gain_places(ids[0], at), 0, 0)
    gains[...] = total[2:4, :]


def enter_kernel(places, *refs):
    pieces, (near, far, normed, gain) = refs[:8], refs[8:]
    gain_line(near, far, 0, gain)
    for k in range(8):

        def norm_rows(j, _):
            held = pieces[k][pl.ds(pl.multiple_of(j * 16, 16), 16), :].astype(F32)
            rate = lax.rsqrt(jnp.mean(held * held, axis=1, keepdims=True) + EPSILON)
            normed[rows_at(places, 8 * k + j), :] = (held * rate * gain[...]).astype(BF)
            return 0

        lax.fori_loop(0, 8, norm_rows, 0)


def project_kernel(normed, near, far, qkv, stats):
    for b in range(4):
        rows = slice(256 * b, 256 * b + 256)
        held = dot(normed[rows, :1024], near[:, :384]) + dot(normed[rows, 1024:], far[:, :384])
        qkv[rows, :] = held
        for at in range(2):
            columns = slice(128 * at, 128 * at + 128)
            put_sums(stats, at, b, row_sums(held[:, columns] * held[:, columns]))


def allowed_block(length, at):
    q_pos = 256 * at + lax.broadcasted_iota(jnp.int32, (256, 256 * at + 256), 0)
    k_pos = lax.broadcasted_iota(jnp.int32, (256, 256 * at + 256), 1)
    return jnp.logical_and(k_pos <= q_pos, k_pos < length[0])


def forward_kernel(
    places, length, qkv, s0, s1, s2, s3, gains, cosine, sine, near, far,
    rates, queries, keys, values, attended, log_total, *rest,
):
    pieces, ordered = rest[:8], rest[8]
    for n, column in enumerate(as_column((s0[...] + s1[...]) + (s2[...] + s3[...]))):
        rate = lax.rsqrt(column * (1.0 / 2048) + EPSILON)
        rates[128 * (n % 8) : 128 * (n % 8) + 128, n // 8 : n // 8 + 1] = rate

    def turn(held):
        return held * cosine[...] + pltpu.roll(held, 64, 1) * sine[...]

    queries[...] = turn(qkv[:, :128] * rates[:, 0:1] * gains[0:1, :]).astype(BF)
    keys[...] = turn(qkv[:, 128:256] * rates[:, 1:2] * gains[1:2, :]).astype(BF)
    values[...] = qkv[:, 256:].astype(BF)
    for at in range(4):
        rows, upto = slice(256 * at, 256 * at + 256), slice(0, 256 * at + 256)
        scores = dot(queries[rows, :], keys[upto, :], 1, 1) * SCALE
        scores = jnp.where(allowed_block(length, at), scores, -1e30)
        peak = jnp.max(scores, axis=1, keepdims=True)
        raised = jnp.exp(scores - peak)
        total = jnp.sum(raised, axis=1, keepdims=True)
        probs = (raised * (1.0 / total)).astype(BF)
        attended[rows, :] = dot(probs, values[upto, :]).astype(BF)
        log_total[rows, :] = peak + jnp.log(total)
    take_rows(places, attended, ordered)
    project(ordered, near, far, slice(512, 640), pieces)


def middle_kernel(*refs):
    terms, (own, gain, middle), outs = refs[:8], refs[8:11], refs[11:]
    for i in range(4):
        rows = slice(16 * i, 16 * i + 16)
        held = own[rows, :].astype(F32) + (terms[i][...].astype(F32) + terms[4 + i][...].astype(F32))
        middle[rows, :] = held
        rate = lax.rsqrt(jnp.mean(held * held, axis=1, keepdims=True) + EPSILON)
        outs[i][...] = (held * rate * gain[...]).astype(BF)


def mixture_kernel(places, length, ids, *refs):
    arrays, scratch = refs[:30], refs[30:]
    sources, outs = arrays[:18], arrays[18:]
    buffers, (near, far, mixed, grad_out, gated, hidden_grad) = scratch[:8], scratch[8:14]
    chosen_rows, ordered, gated_ordered, spread, in_sems, out_sems = scratch[14:]
    pieces = [held.at[:, :2048] for held in buffers]
    routed = [held.at[:, 2048:] for held in buffers]
    made = [held.at[:, :4096] for held in buffers]
    held = pieces + routed + [near, far]
    loads = [
        pltpu.make_async_copy(source, target, in_sems.at[n])
        for n, (source, target) in enumerate(zip(sources, held))
    ]
    stores = [
        pltpu.make_async_copy(source, target, out_sems.at[n])
        for n, (source, target) in enumerate(
            zip([mixed, grad_out, gated, hidden_grad] + made, outs)
        )
    ]
    for load in loads:
        load.start()
    expert = lax.broadcasted_iota(jnp.int32, (128, 640), 0)
    tile = 5 * ids[3] + (lax.broadcasted_iota(jnp.int32, (128, 640), 1) >> 7)
    spread[...] = ((tile >> 1) == expert).astype(F32).astype(BF)
    for load in loads[:8]:
        load.wait()
    put_pieces(places, pieces, mixed)
    stores[0].start()
    for load in loads[8:16]:
        load.wait()
    row = lax.broadcasted_iota(jnp.int32, (16, 1), 0)
    for k, piece in enumerate(routed):
        for j in range(8):
            rows = rows_at(places, 8 * k + j)
            inside = row < length[0] - places[8 * k + j] * 16
            kept = piece[16 * j : 16 * j + 16, :2048]
            grad_out[rows, :] = jnp.where(inside, kept, jnp.zeros((), BF))
            chosen_rows[rows, :] = piece[16 * j : 16 * j + 16, 2048:]
    stores[1].start()
    for load in loads[16:]:
        load.wait()
    lane = lax.broadcasted_iota(jnp.int32, (512, 128), 1)

    def block(b, _):
        rows = pl.ds(pl.multiple_of(b * 512, 512), 512)
        chosen = chosen_rows[rows, :].astype(F32)
        hidden = dot(mixed[rows, :1024], near[:, :1408]) + dot(mixed[rows, 1024:], far[:, :1408])
        out_grad = dot(grad_out[rows, :1024], near[:, 1408:]) + dot(
            grad_out[rows, 1024:], far[:, 1408:]
        )
        gate_h, up_h = hidden[:, :640], hidden[:, 640:1280]
        logits = jnp.where(lane < 10, hidden[:, 1280:], -1e30)
        raised = jnp.exp(logits - jnp.max(logits, axis=1, keepdims=True))
        route_probs = raised / jnp.sum(raised, axis=1, keepdims=True)
        gates = dot_in_two(route_probs * chosen, spread[...], 1, 0)
        sig = 1.0 / (1.0 + jnp.exp(-gate_h))
        silu = gate_h * sig
        activated = (silu * up_h).astype(BF).astype(F32)
        gated[rows, :] = (activated * gates).astype(BF)
        act_grad = out_grad * gates
        hidden_grad[rows, :640] = (act_grad * up_h * sig * (1.0 + gate_h * (1.0 - sig))).astype(BF)
        hidden_grad[rows, 640:1280] = (act_grad * silu).astype(BF)
        chosen_grad = dot_in_two(activated * out_grad, spread[...], 1, 1) * chosen
        inner = jnp.sum(chosen_grad * route_probs, axis=1, keepdims=True)
        hidden_grad[rows, 1280:] = (route_probs * (chosen_grad - inner)).astype(BF)
        return 0

    lax.fori_loop(0, 2, block, 0)
    stores[2].start()
    stores[3].start()
    for first in (4, 0):
        outs = made[first : first + 4]
        take_rows(places, hidden_grad, ordered, 8 * first)
        project(ordered, near, far, slice(0, 1408), outs)
        take_rows(places, gated, gated_ordered, 8 * first)
        project(gated_ordered, near, far, slice(1408, 2048), outs, 2048)
        for store in stores[4 + first : 8 + first]:
            store.start()
    for store in stores:
        store.wait()


def middle_grad_kernel(ids, length, *refs):
    terms, (middle, cot, gain, middle_grad, output), outs = refs[:8], refs[8:13], refs[13:]
    for i in range(4):
        rows = slice(16 * i, 16 * i + 16)
        inside = ids[2] + 16 * i + lax.broadcasted_iota(jnp.int32, (16, 1), 0) < length[0]
        grad = jnp.where(inside, cot[rows, :].astype(F32), 0.0)
        summed = terms[i][...].astype(F32) + terms[4 + i][...].astype(F32)
        scaled = summed[:, :2048] * gain[...]
        held = middle[rows, :]
        rate = lax.rsqrt(jnp.mean(held * held, axis=1, keepdims=True) + EPSILON)
        inner = jnp.mean(scaled * held, axis=1, keepdims=True)
        total = grad + rate * scaled - held * (rate * rate * rate * inner)
        middle_grad[rows, :] = total
        outs[i][...] = total.astype(BF)
        natural_order(held + summed[:, 2048:], ids[0], output.at[rows, :])


def backward_kernel(places, length, *refs):
    pieces, refs = refs[:8], refs[8:]
    (near, far, qkv, rates, gains, cosine, sine, queries, keys, values, log_total) = refs[:11]
    (branch, q_scaled, k_scaled, v_grad, inner, gain_grads) = refs[11:17]
    grad, key_grad, value_grad = refs[17:]

    def turn_back(held):
        return held * cosine[...] - pltpu.roll(held, 64, 1) * sine[...]

    put_pieces(places, pieces, branch)
    key_grad[...] = jnp.zeros_like(key_grad)
    value_grad[...] = jnp.zeros_like(value_grad)
    for at in range(4):
        rows, upto = slice(256 * at, 256 * at + 256), slice(0, 256 * at + 256)
        held = dot(branch[rows, :1024], near[:, 512:]) + dot(branch[rows, 1024:], far[:, 512:])
        grad[rows, :] = held.astype(BF)
        scores = dot(queries[rows, :], keys[upto, :], 1, 1) * SCALE
        probs = jnp.where(allowed_block(length, at), jnp.exp(scores - log_total[rows, :]), 0.0)
        prob_grad = dot(grad[rows, :], values[upto, :], 1, 1)
        delta = jnp.sum(probs * prob_grad, axis=1, keepdims=True)
        score_grad = (probs * (prob_grad - delta)).astype(BF)
        q_scaled[rows, :] = dot(score_grad, keys[upto, :]) * SCALE
        key_grad[upto, :] += dot(score_grad, queries[rows, :], 0, 0) * SCALE
        value_grad[upto, :] += dot(probs.astype(BF), grad[rows, :], 0, 0)
    v_grad[...] = value_grad[...].astype(BF)
    q_norm_grad = turn_back(q_scaled[...])
    k_norm_grad = turn_back(key_grad[...])
    q_turned = q_norm_grad * qkv[:, :128]
    k_turned = k_norm_grad * qkv[:, 128:256]
    gain_grads[0:1, :] = jnp.sum(q_turned * rates[:, 0:1], axis=0, keepdims=True)
    gain_grads[1:2, :] = jnp.sum(k_turned * rates[:, 1:2], axis=0, keepdims=True)
    for at, turned in enumerate((q_turned, k_turned)):
        products = turned * gains[at : at + 1, :]
        for b in range(4):
            put_sums(inner, at, b, row_sums(products[256 * b : 256 * b + 256]))
    q_scaled[...] = q_norm_grad * gains[0:1, :]
    k_scaled[...] = k_norm_grad * gains[1:2, :]


def exit_kernel(
    places, q_scaled, k_scaled, v_grad, qkv, rates, s0, s1, s2, s3, near, far, grad, *rest
):
    pieces, ordered = rest[:8], rest[8]
    for n, column in enumerate(as_column((s0[...] + s1[...]) + (s2[...] + s3[...]))):
        at, rows = n // 8, slice(128 * (n % 8), 128 * (n % 8) + 128)
        columns, scaled = slice(128 * at, 128 * at + 128), (q_scaled, k_scaled)[at]
        rate = rates[rows, at : at + 1]
        factor = rate * rate * rate * column * (1.0 / 2048)
        grad[rows, columns] = (rate * scaled[rows, :] - qkv[rows, columns] * factor).astype(BF)
    grad[:, 256:] = v_grad[...]
    take_rows(places, grad, ordered)
    project(ordered, near, far, slice(0, 384), pieces)


def exit_rest_kernel(places, grad, near, far, *refs):
    take_rows(places, grad, refs[4])
    project(refs[4], near, far, slice(0, 384), refs[:4])


def expert_weights_kernel(mixed, hidden_grad, grad_out, gated, near, far):
    for at, out in enumerate((near, far)):
        for n in range(1024 * at, 1024 * at + 1024, 512):
            rows, columns = slice(n - 1024 * at, n - 1024 * at + 512), slice(n, n + 512)
            out[rows, :1408] = dot(mixed[:, columns], hidden_grad[...], 0, 0).astype(BF)
            out[rows, 1408:] = dot(grad_out[:, columns], gated[...], 0, 0).astype(BF)


def attention_weights_kernel(ids, normed, qkv_grad, branch, attended, gain_grads, near, far):
    gains = jnp.concatenate([gain_grads[...], jnp.zeros((6, 128), F32)], axis=0).astype(BF)
    for at, out in enumerate((near, far)):
        columns = slice(1024 * at, 1024 * at + 1024)
        out[:, :384] = dot(normed[:, columns], qkv_grad[...], 0, 0).astype(BF)
        out[:, 384:512] = dot(branch[:, columns], attended[...], 0, 0).astype(BF)
        out[:, 512:] = jnp.zeros((1024, 128), BF)
        out[:, 512:520] = dot(gain_places(ids[0], at), gains, 1, 1).astype(BF)


def input_grad_kernel(ids, *refs):
    terms, (middle_grad, own, gain, out) = refs[:8], refs[8:]
    for i in range(4):
        rows = slice(16 * i, 16 * i + 16)
        scaled = (terms[i][...].astype(F32) + terms[4 + i][...].astype(F32)) * gain[...]
        held = own[rows, :].astype(F32)
        rate = lax.rsqrt(jnp.mean(held * held, axis=1, keepdims=True) + EPSILON)
        inner = jnp.mean(scaled * held, axis=1, keepdims=True)
        total = middle_grad[rows, :] + rate * scaled - held * (rate * rate * rate * inner)
        natural_order(total, ids[0], out.at[rows, :])


def both_kernel(ids, own, far, out):
    here = pl.multiple_of(ids[1] * 64, 64)
    out[pl.ds(here, 64), :] = own[...]
    out[pl.ds(64 - here, 64), :] = far[...]


def two_slots_kernel(ids, own, far, out):
    out[pl.ds(ids[0], 1), :, :] = own[...][None]
    out[pl.ds(1 - ids[0], 1), :, :] = far[...][None]


def slots_kernel(ids, own, half, core, both, out):
    here = pl.multiple_of(ids[1] * 64, 64)
    for slot, near, far in ((ids[0], own, half), (1 - ids[0], core, both)):
        out[slot, pl.ds(here, 64), :] = near[...].astype(out.dtype)
        out[slot, pl.ds(64 - here, 64), :] = far[...].astype(out.dtype)


def angles(head_size):
    steps_half = np.arange(head_size // 2, dtype=np.float32)
    frequency = np.exp(steps_half * np.float32(-2.0 * math.log(ROPE_BASE) / head_size))
    turned = np.arange(1024, dtype=np.float32)[:, None] * frequency.astype(np.float32)[None, :]
    cosine, sine = np.cos(turned.astype(np.float64)), np.sin(turned.astype(np.float64))
    return (
        jnp.asarray(np.concatenate([cosine, cosine], axis=-1).astype(np.float32)),
        jnp.asarray(np.concatenate([-sine, sine], axis=-1).astype(np.float32)),
    )


def after(value, earlier):
    return lax.optimization_barrier((value, earlier))[0]


def per_device(
    tokens,
    lengths,
    routes,
    attn_gain,
    q_gain,
    k_gain,
    w_query,
    w_key,
    w_value,
    w_out,
    mlp_gain,
    router,
    w_gate,
    w_up,
    w_down,
    cotangent,
):
    z = lax.axis_index("z")
    yh = lax.axis_index("yh")
    core = lax.axis_index("c")

    own_place = (2 * z + lax.axis_index("yl")) * 128 + yh * 64
    x = lax.axis_index("x")
    ids = jnp.stack([core, yh, own_place, z, x & 1, x >> 1]).astype(jnp.int32)
    places = block_places()
    slot_length = lax.dynamic_slice(lengths, (core,), (1,))
    own_tokens, own_cot, *parts = prepare(
        ids, places, slot_length, tokens, cotangent, routes.swapaxes(1, 2)
    )
    (first_pack,) = kernel_call(first_pack_kernel, [((4, 64, 640), BF)], [VMEM] * 8, 8)(
        w_query, w_key, w_value, w_out.T, attn_gain[None], mlp_gain[None], q_gain, k_gain
    )

    held = line_exchange(after(first_pack, own_tokens), ids).reshape(256, 640)
    arrived = cube_step(parts, 0)
    parts = join(parts, arrived, [4224])
    arrived = cube_step(parts, 1)
    parts = join(parts, arrived, [4224])
    held = after(pair(4, ids, held, X_PAIR(held)), arrived)
    (second_pack,) = kernel_call(
        second_pack_kernel, [((4, 64, 2048), BF)], [VMEM] * 4, 12, earlier=arrived
    )(w_gate, w_up, w_down.swapaxes(1, 2), router.T)
    arrived = cube_step(parts, 2)
    joined = join(parts, arrived, [2048, 2176])
    first = after(pair(5, ids, held, X_ACROSS(held)), joined)
    first_far = other_core(first)
    token_pieces, routed_pieces = list(joined[0::2]), list(joined[1::2])
    token_pieces += cube_step(token_pieces, 3)
    routed_pieces += cube_step(after(routed_pieces, token_pieces), 3)

    normed, attn_row = kernel_call(
        enter_kernel,
        [((1024, 2048), BF), ((1, 2048), F32)],
        [SMEM] + [VMEM] * 10,
        20,
        2 * 1024 * 2048 * 384,
    )(places, *token_pieces, first, first_far)
    qkv, stats = kernel_call(
        project_kernel,
        [((1024, 384), F32), ((16, 128), F32)],
        [VMEM] * 3,
        20,
        2 * 1024 * 2048 * 384,
        earlier=routed_pieces[4:],
    )(normed, first, first_far)
    mlp_row, gain_rows = kernel_call(
        gains_kernel, [((1, 2048), F32), ((2, 128), F32)], [SMEM] + [VMEM] * 2, 12, earlier=[stats]
    )(ids, first, first_far)
    terms = token_terms(stats)
    held = line_exchange(after(second_pack, terms[1:]), ids).reshape(256, 2048)
    cosine, sine = angles(128)
    rates, queries, keys, values, attended, log_total, *pieces = kernel_call(
        forward_kernel,
        [((1024, 2), F32), HEAD, HEAD, HEAD, HEAD, ((1024, 1), F32)] + [PIECE] * 8,
        [SMEM, SMEM] + [VMEM] * 10,
        28,
        4 * 1024 * 1024 * 128,
        [pltpu.VMEM((1024, 128), BF)],
    )(
        places, slot_length, qkv, *terms, gain_rows, cosine, sine, first, first_far
    )
    own_row = ((64, 2048), F32)
    own_part = ((16, 2048), BF)
    held = pair(4, ids, held, X_PAIR(after(held, pieces)))
    seen = []
    terms = cube_scatter(pieces, seen)
    second = pair(5, ids, held, X_ACROSS(after(held, seen[1])))
    middle, *parts = kernel_call(
        middle_kernel, [own_row] + [own_part] * 4, [VMEM] * 10, 8
    )(*terms, own_tokens, mlp_row)

    seen = []
    mixed_pieces = cube_gather(parts, seen)
    second_far = other_core(after(second, seen[2]))
    sums = [((1024, 2048), BF), ((1024, 2048), BF), ((1024, 640), BF), ((1024, 1408), BF)]
    sums += [((128, 4096), BF)] * 8
    taken = [*mixed_pieces, *routed_pieces, second, second_far]
    mixed, grad_out, gated, hidden_grad, *pieces = pl.pallas_call(
        mixture_kernel,
        out_shape=[jax.ShapeDtypeStruct(shape, kind) for shape, kind in sums],
        in_specs=[SMEM] * 3 + [ANY] * 18,
        out_specs=[ANY] * 12,
        scratch_shapes=[pltpu.VMEM((128, 4224), BF)] * 8
        + [pltpu.VMEM((1024, 2048), BF)] * 2
        + [pltpu.VMEM(shape, BF) for shape, _ in sums[:4]]
        + [
            pltpu.VMEM((1024, 128), BF),
            pltpu.VMEM((512, 1408), BF),
            pltpu.VMEM((512, 640), BF),
            pltpu.VMEM((128, 640), BF),
            pltpu.SemaphoreType.DMA((18,)),
            pltpu.SemaphoreType.DMA((12,)),
        ],
        compiler_params=pltpu.CompilerParams(vmem_limit_bytes=58 * MIB),
        cost_estimate=pl.CostEstimate(
            flops=2 * 1024 * 2048 * 4096, bytes_accessed=36 * MIB, transcendentals=0
        ),
    )(places, slot_length, ids, *taken)
    seen = []
    terms = cube_scatter(pieces, seen)
    near, far = kernel_call(
        expert_weights_kernel,
        [((1024, 2048), BF)] * 2,
        [VMEM] * 4,
        40,
        2 * 1024 * 2048 * 2048,
    )(mixed, hidden_grad, grad_out, gated)
    keep, send = split(5, ids, near, other_core(after(far, seen[0])))
    first_send = X_ACROSS(after(send, seen[2]))
    middle_grad, own_output, *parts = kernel_call(
        middle_grad_kernel,
        [own_row, ((64, 2048), BF)] + [own_part] * 4,
        [SMEM, SMEM] + [VMEM] * 11,
        8,
    )(ids, slot_length, *terms, middle, own_cot, mlp_row)
    keep, send = split(4, ids, keep, first_send)
    seen = []
    branch_pieces = cube_gather(parts, seen)
    expert_grads = (keep + X_PAIR(after(send, seen[0]))).reshape(4, 64, 2048)
    output_far = other_half(after(own_output, seen[2]))

    branch, q_scaled, k_scaled, v_grad, inner, gain_grads = kernel_call(
        backward_kernel,
        [((1024, 2048), BF), WIDE_HEAD, WIDE_HEAD, HEAD, ((16, 128), F32), ((2, 128), F32)],
        [SMEM, SMEM] + [VMEM] * 19,
        40,
        10 * 1024 * 1024 * 128,
        [pltpu.VMEM((1024, 128), BF), pltpu.VMEM((1024, 128), F32), pltpu.VMEM((1024, 128), F32)],
    )(
        places, slot_length, *branch_pieces, first, first_far,
        qkv, rates, gain_rows, cosine, sine, queries, keys, values, log_total,
    )
    def whole(quarters, kind):
        return kernel_call(slots_kernel, [((2, 128, 2048), kind)], [SMEM] + [VMEM] * 4, 8)(
            ids, *quarters
        )[0]

    (both,) = kernel_call(both_kernel, [((128, 2048), BF)], [SMEM] + [VMEM] * 2, 4)(
        ids, own_output, output_far
    )
    both = after(both, inner)
    (output,) = kernel_call(
        two_slots_kernel, [((2, 128, 2048), BF)], [SMEM] + [VMEM] * 2, 8
    )(ids, both, other_core(both))
    inner_terms = token_terms(inner)
    qkv_grad, *pieces = kernel_call(
        exit_kernel,
        [((1024, 384), BF)] + [PIECE] * 8,
        [SMEM] + [VMEM] * 11,
        20,
        2 * 1024 * 2048 * 384,
        [pltpu.VMEM((1024, 384), BF)],
        [output, expert_grads],
    )(places, q_scaled, k_scaled, v_grad, qkv, rates, *inner_terms, first, first_far)
    seen = []
    terms = cube_scatter(pieces, seen)
    near, far = kernel_call(
        attention_weights_kernel,
        [((1024, 640), BF)] * 2,
        [SMEM] + [VMEM] * 5,
        24,
        2 * 1024 * 2048 * 512,
    )(ids, normed, qkv_grad, branch, attended, gain_grads)
    keep, send = split(5, ids, near, other_core(after(far, seen[0])))
    keep, send = split(4, ids, keep, X_ACROSS(send))
    attn_grads = (keep + X_PAIR(after(send, seen[2]))).reshape(4, 64, 640)
    attn_grads = line_exchange(attn_grads, ids)
    (own_input_grad,) = kernel_call(
        input_grad_kernel, [((64, 2048), BF)], [SMEM] + [VMEM] * 11, 8
    )(ids, *terms, middle_grad, own_tokens, attn_row)

    expert_grads = line_exchange(after(expert_grads, own_input_grad), ids)
    input_quarters = [own_input_grad] + [
        move(own_input_grad) for move in (other_half, other_core, other_both)
    ]
    q_grads, k_grads, v_grads, o_grads, attn_part = kernel_call(
        first_unpack_kernel,
        [((64, 512), F32)] * 4 + [((64, 128), F32)],
        [VMEM] * 4,
        8,
    )(attn_grads, w_query, w_key, w_value)
    o_grads = o_grads.T
    gate_grads, up_grads, down_grads, small = kernel_call(
        second_unpack_kernel,
        [((10, 64, 256), F32)] * 3 + [((64, 128), F32)],
        [VMEM] * 4,
        20,
    )(expert_grads, w_gate, w_up, router.T)
    summed = jnp.concatenate([small[:, :11], attn_part[:, :1]], axis=1)
    summed = summed + other_core(summed)
    summed = summed + other_half(summed)
    return (
        output,
        whole(input_quarters, F32),
        summed[:, 11] / attn_gain.astype(F32),
        attn_grads[:, :4, 512].astype(F32),
        attn_grads[:, :4, 513].astype(F32),
        q_grads,
        k_grads,
        v_grads,
        o_grads,
        summed[:, 10] / mlp_gain.astype(F32),
        summed[:, :10],
        gate_grads,
        up_grads,
        down_grads.swapaxes(1, 2),
    )


def solution(mesh):
    fine = Mesh(mesh.devices.reshape(SIZES), AXES)
    rows = P("x", CONTEXT, None)
    vector = P(WEIGHT)
    gains = P(TENSOR, WEIGHT)
    tall = P(WEIGHT, TENSOR)
    routed = P(WEIGHT, None)
    hidden = P(None, WEIGHT, TENSOR)
    back = P(None, TENSOR, WEIGHT)
    weights = (vector, gains, gains, tall, tall, tall, gains, vector, routed, hidden, hidden, back)
    return jax.shard_map(
        per_device,
        mesh=fine,
        in_specs=(rows, P("x"), rows) + weights + (rows,),
        out_specs=(rows, rows) + weights,
        check_vma=False,
    )
```

```python
import math

import jax
import jax.numpy as jnp
import numpy as np
from jax import lax
from jax.experimental import pallas as pl
from jax.experimental.pallas import tpu as pltpu
from jax.sharding import Mesh
from jax.sharding import PartitionSpec as P

EPSILON = 1e-05
ROPE_BASE = 10000.0
SCALE = 128 ** (-0.5)
BF = jnp.bfloat16
F32 = jnp.float32
HIGHEST = lax.Precision.HIGHEST

AXES = ("x", "z", "yl", "yh", "c")
SIZES = (4, 4, 2, 2, 2)
CONTEXT = ("z", "yl")
TENSOR = ("yh", "c")
WEIGHT = ("x", "z", "yl")
GROUP = ("z", "yl", "yh")
Y = ("yl", "yh")
VMEM = pl.BlockSpec(memory_space=pltpu.VMEM)
SMEM = pl.BlockSpec(memory_space=pltpu.SMEM)
ANY = pl.BlockSpec(memory_space=pl.ANY)
MIB = 1024 * 1024


def exchange(axes, size, mask):
    pairs = [(at, at ^ mask) for at in range(size)]
    return lambda v: lax.ppermute(v, axes, pairs)


CUBE = (exchange("z", 4, 1), exchange(Y, 4, 2), exchange("z", 4, 3), exchange(Y, 4, 3))
ALONG_Z = (exchange("z", 4, 1), exchange("z", 4, 3), exchange("z", 4, 2))
ALONG_Y = (exchange(Y, 4, 2), exchange(Y, 4, 3), exchange(Y, 4, 1))
X_PAIR, X_ACROSS = exchange("x", 4, 1), exchange("x", 4, 3)
LINE = ("z", "yl", "c")


def swapped_along_z(mask):
    pairs = [
        (4 * z + 2 * yl + core, 4 * (z ^ mask) + 2 * core + yl)
        for z in range(4)
        for yl in range(2)
        for core in range(2)
    ]
    return lambda v: lax.ppermute(v, LINE, pairs)


SWAPPED = tuple(swapped_along_z(mask) for mask in (0, 1, 3, 2))
other_core = exchange("c", 2, 1)
other_half = exchange("yh", 2, 1)
other_both = exchange(TENSOR, 4, 3)


def dot(a, b, left=1, right=0, precision=None):
    return lax.dot_general(
        a, b, (((left,), (right,)), ((), ())), preferred_element_type=F32, precision=precision
    )


def dot_in_two(a, b, left, right):
    upper = a.astype(BF)
    return dot(upper, b, left, right) + dot((a - upper.astype(F32)).astype(BF), b, left, right)


def all_to_all(v, axes):
    return lax.all_to_all(v, axes, split_axis=0, concat_axis=0, tiled=True)


def kernel_call(body, outs, in_specs, limit, flops=0, scratch=(), earlier=()):
    def whole_body(*refs):
        body(*refs[len(earlier) :])

    call = pl.pallas_call(
        whole_body,
        out_shape=[jax.ShapeDtypeStruct(shape, kind) for shape, kind in outs],
        in_specs=[ANY] * len(earlier) + in_specs,
        out_specs=[VMEM] * len(outs),
        scratch_shapes=list(scratch),
        compiler_params=pltpu.CompilerParams(vmem_limit_bytes=limit * MIB),
        cost_estimate=pl.CostEstimate(flops=flops, bytes_accessed=4 * MIB, transcendentals=0),
    )
    return lambda *args: call(*earlier, *args)


PIECE = ((128, 2048), BF)
HEAD = ((1024, 128), BF)
WIDE_HEAD = ((1024, 128), F32)


def rows_at(places, at):
    return pl.ds(pl.multiple_of(places[at] * 16, 16), 16)


def join_kernel(*refs):
    half, cuts = refs[0].shape[0], len(refs[8:]) // 4
    for i in range(4):
        at = 0
        for out in refs[8 + cuts * i : 8 + cuts * i + cuts]:
            columns = slice(at, at + out.shape[1])
            out[:half, :] = refs[i][:, columns]
            out[half:, :] = refs[4 + i][:, columns]
            at += out.shape[1]


def join(parts, arrived, widths, earlier=()):
    rows = 2 * parts[0].shape[0]
    outs = [((rows, width), BF) for width in widths] * 4
    return kernel_call(join_kernel, outs, [VMEM] * 8, 16, earlier=earlier)(*parts, *arrived)


def cube_step(parts, step):
    return [CUBE[(i + step) % 4](parts[i]) for i in range(4)]


def cube_gather(parts, seen=None, earlier=None):
    parts = list(parts)
    for step in range(3):
        arrived = cube_step(parts, step)
        parts = join(parts, arrived, [parts[0].shape[1]], (earlier or {}).get(step, ()))
        if seen is not None:
            seen.append(arrived)
    return list(parts) + cube_step(parts, 3)


def pick_kernel(ids, *refs):
    arrays, outs = refs[:-4], refs[-4:]
    for mask, out in zip((0, 1, 3, 2), outs):
        at = 0
        for blocks in arrays:
            columns = slice(at, at + blocks.shape[2])
            out[:, :, columns] = blocks[pl.ds(ids[3] ^ mask, 1)]
            at += blocks.shape[2]


def place_kernel(ids, *refs):
    arrived, outs = refs[:4], refs[4:]
    for mask, held in zip((0, 1, 3, 2), arrived):
        at = 0
        for out in outs:
            out[pl.ds(ids[3] ^ mask, 1)] = held[:, :, at : at + out.shape[2]]
            at += out.shape[2]


def pair_kernel(bit, ids, own, far, out):
    rows = own.shape[0]
    here = pl.multiple_of(ids[bit] * rows, rows)
    out[pl.ds(here, rows), :] = own[...]
    out[pl.ds(rows - here, rows), :] = far[...]


def pair(bit, ids, own, far):
    rows, width = own.shape
    return kernel_call(
        lambda *refs: pair_kernel(bit, *refs),
        [((2 * rows, width), BF)],
        [SMEM] + [VMEM] * 2,
        max(4, rows * width * 8 // MIB + 2),
    )(ids, own, far)[0]


def split_kernel(bit, ids, a, b, keep, send):
    rows = keep.shape[0]
    here = pl.multiple_of(ids[bit] * rows, rows)
    for out, at in ((keep, here), (send, rows - here)):
        for n in range(0, rows, 64):
            held = pl.ds(pl.multiple_of(at + n, 64), 64)
            out[n : n + 64, :] = (a[held, :].astype(F32) + b[held, :].astype(F32)).astype(BF)


def split(bit, ids, a, b):
    rows, width = a.shape
    return kernel_call(
        lambda *refs: split_kernel(bit, *refs),
        [((rows // 2, width), BF)] * 2,
        [SMEM] + [VMEM] * 2,
        max(4, rows * width * 8 // MIB + 2),
    )(ids, a, b)


def line_exchange(ids, *arrays):
    wide = ((1, arrays[0].shape[1], sum(v.shape[2] for v in arrays)), BF)
    sent = kernel_call(pick_kernel, [wide] * 4, [SMEM] + [VMEM] * len(arrays), 8)(ids, *arrays)
    arrived = [move(held) for move, held in zip(SWAPPED, sent)]
    return kernel_call(
        place_kernel, [(v.shape, BF) for v in arrays], [SMEM] + [VMEM] * 4, 8
    )(ids, *arrived)


def token_terms(stats):
    held = stats + ALONG_Z[0](stats) + ALONG_Z[1](stats) + ALONG_Z[2](stats)
    return [held] + [move(held) for move in ALONG_Y]


def fold_kernel(*refs):
    half = refs[0].shape[0] // 2
    for i in range(4):
        kept, arrived, keep, send = refs[i], refs[4 + i], refs[8 + i], refs[12 + i]
        keep[...] = (kept[:half, :].astype(F32) + arrived[:half, :].astype(F32)).astype(BF)
        send[...] = (kept[half:, :].astype(F32) + arrived[half:, :].astype(F32)).astype(BF)


def cube_scatter(pieces, seen=None, earlier=None):
    kept, sent = pieces[:4], pieces[4:]
    for step in (3, 2, 1, 0):
        arrived = cube_step(sent, step)
        if seen is not None:
            seen.append(arrived)
        if step:
            half = ((kept[0].shape[0] // 2, kept[0].shape[1]), BF)
            folded = kernel_call(
                fold_kernel, [half] * 8, [VMEM] * 8, 16, earlier=(earlier or {}).get(step, ())
            )(*kept, *arrived)
            kept, sent = folded[:4], folded[4:]
    return list(kept) + arrived


def block_places():
    at = jnp.arange(64, dtype=jnp.int32)
    part, block = (at >> 3) & 3, (at & 7) | ((at >> 5) << 3)
    turned = [(block >> ((dim - part) & 3)) & 1 for dim in range(4)]
    z = lax.axis_index("z") ^ (turned[0] ^ (3 * turned[2]))
    y = (2 * lax.axis_index("yh") + lax.axis_index("yl")) ^ (turned[1] ^ (3 * turned[3]))
    return ((2 * z + (y & 1)) * 2 + (y >> 1)) * 4 + part


def put_pieces(places, pieces, out):
    for k, piece in enumerate(pieces):
        for j in range(8):
            out[rows_at(places, 8 * k + j), :] = piece[16 * j : 16 * j + 16, :]


def take_rows(places, source, out, start=0):
    for n in range(out.shape[0] // 16):
        out[16 * n : 16 * n + 16, :] = source[rows_at(places, start + n), :]


def project(rows, near, far, columns, pieces, start=0):
    for b in range(len(pieces) // 2):
        held = rows[256 * b : 256 * b + 256, :]
        for at, weight in enumerate((near, far)):
            wide = dot(held, weight[:, columns], 1, 1).astype(BF)
            place = slice(start + 1024 * at, start + 1024 * at + 1024)
            for k in range(2):
                pieces[2 * b + k][:, place] = wide[128 * k : 128 * k + 128]


def natural_order(near, core, out):
    first = lax.broadcasted_iota(jnp.int32, (near.shape[0], 128), 1) < 64
    for j in range(8):
        mine = near[:, 128 * j : 128 * j + 128]
        other = near[:, 1024 + 128 * j : 1024 + 128 * j + 128]
        low = jnp.where(core == 0, mine, other)
        high = jnp.where(core == 0, other, mine)
        out[:, 256 * j : 256 * j + 128] = jnp.where(first, low, pltpu.roll(high, 64, 1)).astype(BF)
        out[:, 256 * j + 128 : 256 * j + 256] = jnp.where(
            first, pltpu.roll(low, 64, 1), high
        ).astype(BF)


def prepare_kernel(ids, places, length, tokens, cot, routes, own_tokens, own_cot, p0, p1, p2, p3, wide):
    core, parts = ids[0], (p0, p1, p2, p3)
    first = lax.broadcasted_iota(jnp.int32, (64, 128), 1) < 64
    for source, out, at in ((tokens, own_tokens, 0), (cot, own_cot, 2048)):
        for j in range(8):
            a = source[0, :, 256 * j : 256 * j + 128].astype(F32)
            b = source[0, :, 256 * j + 128 : 256 * j + 256].astype(F32)
            low = jnp.where(first, a, pltpu.roll(b, 64, 1))
            high = jnp.where(first, pltpu.roll(a, 64, 1), b)
            out[:, 128 * j : 128 * j + 128] = jnp.where(core == 0, low, high).astype(BF)
            out[:, 1024 + 128 * j : 1152 + 128 * j] = jnp.where(core == 0, high, low).astype(BF)
        for i in range(4):
            parts[i][:, at : at + 2048] = out[16 * i : 16 * i + 16, :]
    expert = lax.broadcasted_iota(jnp.int32, (128, 128), 0)
    chosen = jnp.zeros((128, 128), F32)
    for k in range(8):
        chosen += (expert == routes[0, k : k + 1, :]).astype(F32)
    wide[...] = dot(chosen.astype(BF), identity(128, BF), 0, 0)
    for i in range(4):
        rows = pl.ds(pl.multiple_of(ids[1] * 64 + 16 * i, 16), 16)
        parts[i][:, 4096:] = wide[rows, :].astype(BF)


def prepare(ids, places, length, tokens, cot, routes):
    own = lambda n, ids: (ids[0], ids[1], 0)
    whole = lambda n, ids: (0, 0)
    return pl.pallas_call(
        prepare_kernel,
        grid_spec=pltpu.PrefetchScalarGridSpec(
            num_scalar_prefetch=1,
            grid=(1,),
            in_specs=[
                SMEM,
                SMEM,
                pl.BlockSpec((1, 64, 2048), own),
                pl.BlockSpec((1, 64, 2048), own),
                pl.BlockSpec((1, 8, 128), lambda n, ids: (ids[0], 0, 0)),
            ],
            out_specs=[pl.BlockSpec((64, 2048), whole)] * 2 + [pl.BlockSpec((16, 4224), whole)] * 4,
            scratch_shapes=[pltpu.VMEM((128, 128), F32)],
        ),
        out_shape=[jax.ShapeDtypeStruct((64, 2048), BF)] * 2
        + [jax.ShapeDtypeStruct((16, 4224), BF)] * 4,
        compiler_params=pltpu.CompilerParams(vmem_limit_bytes=8 * MIB),
    )(ids, places, length, tokens, cot, routes)


def identity(size, kind):
    row = lax.broadcasted_iota(jnp.int32, (size, size), 0)
    return (row == lax.broadcasted_iota(jnp.int32, (size, size), 1)).astype(kind)


def first_pack_kernel(query, key, value, w_out, attn_gain, mlp_gain, q_gain, k_gain, out):
    row = lax.broadcasted_iota(jnp.int32, (64, 128), 0)
    lane = lax.broadcasted_iota(jnp.int32, (64, 128), 1)
    extra = jnp.zeros((64, 128), F32)
    for at, gain in enumerate((attn_gain, mlp_gain)):
        column = jnp.sum(gain[...].astype(F32) * identity(64, F32), axis=1, keepdims=True)
        extra = jnp.where(lane == at, column, extra)
    for k in range(4):
        columns = slice(128 * k, 128 * k + 128)
        for at, w in ((0, query), (128, key), (256, value), (512, w_out)):
            out[k, :, at : at + 128] = w[:, columns]
        held = extra
        for at, gain in enumerate((q_gain, k_gain)):
            for j in range(4):
                here = jnp.logical_and(row == j, lane == 2 + at)
                held = jnp.where(here, gain[k : k + 1, j : j + 1].astype(F32), held)
        out[k, :, 384:512] = held.astype(BF)


def second_pack_kernel(gate, up, down, router, out):
    lane = lax.broadcasted_iota(jnp.int32, (64, 128), 1)
    routed = jnp.zeros((64, 128), F32)
    for e in range(10):
        column = jnp.sum(
            router[e : e + 1, :].astype(F32) * identity(64, F32), axis=1, keepdims=True
        )
        routed = jnp.where(lane == e, column, routed)
    for k in range(4):
        for m in range(5):
            tile = 5 * k + m
            columns = slice(128 * (tile % 2), 128 * (tile % 2) + 128)
            for w, at in ((gate, 0), (up, 640), (down, 1408)):
                out[k, :, at + 128 * m : at + 128 * m + 128] = w[tile // 2, :, columns]
        out[k, :, 1280:1408] = routed.astype(BF)


def second_unpack_kernel(grads, gate, up, router, gate_out, up_out, down_out, small):
    part = jnp.zeros((64, 1), F32)
    routed = jnp.zeros((64, 128), F32)
    for k in range(4):
        for m in range(5):
            tile = 5 * k + m
            expert, columns = tile // 2, slice(128 * (tile % 2), 128 * (tile % 2) + 128)
            for w, out, at in ((gate, gate_out, 0), (up, up_out, 640), (None, down_out, 1408)):
                held = grads[k, :, at + 128 * m : at + 128 * m + 128].astype(F32)
                out[expert, :, columns] = held
                if w is not None:
                    held = held * w[expert, :, columns].astype(F32)
                    part += jnp.sum(held, axis=1, keepdims=True)
        routed += grads[k, :, 1280:1408].astype(F32)
    weights = dot(identity(64, BF), router[...], 1, 1)
    part += jnp.sum(routed[:, :10] * weights, axis=1, keepdims=True)
    lane = lax.broadcasted_iota(jnp.int32, (64, 128), 1)
    small[...] = jnp.where(lane < 10, routed, 0.0) + jnp.where(lane == 10, part, 0.0)


def first_unpack_kernel(grads, query, key, value, query_out, key_out, value_out, out_out, small):
    part = jnp.zeros((64, 1), F32)
    for k in range(4):
        columns = slice(128 * k, 128 * k + 128)
        for at, (w, out) in enumerate(((query, query_out), (key, key_out), (value, value_out))):
            held = grads[k, :, 128 * at : 128 * at + 128].astype(F32)
            out[:, columns] = held
            part += jnp.sum(held * w[:, columns].astype(F32), axis=1, keepdims=True)
        out_out[:, columns] = grads[k, :, 384:512].astype(F32)
    small[...] = jnp.broadcast_to(part, (64, 128))


def as_column(rows):
    eye = identity(128, F32)
    return [
        jnp.sum(rows[n : n + 1, :] * eye, axis=1, keepdims=True) for n in range(rows.shape[0])
    ]


def row_sums(v):
    return dot(jnp.ones((8, 128), F32), v, 1, 1, HIGHEST)[0:1]


def put_sums(stats, at, b, row):
    for half in range(2):
        place = 8 * at + 2 * b + half
        stats[place : place + 1, :] = row[:, 128 * half : 128 * half + 128]


def gain_places(core, at):
    row = lax.broadcasted_iota(jnp.int32, (1024, 128), 0)
    element = lax.broadcasted_iota(jnp.int32, (1024, 128), 1)
    yl = core if at == 0 else 1 - core
    here = ((row >> 6) * 2 + yl) * 4 + (row & 63) == element
    return jnp.where(jnp.logical_and(here, (row & 63) < 4), 1.0, 0.0).astype(BF)


def gain_line(near, far, column, out):
    eye = identity(128, F32)
    for at, weight in enumerate((near, far)):
        for b in range(8):
            held = weight[128 * b : 128 * b + 128, 384:512].astype(F32)
            line = jnp.sum(held[:, column : column + 1] * eye, axis=0, keepdims=True)
            out[0:1, 1024 * at + 128 * b : 1024 * at + 128 * b + 128] = line


def gains_kernel(ids, near, far, line, gains):
    gain_line(near, far, 1, line)
    total = jnp.zeros((128, 128), F32)
    for at, weight in enumerate((near, far)):
        total += dot(weight[:, 384:512], gain_places(ids[0], at), 0, 0)
    gains[...] = total[2:4, :]


def enter_kernel(places, *refs):
    pieces, (near, far, normed, gain) = refs[:8], refs[8:]
    gain_line(near, far, 0, gain)
    for k in range(8):

        def norm_rows(j, _):
            held = pieces[k][pl.ds(pl.multiple_of(j * 16, 16), 16), :].astype(F32)
            rate = lax.rsqrt(jnp.mean(held * held, axis=1, keepdims=True) + EPSILON)
            normed[rows_at(places, 8 * k + j), :] = (held * rate * gain[...]).astype(BF)
            return 0

        lax.fori_loop(0, 8, norm_rows, 0, unroll=True)


def project_kernel(normed, near, far, qkv, stats):
    for b in range(4):
        rows = slice(256 * b, 256 * b + 256)
        held = dot(normed[rows, :1024], near[:, :384]) + dot(normed[rows, 1024:], far[:, :384])
        qkv[rows, :] = held
        for at in range(2):
            columns = slice(128 * at, 128 * at + 128)
            put_sums(stats, at, b, row_sums(held[:, columns] * held[:, columns]))


def allowed_block(length, at):
    q_pos = 256 * at + lax.broadcasted_iota(jnp.int32, (256, 256 * at + 256), 0)
    k_pos = lax.broadcasted_iota(jnp.int32, (256, 256 * at + 256), 1)
    return jnp.logical_and(k_pos <= q_pos, k_pos < length[0])


def forward_kernel(
    places, length, qkv, s0, s1, s2, s3, gains, cosine, sine, near, far,
    rates, queries, keys, values, attended, log_total, *rest,
):
    pieces, ordered = rest[:8], rest[8]
    for n, column in enumerate(as_column((s0[...] + s1[...]) + (s2[...] + s3[...]))):
        rate = lax.rsqrt(column * (1.0 / 2048) + EPSILON)
        rates[128 * (n % 8) : 128 * (n % 8) + 128, n // 8 : n // 8 + 1] = rate

    def turn(held):
        return held * cosine[...] + pltpu.roll(held, 64, 1) * sine[...]

    queries[...] = turn(qkv[:, :128] * rates[:, 0:1] * gains[0:1, :]).astype(BF)
    keys[...] = turn(qkv[:, 128:256] * rates[:, 1:2] * gains[1:2, :]).astype(BF)
    values[...] = qkv[:, 256:].astype(BF)
    for at in range(4):
        rows, upto = slice(256 * at, 256 * at + 256), slice(0, 256 * at + 256)
        scores = dot(queries[rows, :], keys[upto, :], 1, 1) * SCALE
        scores = jnp.where(allowed_block(length, at), scores, -1e30)
        peak = jnp.max(scores, axis=1, keepdims=True)
        raised = jnp.exp(scores - peak)
        total = jnp.sum(raised, axis=1, keepdims=True)
        probs = (raised * (1.0 / total)).astype(BF)
        attended[rows, :] = dot(probs, values[upto, :]).astype(BF)
        log_total[rows, :] = peak + jnp.log(total)
    take_rows(places, attended, ordered)
    project(ordered, near, far, slice(512, 640), pieces)


def middle_kernel(*refs):
    terms, (own, gain, middle), outs = refs[:8], refs[8:11], refs[11:]
    for i in range(4):
        rows = slice(16 * i, 16 * i + 16)
        held = own[rows, :].astype(F32) + (terms[i][...].astype(F32) + terms[4 + i][...].astype(F32))
        middle[rows, :] = held
        rate = lax.rsqrt(jnp.mean(held * held, axis=1, keepdims=True) + EPSILON)
        outs[i][...] = (held * rate * gain[...]).astype(BF)


def mixture_kernel(places, length, ids, *refs):
    arrays, scratch = refs[:30], refs[30:]
    sources, outs = arrays[:18], arrays[18:]
    buffers, (near, far, mixed, grad_out, gated, hidden_grad) = scratch[:8], scratch[8:14]
    chosen_rows, ordered, gated_ordered, spread, in_sems, out_sems = scratch[14:]
    pieces = [held.at[:, :2048] for held in buffers]
    routed = [held.at[:, 2048:] for held in buffers]
    made = [held.at[:, :4096] for held in buffers]
    held = pieces + routed + [near, far]
    loads = [
        pltpu.make_async_copy(source, target, in_sems.at[n])
        for n, (source, target) in enumerate(zip(sources, held))
    ]
    stores = [
        pltpu.make_async_copy(source, target, out_sems.at[n])
        for n, (source, target) in enumerate(
            zip([mixed, grad_out, gated, hidden_grad] + made, outs)
        )
    ]
    for load in loads:
        load.start()
    expert = lax.broadcasted_iota(jnp.int32, (128, 640), 0)
    tile = 5 * ids[3] + (lax.broadcasted_iota(jnp.int32, (128, 640), 1) >> 7)
    spread[...] = ((tile >> 1) == expert).astype(F32).astype(BF)
    for load in loads[:8]:
        load.wait()
    put_pieces(places, pieces, mixed)
    stores[0].start()
    for load in loads[8:16]:
        load.wait()
    row = lax.broadcasted_iota(jnp.int32, (16, 1), 0)
    for k, piece in enumerate(routed):
        for j in range(8):
            rows = rows_at(places, 8 * k + j)
            inside = row < length[0] - places[8 * k + j] * 16
            kept = piece[16 * j : 16 * j + 16, :2048]
            grad_out[rows, :] = jnp.where(inside, kept, jnp.zeros((), BF))
            chosen_rows[rows, :] = piece[16 * j : 16 * j + 16, 2048:]
    stores[1].start()
    for load in loads[16:]:
        load.wait()
    lane = lax.broadcasted_iota(jnp.int32, (512, 128), 1)

    def block(b, _):
        rows = pl.ds(pl.multiple_of(b * 512, 512), 512)
        chosen = chosen_rows[rows, :].astype(F32)
        hidden = dot(mixed[rows, :1024], near[:, :1408]) + dot(mixed[rows, 1024:], far[:, :1408])
        out_grad = dot(grad_out[rows, :1024], near[:, 1408:]) + dot(
            grad_out[rows, 1024:], far[:, 1408:]
        )
        gate_h, up_h = hidden[:, :640], hidden[:, 640:1280]
        logits = jnp.where(lane < 10, hidden[:, 1280:], -1e30)
        raised = jnp.exp(logits - jnp.max(logits, axis=1, keepdims=True))
        route_probs = raised / jnp.sum(raised, axis=1, keepdims=True)
        gates = dot_in_two(route_probs * chosen, spread[...], 1, 0)
        sig = 1.0 / (1.0 + jnp.exp(-gate_h))
        silu = gate_h * sig
        activated = (silu * up_h).astype(BF).astype(F32)
        gated[rows, :] = (activated * gates).astype(BF)
        act_grad = out_grad * gates
        hidden_grad[rows, :640] = (act_grad * up_h * sig * (1.0 + gate_h * (1.0 - sig))).astype(BF)
        hidden_grad[rows, 640:1280] = (act_grad * silu).astype(BF)
        chosen_grad = dot_in_two(activated * out_grad, spread[...], 1, 1) * chosen
        inner = jnp.sum(chosen_grad * route_probs, axis=1, keepdims=True)
        hidden_grad[rows, 1280:] = (route_probs * (chosen_grad - inner)).astype(BF)
        return 0

    lax.fori_loop(0, 2, block, 0, unroll=True)
    stores[2].start()
    stores[3].start()
    for first in (4, 0):
        outs = made[first : first + 4]
        take_rows(places, hidden_grad, ordered, 8 * first)
        project(ordered, near, far, slice(0, 1408), outs)
        take_rows(places, gated, gated_ordered, 8 * first)
        project(gated_ordered, near, far, slice(1408, 2048), outs, 2048)
        for store in stores[4 + first : 8 + first]:
            store.start()
    for store in stores:
        store.wait()


def middle_grad_kernel(ids, length, *refs):
    terms, (middle, cot, gain, middle_grad, output), outs = refs[:8], refs[8:13], refs[13:]
    for i in range(4):
        rows = slice(16 * i, 16 * i + 16)
        inside = ids[2] + 16 * i + lax.broadcasted_iota(jnp.int32, (16, 1), 0) < length[0]
        grad = jnp.where(inside, cot[rows, :].astype(F32), 0.0)
        summed = terms[i][...].astype(F32) + terms[4 + i][...].astype(F32)
        scaled = summed[:, :2048] * gain[...]
        held = middle[rows, :]
        rate = lax.rsqrt(jnp.mean(held * held, axis=1, keepdims=True) + EPSILON)
        inner = jnp.mean(scaled * held, axis=1, keepdims=True)
        total = grad + rate * scaled - held * (rate * rate * rate * inner)
        middle_grad[rows, :] = total
        outs[i][...] = total.astype(BF)
        natural_order(held + summed[:, 2048:], ids[0], output.at[rows, :])


def backward_kernel(places, length, *refs):
    pieces, refs = refs[:8], refs[8:]
    (near, far, qkv, rates, gains, cosine, sine, queries, keys, values, log_total) = refs[:11]
    (branch, q_scaled, k_scaled, v_grad, inner, gain_grads) = refs[11:17]
    grad, key_grad, value_grad = refs[17:]

    def turn_back(held):
        return held * cosine[...] - pltpu.roll(held, 64, 1) * sine[...]

    put_pieces(places, pieces, branch)
    key_grad[...] = jnp.zeros_like(key_grad)
    value_grad[...] = jnp.zeros_like(value_grad)
    for at in range(4):
        rows, upto = slice(256 * at, 256 * at + 256), slice(0, 256 * at + 256)
        held = dot(branch[rows, :1024], near[:, 512:]) + dot(branch[rows, 1024:], far[:, 512:])
        grad[rows, :] = held.astype(BF)
        scores = dot(queries[rows, :], keys[upto, :], 1, 1) * SCALE
        probs = jnp.where(allowed_block(length, at), jnp.exp(scores - log_total[rows, :]), 0.0)
        prob_grad = dot(grad[rows, :], values[upto, :], 1, 1)
        delta = jnp.sum(probs * prob_grad, axis=1, keepdims=True)
        score_grad = (probs * (prob_grad - delta)).astype(BF)
        q_scaled[rows, :] = dot(score_grad, keys[upto, :]) * SCALE
        key_grad[upto, :] += dot(score_grad, queries[rows, :], 0, 0) * SCALE
        value_grad[upto, :] += dot(probs.astype(BF), grad[rows, :], 0, 0)
    v_grad[...] = value_grad[...].astype(BF)
    q_norm_grad = turn_back(q_scaled[...])
    k_norm_grad = turn_back(key_grad[...])
    q_turned = q_norm_grad * qkv[:, :128]
    k_turned = k_norm_grad * qkv[:, 128:256]
    gain_grads[0:1, :] = jnp.sum(q_turned * rates[:, 0:1], axis=0, keepdims=True)
    gain_grads[1:2, :] = jnp.sum(k_turned * rates[:, 1:2], axis=0, keepdims=True)
    for at, turned in enumerate((q_turned, k_turned)):
        products = turned * gains[at : at + 1, :]
        for b in range(4):
            put_sums(inner, at, b, row_sums(products[256 * b : 256 * b + 256]))
    q_scaled[...] = q_norm_grad * gains[0:1, :]
    k_scaled[...] = k_norm_grad * gains[1:2, :]


def exit_kernel(
    places, q_scaled, k_scaled, v_grad, qkv, rates, s0, s1, s2, s3, near, far, grad, *rest
):
    pieces, ordered = rest[:8], rest[8]
    for n, column in enumerate(as_column((s0[...] + s1[...]) + (s2[...] + s3[...]))):
        at, rows = n // 8, slice(128 * (n % 8), 128 * (n % 8) + 128)
        columns, scaled = slice(128 * at, 128 * at + 128), (q_scaled, k_scaled)[at]
        rate = rates[rows, at : at + 1]
        factor = rate * rate * rate * column * (1.0 / 2048)
        grad[rows, columns] = (rate * scaled[rows, :] - qkv[rows, columns] * factor).astype(BF)
    grad[:, 256:] = v_grad[...]
    take_rows(places, grad, ordered)
    project(ordered, near, far, slice(0, 384), pieces)


def exit_rest_kernel(places, grad, near, far, *refs):
    take_rows(places, grad, refs[4])
    project(refs[4], near, far, slice(0, 384), refs[:4])


def expert_weights_kernel(mixed, hidden_grad, grad_out, gated, near, far):
    for at, out in enumerate((near, far)):
        for n in range(1024 * at, 1024 * at + 1024, 512):
            rows, columns = slice(n - 1024 * at, n - 1024 * at + 512), slice(n, n + 512)
            out[rows, :1408] = dot(mixed[:, columns], hidden_grad[...], 0, 0).astype(BF)
            out[rows, 1408:] = dot(grad_out[:, columns], gated[...], 0, 0).astype(BF)


def attention_weights_kernel(ids, normed, qkv_grad, branch, attended, gain_grads, near, far):
    gains = jnp.concatenate([gain_grads[...], jnp.zeros((6, 128), F32)], axis=0).astype(BF)
    for at, out in enumerate((near, far)):
        columns = slice(1024 * at, 1024 * at + 1024)
        out[:, :384] = dot(normed[:, columns], qkv_grad[...], 0, 0).astype(BF)
        out[:, 384:512] = dot(branch[:, columns], attended[...], 0, 0).astype(BF)
        out[:, 512:] = jnp.zeros((1024, 128), BF)
        out[:, 512:520] = dot(gain_places(ids[0], at), gains, 1, 1).astype(BF)


def input_grad_kernel(ids, *refs):
    terms, (middle_grad, own, gain, out) = refs[:8], refs[8:]
    for i in range(4):
        rows = slice(16 * i, 16 * i + 16)
        scaled = (terms[i][...].astype(F32) + terms[4 + i][...].astype(F32)) * gain[...]
        held = own[rows, :].astype(F32)
        rate = lax.rsqrt(jnp.mean(held * held, axis=1, keepdims=True) + EPSILON)
        inner = jnp.mean(scaled * held, axis=1, keepdims=True)
        total = middle_grad[rows, :] + rate * scaled - held * (rate * rate * rate * inner)
        natural_order(total, ids[0], out.at[rows, :])


def both_kernel(ids, own, far, out):
    here = pl.multiple_of(ids[1] * 64, 64)
    out[pl.ds(here, 64), :] = own[...]
    out[pl.ds(64 - here, 64), :] = far[...]


def two_slots_kernel(ids, own, far, out):
    out[pl.ds(ids[0], 1), :, :] = own[...][None]
    out[pl.ds(1 - ids[0], 1), :, :] = far[...][None]


def slots_kernel(ids, own, half, core, both, out):
    here = pl.multiple_of(ids[1] * 64, 64)
    for slot, near, far in ((ids[0], own, half), (1 - ids[0], core, both)):
        out[slot, pl.ds(here, 64), :] = near[...].astype(out.dtype)
        out[slot, pl.ds(64 - here, 64), :] = far[...].astype(out.dtype)


def angles(head_size):
    steps_half = np.arange(head_size // 2, dtype=np.float32)
    frequency = np.exp(steps_half * np.float32(-2.0 * math.log(ROPE_BASE) / head_size))
    turned = np.arange(1024, dtype=np.float32)[:, None] * frequency.astype(np.float32)[None, :]
    cosine, sine = np.cos(turned.astype(np.float64)), np.sin(turned.astype(np.float64))
    return (
        jnp.asarray(np.concatenate([cosine, cosine], axis=-1).astype(np.float32)),
        jnp.asarray(np.concatenate([-sine, sine], axis=-1).astype(np.float32)),
    )


def after(value, earlier):
    return lax.optimization_barrier((value, earlier))[0]


def per_device(
    tokens,
    lengths,
    routes,
    attn_gain,
    q_gain,
    k_gain,
    w_query,
    w_key,
    w_value,
    w_out,
    mlp_gain,
    router,
    w_gate,
    w_up,
    w_down,
    cotangent,
):
    z = lax.axis_index("z")
    yh = lax.axis_index("yh")
    core = lax.axis_index("c")

    own_place = (2 * z + lax.axis_index("yl")) * 128 + yh * 64
    x = lax.axis_index("x")
    ids = jnp.stack([core, yh, own_place, z, x & 1, x >> 1]).astype(jnp.int32)
    places = block_places()
    slot_length = lax.dynamic_slice(lengths, (core,), (1,))
    own_tokens, own_cot, *parts = prepare(
        ids, places, slot_length, tokens, cotangent, routes.swapaxes(1, 2)
    )
    (first_pack,) = kernel_call(first_pack_kernel, [((4, 64, 640), BF)], [VMEM] * 8, 8)(
        w_query, w_key, w_value, w_out.T, attn_gain[None], mlp_gain[None], q_gain, k_gain
    )

    held = line_exchange(ids, after(first_pack, own_tokens))[0].reshape(256, 640)
    arrived = cube_step(parts, 0)
    parts = join(parts, arrived, [4224])
    arrived = cube_step(parts, 1)
    parts = join(parts, arrived, [4224])
    held = after(pair(4, ids, held, X_PAIR(held)), arrived)
    (second_pack,) = kernel_call(
        second_pack_kernel, [((4, 64, 2048), BF)], [VMEM] * 4, 12, earlier=arrived
    )(w_gate, w_up, w_down.swapaxes(1, 2), router.T)
    arrived = cube_step(parts, 2)
    joined = join(parts, arrived, [2048, 2176])
    first = after(pair(5, ids, held, X_ACROSS(held)), joined)
    first_far = other_core(first)
    token_pieces, routed_pieces = list(joined[0::2]), list(joined[1::2])
    token_pieces += cube_step(token_pieces, 3)
    routed_pieces += cube_step(after(routed_pieces, token_pieces), 3)

    normed, attn_row = kernel_call(
        enter_kernel,
        [((1024, 2048), BF), ((1, 2048), F32)],
        [SMEM] + [VMEM] * 10,
        20,
        2 * 1024 * 2048 * 384,
    )(places, *token_pieces, first, first_far)
    qkv, stats = kernel_call(
        project_kernel,
        [((1024, 384), F32), ((16, 128), F32)],
        [VMEM] * 3,
        20,
        2 * 1024 * 2048 * 384,
    )(normed, first, first_far)
    mlp_row, gain_rows = kernel_call(
        gains_kernel, [((1, 2048), F32), ((2, 128), F32)], [SMEM] + [VMEM] * 2, 12, earlier=[stats]
    )(ids, first, first_far)
    terms = token_terms(after(stats, routed_pieces[4:]))
    held = line_exchange(ids, after(second_pack, terms[1:]))[0].reshape(256, 2048)
    cosine, sine = angles(128)
    rates, queries, keys, values, attended, log_total, *pieces = kernel_call(
        forward_kernel,
        [((1024, 2), F32), HEAD, HEAD, HEAD, HEAD, ((1024, 1), F32)] + [PIECE] * 8,
        [SMEM, SMEM] + [VMEM] * 10,
        28,
        4 * 1024 * 1024 * 128,
        [pltpu.VMEM((1024, 128), BF)],
    )(
        places, slot_length, qkv, *terms, gain_rows, cosine, sine, first, first_far
    )
    own_row = ((64, 2048), F32)
    own_part = ((16, 2048), BF)
    held = pair(4, ids, held, X_PAIR(after(held, pieces)))
    seen = []
    terms = cube_scatter(pieces, seen)
    second = pair(5, ids, held, X_ACROSS(after(held, seen[1])))
    middle, *parts = kernel_call(
        middle_kernel, [own_row] + [own_part] * 4, [VMEM] * 10, 8
    )(*terms, own_tokens, mlp_row)

    seen = []
    mixed_pieces = cube_gather(parts, seen)
    second_far = other_core(after(second, seen[2]))
    sums = [((1024, 2048), BF), ((1024, 2048), BF), ((1024, 640), BF), ((1024, 1408), BF)]
    sums += [((128, 4096), BF)] * 8
    taken = [*mixed_pieces, *routed_pieces, second, second_far]
    mixed, grad_out, gated, hidden_grad, *pieces = pl.pallas_call(
        mixture_kernel,
        out_shape=[jax.ShapeDtypeStruct(shape, kind) for shape, kind in sums],
        in_specs=[SMEM] * 3 + [ANY] * 18,
        out_specs=[ANY] * 12,
        scratch_shapes=[pltpu.VMEM((128, 4224), BF)] * 8
        + [pltpu.VMEM((1024, 2048), BF)] * 2
        + [pltpu.VMEM(shape, BF) for shape, _ in sums[:4]]
        + [
            pltpu.VMEM((1024, 128), BF),
            pltpu.VMEM((512, 1408), BF),
            pltpu.VMEM((512, 640), BF),
            pltpu.VMEM((128, 640), BF),
            pltpu.SemaphoreType.DMA((18,)),
            pltpu.SemaphoreType.DMA((12,)),
        ],
        compiler_params=pltpu.CompilerParams(vmem_limit_bytes=58 * MIB),
        cost_estimate=pl.CostEstimate(
            flops=2 * 1024 * 2048 * 4096, bytes_accessed=36 * MIB, transcendentals=0
        ),
    )(places, slot_length, ids, *taken)
    seen = []
    terms = cube_scatter(pieces, seen)
    near, far = kernel_call(
        expert_weights_kernel,
        [((1024, 2048), BF)] * 2,
        [VMEM] * 4,
        40,
        2 * 1024 * 2048 * 2048,
    )(mixed, hidden_grad, grad_out, gated)
    keep, send = split(5, ids, near, other_core(after(far, seen[0])))
    first_send = X_ACROSS(after(send, seen[2]))
    middle_grad, own_output, *parts = kernel_call(
        middle_grad_kernel,
        [own_row, ((64, 2048), BF)] + [own_part] * 4,
        [SMEM, SMEM] + [VMEM] * 11,
        8,
    )(ids, slot_length, *terms, middle, own_cot, mlp_row)
    keep, send = split(4, ids, keep, first_send)
    seen = []
    branch_pieces = cube_gather(parts, seen)
    expert_grads = (keep + X_PAIR(after(send, seen[0]))).reshape(4, 64, 2048)
    output_far = other_half(after(own_output, seen[2]))

    branch, q_scaled, k_scaled, v_grad, inner, gain_grads = kernel_call(
        backward_kernel,
        [((1024, 2048), BF), WIDE_HEAD, WIDE_HEAD, HEAD, ((16, 128), F32), ((2, 128), F32)],
        [SMEM, SMEM] + [VMEM] * 19,
        40,
        10 * 1024 * 1024 * 128,
        [pltpu.VMEM((1024, 128), BF), pltpu.VMEM((1024, 128), F32), pltpu.VMEM((1024, 128), F32)],
    )(
        places, slot_length, *branch_pieces, first, first_far,
        qkv, rates, gain_rows, cosine, sine, queries, keys, values, log_total,
    )
    def whole(quarters, kind):
        return kernel_call(slots_kernel, [((2, 128, 2048), kind)], [SMEM] + [VMEM] * 4, 8)(
            ids, *quarters
        )[0]

    (both,) = kernel_call(both_kernel, [((128, 2048), BF)], [SMEM] + [VMEM] * 2, 4)(
        ids, own_output, output_far
    )
    both = after(both, inner)
    (output,) = kernel_call(
        two_slots_kernel, [((2, 128, 2048), BF)], [SMEM] + [VMEM] * 2, 8
    )(ids, both, other_core(both))
    inner_terms = token_terms(inner)
    qkv_grad, *pieces = kernel_call(
        exit_kernel,
        [((1024, 384), BF)] + [PIECE] * 8,
        [SMEM] + [VMEM] * 11,
        20,
        2 * 1024 * 2048 * 384,
        [pltpu.VMEM((1024, 384), BF)],
        [output, expert_grads],
    )(places, q_scaled, k_scaled, v_grad, qkv, rates, *inner_terms, first, first_far)
    seen = []
    terms = cube_scatter(pieces, seen)
    near, far = kernel_call(
        attention_weights_kernel,
        [((1024, 640), BF)] * 2,
        [SMEM] + [VMEM] * 5,
        24,
        2 * 1024 * 2048 * 512,
    )(ids, normed, qkv_grad, branch, attended, gain_grads)
    keep, send = split(5, ids, near, other_core(after(far, seen[0])))
    keep, send = split(4, ids, keep, X_ACROSS(send))
    attn_grads = (keep + X_PAIR(after(send, seen[2]))).reshape(4, 64, 640)
    (own_input_grad,) = kernel_call(
        input_grad_kernel, [((64, 2048), BF)], [SMEM] + [VMEM] * 11, 8
    )(ids, *terms, middle_grad, own_tokens, attn_row)

    expert_grads, attn_grads = line_exchange(
        ids, expert_grads, after(attn_grads, own_input_grad)
    )
    input_quarters = [own_input_grad] + [
        move(own_input_grad) for move in (other_half, other_core, other_both)
    ]
    q_grads, k_grads, v_grads, o_grads, attn_part = kernel_call(
        first_unpack_kernel,
        [((64, 512), F32)] * 4 + [((64, 128), F32)],
        [VMEM] * 4,
        8,
    )(attn_grads, w_query, w_key, w_value)
    o_grads = o_grads.T
    gate_grads, up_grads, down_grads, small = kernel_call(
        second_unpack_kernel,
        [((10, 64, 256), F32)] * 3 + [((64, 128), F32)],
        [VMEM] * 4,
        20,
    )(expert_grads, w_gate, w_up, router.T)
    summed = jnp.concatenate([small[:, :11], attn_part[:, :1]], axis=1)
    summed = summed + other_core(summed)
    summed = summed + other_half(summed)
    return (
        output,
        whole(input_quarters, F32),
        summed[:, 11] / attn_gain.astype(F32),
        attn_grads[:, :4, 512].astype(F32),
        attn_grads[:, :4, 513].astype(F32),
        q_grads,
        k_grads,
        v_grads,
        o_grads,
        summed[:, 10] / mlp_gain.astype(F32),
        summed[:, :10],
        gate_grads,
        up_grads,
        down_grads.swapaxes(1, 2),
    )


def solution(mesh):
    fine = Mesh(mesh.devices.reshape(SIZES), AXES)
    rows = P("x", CONTEXT, None)
    vector = P(WEIGHT)
    gains = P(TENSOR, WEIGHT)
    tall = P(WEIGHT, TENSOR)
    routed = P(WEIGHT, None)
    hidden = P(None, WEIGHT, TENSOR)
    back = P(None, TENSOR, WEIGHT)
    weights = (vector, gains, gains, tall, tall, tall, gains, vector, routed, hidden, hidden, back)
    return jax.shard_map(
        per_device,
        mesh=fine,
        in_specs=(rows, P("x"), rows) + weights + (rows,),
        out_specs=(rows, rows) + weights,
        check_vma=False,
    )
```
